128 devices in a mesh: band: 4 (over x_hi, core), wide: 32 (over y, z, x_lo).
Axes of the slice: x: 4 (x_hi: 2, x_lo: 2; x = x_hi * 2 + x_lo), y: 4, z: 4, core: 2. Of those that a mesh axis runs over, the one named last changes fastest.
Arguments:
- panels: bfloat16 [4096, 16512], P(('wide', 'band')), may hold values from -6 to 6
- void_mask: int32 [4096, 16384], P(('wide', 'band')), may hold values 0 or 1
- background: float32 [4096, 16384], P(('wide', 'band')), may hold values from -6 to 6
- row_offset: int32 [4096], P(('wide', 'band')), may hold values from 0 to 124
- row_frac: float32 [4096], P(('wide', 'band')), may hold values from 0 to 1
- tile_kind: int32 [128], replicated, may hold values from 0 to 1
- tile_shift: int32 [128], replicated, may hold values from 0 to 125
- tile_frac: float32 [128], replicated, may hold values from 0 to 1
- inverse_x: float32 [128, 128, 128], replicated, may hold values from -0.4 to 1.2, as said below
- couple_x: float32 [2, 128], replicated, may hold values from 0.2 to 0.8
- inverse_y: float32 [32, 128, 128], replicated, may hold values from -0.4 to 1.2, as said below
- couple_y: float32 [2, 32], replicated, may hold values from 0.2 to 0.8
Outputs:
- increment: float32 [4096, 16384], P(('wide', 'band'))
The draws below stay inside these ranges and needn't reach their ends.
Inputs may be any that keep to these rules, and one draw needn't show every extreme that they name: `inverse_x`: each block has a diagonal of positive entries and small off-diagonal entries. `inverse_y`: each block has a diagonal of positive entries and small off-diagonal entries.
All inputs are finite; a program needn't handle non-finite values. No bound on the sum of `void_mask` on one device may be relied on, other than what follows from the above.
Results may differ from the reference program's by a relative error of at most 0.0027.
Values may be sent and summed in bfloat16 or wider, within the bound.
No kernel may reach another device: no remote copies, remote signals or barrier semaphores. Data moves between devices by JAX's collectives and lax.ppermute only.
A program may use at most 128 MiB of HBM per device.

```python
import math
import jax
import jax.numpy as jnp
from jax import lax

BLK = 128
ITERS = 4
ROWS_ALL = 4096
NX = 16384
NXS = 16512
NBX = 128
NBY = 32
GROUP = 128


def build_blocks(diag_key, noise, count):
    scaled = jnp.exp(jax.random.uniform(diag_key, (count, BLK), jnp.float32, math.log(0.3), math.log(1.0)))
    eye = jnp.eye(BLK, dtype=jnp.float32)[None]
    return noise * (0.5 / math.sqrt(BLK)) * (1.0 - eye) + scaled[:, :, None] * eye


def draw_inverse_x(key, part):
    key = jax.random.fold_in(key, 11)
    diag_key, noise_key = jax.random.split(key)
    noise = jnp.clip(jax.random.normal(noise_key, (NBX, BLK, BLK), jnp.float32), -3.0, 3.0)
    return build_blocks(diag_key, noise, NBX)


def draw_inverse_y(key, part):
    key = jax.random.fold_in(key, 23)
    diag_key, noise_key = jax.random.split(key)
    noise = jnp.clip(jax.random.normal(noise_key, (NBY, BLK, BLK), jnp.float32), -3.0, 3.0)
    return build_blocks(diag_key, noise, NBY)


def set_ends(result, own_key, low, largest):
    longest = result.shape.index(max(result.shape))
    spots = []
    for shift in (0, 1):
        where = [jax.random.randint(jax.random.fold_in(own_key, axis), (), 0, length) for axis, length in enumerate(result.shape)]
        where[longest] = (where[longest] + shift) % result.shape[longest]
        spots.append(tuple(where))
    return result.at[spots[0]].set(low).at[spots[1]].set(largest)


def levels(rng, dims, shards, least, high):
    level, own = 1.0, jax.random.fold_in(rng, 6)
    for position, shards_of in shards:
        steps = jnp.exp(jax.random.uniform(jax.random.fold_in(own, position), (shards_of,), jnp.float32, least / len(shards), high / len(shards)))
        level = level * jnp.repeat(steps, dims[position] // shards_of).reshape([-1 if axis == position else 1 for axis in range(len(dims))])
    return level


def centred(stream_key, shape, scale, reach, pieces=(), kind=jnp.bfloat16):
    values = scale * jax.random.normal(stream_key, shape, jnp.float32)
    if pieces:
        values = values * levels(stream_key, shape, pieces, -0.22, 0.18)
    return jnp.clip(values, -reach, reach).astype(kind)


def setup_inputs(seed: int = 0) -> dict:
    streams_of = jax.random.split(jax.random.key(seed), 13)
    panels = centred(streams_of[0], (ROWS_ALL, NXS), 1.0, 6.0, ((0, 128),))
    void_mask = set_ends((jax.random.randint(streams_of[1], (ROWS_ALL, NX), 0, 4) < 3).astype(jnp.int32), jax.random.fold_in(streams_of[1], 1), 0, 1)
    background = centred(streams_of[2], (ROWS_ALL, NX), 1.0, 6.0, ((0, 128),), jnp.float32)
    row_offset = set_ends(jax.random.randint(streams_of[3], (ROWS_ALL,), 0, GROUP - 3), jax.random.fold_in(streams_of[3], 1), 0, (GROUP - 3) - 1).astype(jnp.int32)
    row_frac = jnp.clip(1.0 * jax.random.uniform(streams_of[4], (ROWS_ALL,), jnp.float32) ** levels(streams_of[4], (ROWS_ALL,), ((0, 128),), -0.2, 0.2), 0.0, 1.0)
    tile_kind = set_ends(jax.random.randint(streams_of[5], (NBX,), 0, 2), jax.random.fold_in(streams_of[5], 1), 0, 1).astype(jnp.int32)
    tile_shift = set_ends(jax.random.randint(streams_of[6], (NBX,), 0, BLK - 2), jax.random.fold_in(streams_of[6], 1), 0, (BLK - 2) - 1).astype(jnp.int32)
    tile_frac = jnp.clip(jax.random.uniform(streams_of[7], (NBX,), jnp.float32, 0.0, 1.0), 0.0, 1.0)
    inverse_x = draw_inverse_x(jax.random.fold_in(streams_of[12], 71), 0)
    couple_x = jnp.clip(jnp.exp(jax.random.uniform(streams_of[9], (2, NBX), jnp.float32, math.log(0.2), math.log(0.8))), 0.2, 0.8)
    inverse_y = draw_inverse_y(jax.random.fold_in(streams_of[12], 71), 0)
    couple_y = jnp.clip(jnp.exp(jax.random.uniform(streams_of[11], (2, NBY), jnp.float32, math.log(0.2), math.log(0.8))), 0.2, 0.8)
    return dict(panels=panels, void_mask=void_mask, background=background, row_offset=row_offset, row_frac=row_frac, tile_kind=tile_kind, tile_shift=tile_shift, tile_frac=tile_frac, inverse_x=inverse_x, couple_x=couple_x, inverse_y=inverse_y, couple_y=couple_y)


def cubic_terms(frac):
    f2 = frac * frac
    f3 = f2 * frac
    return [-0.5 * f3 + f2 - 0.5 * frac, 1.5 * f3 - 2.5 * f2 + 1.0, -1.5 * f3 + 2.0 * f2 + 0.5 * frac, 0.5 * f3 - 0.5 * f2]


def linear_terms(frac):
    zeros = jnp.zeros_like(frac)
    return [zeros, 1.0 - frac, frac, zeros]


def row_matrix(offsets, fracs, width, terms):
    columns = jnp.arange(width, dtype=jnp.int32)[None, :]
    total = jnp.zeros((offsets.shape[0], width), jnp.float32)
    for index, weight in enumerate(terms(fracs)):
        total = total + weight[:, None] * (columns == offsets[:, None] + index).astype(jnp.float32)
    return total.astype(jnp.bfloat16)


def column_tables(tile_kind, tile_frac):
    delta = jnp.arange(BLK + 3, dtype=jnp.int32)[:, None] - jnp.arange(BLK, dtype=jnp.int32)[None, :]
    cubic = jnp.zeros((tile_frac.shape[0], BLK + 3, BLK), jnp.float32)
    linear = jnp.zeros((tile_frac.shape[0], BLK + 3, BLK), jnp.float32)
    for index, (wc, wl) in enumerate(zip(cubic_terms(tile_frac), linear_terms(tile_frac))):
        hit = (delta == index).astype(jnp.float32)[None]
        cubic = cubic + wc[:, None, None] * hit
        linear = linear + wl[:, None, None] * hit
    return jnp.where(tile_kind[:, None, None] == 1, cubic, linear).astype(jnp.bfloat16)


def sweep_rows(source, inverse, couple):
    hp = lax.Precision.HIGHEST
    state = jnp.einsum('rbj,bij->rbi', source, inverse, precision=hp)
    for sweep in range(ITERS - 1):
        left = jnp.pad(state[:, :-1, -1], ((0, 0), (1, 0)))
        right = jnp.pad(state[:, 1:, 0], ((0, 0), (0, 1)))
        forced = source.at[:, :, 0].add(couple[0][None, :] * left)
        forced = forced.at[:, :, -1].add(couple[1][None, :] * right)
        state = jnp.einsum('rbj,bij->rbi', forced, inverse, precision=hp)
    return state


def sweep_columns(source, inverse, couple):
    hp = lax.Precision.HIGHEST
    state = jnp.einsum('bij,bjc->bic', inverse, source, precision=hp)
    for sweep in range(ITERS - 1):
        left = jnp.pad(state[:-1, -1, :], ((1, 0), (0, 0)))
        right = jnp.pad(state[1:, 0, :], ((0, 1), (0, 0)))
        forced = source.at[:, 0, :].add(couple[0][:, None] * left)
        forced = forced.at[:, -1, :].add(couple[1][:, None] * right)
        state = jnp.einsum('bij,bjc->bic', inverse, forced, precision=hp)
    return state


def reference(panels, void_mask, background, row_offset, row_frac, tile_kind, tile_shift, tile_frac, inverse_x, couple_x, inverse_y, couple_y):
    groups = ROWS_ALL // GROUP
    starts = jnp.arange(NBX, dtype=jnp.int32) * BLK + tile_shift.astype(jnp.int32)
    col_weights = column_tables(tile_kind, tile_frac).astype(jnp.float32)

    def one_group(items):
        panel, offsets, fracs = items
        cubic = row_matrix(offsets, fracs, GROUP, cubic_terms)
        linear = row_matrix(offsets, fracs, GROUP, linear_terms)
        tiles = jnp.where(tile_kind[:, None, None] == 1, cubic[None], linear[None]).astype(jnp.float32)
        blocks = jax.vmap(lambda s: lax.dynamic_slice_in_dim(panel, s, BLK + 3, 1))(starts).astype(jnp.float32)
        section = jnp.einsum('trs,tsc->trc', tiles, blocks).astype(jnp.bfloat16).astype(jnp.float32)
        return jnp.einsum('trc,tcj->rtj', section, col_weights).reshape(GROUP, NX)

    estimate = lax.map(one_group, (panels.reshape(groups, GROUP, NXS), row_offset.reshape(groups, GROUP), row_frac.reshape(groups, GROUP)))
    estimate = estimate.reshape(ROWS_ALL, NX)
    misfit = void_mask.astype(jnp.float32) * (estimate - background)
    east_west = sweep_rows(misfit.reshape(ROWS_ALL, NBX, BLK), inverse_x, couple_x).reshape(ROWS_ALL, NX)
    increment = sweep_columns(east_west.reshape(NBY, BLK, NX), inverse_y, couple_y)
    return increment.reshape(ROWS_ALL, NX)
```

```python
import functools

import jax
import jax.numpy as jnp
from jax import lax
from jax.experimental import pallas as pl
from jax.experimental.pallas import tpu as pltpu
from jax.sharding import PartitionSpec as P

BLK = 128
TG = 8
GW = TG * BLK
HALO = 3
PAD = 8
SPLITS = (0, 16)
VMEM_LIMIT = 48 * 1024 * 1024


def cubic_terms(frac):
    f2 = frac * frac
    f3 = f2 * frac
    return [
        -0.5 * f3 + f2 - 0.5 * frac,
        1.5 * f3 - 2.5 * f2 + 1.0,
        -1.5 * f3 + 2.0 * f2 + 0.5 * frac,
        0.5 * f3 - 0.5 * f2,
    ]


def linear_terms(frac):
    zeros = jnp.zeros_like(frac)
    return [zeros, 1.0 - frac, frac, zeros]


def row_matrix(offsets, fracs, columns, terms):
    total = jnp.zeros((offsets.shape[0], columns.shape[0]), jnp.float32)
    for index, weight in enumerate(terms(fracs)):
        hit = (columns[None, :] == offsets[:, None] + index).astype(jnp.float32)
        total = total + weight[:, None] * hit
    return total.astype(jnp.bfloat16)


def column_tables(kind, shift, frac):
    tiles = frac.shape[0]
    delta = (
        jnp.arange(2 * BLK, dtype=jnp.int32)[:, None] - jnp.arange(BLK, dtype=jnp.int32)[None, :]
    )
    tap = delta[None] - shift[:, None, None]
    total = jnp.zeros((tiles, 2 * BLK, BLK), jnp.float32)
    for index, (wc, wl) in enumerate(zip(cubic_terms(frac), linear_terms(frac))):
        weight = jnp.where(kind == 1, wc, wl)
        total = jnp.where(tap == index, weight[:, None, None], total)
    return total.astype(jnp.bfloat16)


def table_hi_lo(value):
    hi = lax.reduce_precision(value, 8, 7)
    return hi.astype(jnp.bfloat16), (value - hi).astype(jnp.bfloat16)


def split_hi_lo(value):
    hi = value.astype(jnp.bfloat16)
    lo = (value - hi.astype(jnp.float32)).astype(jnp.bfloat16)
    return hi, lo


def rows_kernel(first, groups, finals, carried, *refs):
    kind_ref, coef_ref = refs[:2]
    refs = refs[2:]
    (p0, p1, p2, p3, q0, q1, q2, q3, w_ref, t_ref, mask_ref, bg_ref, inv_ref) = refs[:13]
    refs = refs[13:]
    a_ref, b_ref, yw_ref = refs[:3]
    refs = refs[3:]
    if carried:
        u_in, f_in, l_in = refs[:3]
        refs = refs[3:]
    out_ref, part_ref, u_out, f_out, l_out, sec, u_st, f_st, l_st = refs
    step = pl.program_id(0)
    s = step + first

    @pl.when(step == 0)
    def _():
        if carried:
            u_st[0] = u_in[...]
            f_st[...] = f_in[...]
            l_st[...] = l_in[...]
        else:
            u_st[...] = jnp.zeros_like(u_st)
            f_st[...] = jnp.zeros_like(f_st)
            l_st[...] = jnp.zeros_like(l_st)

    @pl.when(step > 0)
    def _():
        u_st[0] = u_st[1]

    for st in (f_st, l_st):
        for i in range(HALO + TG):
            st[i] = st[i + TG]

    @pl.when(s < groups)
    def _():
        rows = jnp.concatenate([p0[...], p1[...], p2[...], p3[...]], axis=0)
        edge = jnp.concatenate([q0[...], q1[...], q2[...], q3[...]], axis=0)
        w = w_ref[...]
        both = jnp.dot(w, rows, preferred_element_type=jnp.float32).astype(jnp.bfloat16)
        tail = jnp.dot(w, edge, preferred_element_type=jnp.float32).astype(jnp.bfloat16)
        for k in range(2):
            sec[k, :, :GW] = both[k * 32 : (k + 1) * 32]
            sec[k, :, GW:] = tail[k * 32 : (k + 1) * 32]
        for i in range(TG):
            kind = kind_ref[s * TG + i]
            cols = slice(i * BLK, (i + 1) * BLK)
            taken = sec[kind, :, i * BLK : (i + 2) * BLK]
            est = jnp.dot(taken, t_ref[i], preferred_element_type=jnp.float32)
            misfit = mask_ref[:, cols].astype(jnp.float32) * (est - bg_ref[:, cols])
            hi, lo = split_hi_lo(misfit)
            u = jnp.dot(
                jnp.concatenate([hi, lo], axis=0), inv_ref[i], preferred_element_type=jnp.float32
            )
            u = u[:32, :BLK] + (u[32:, :BLK] + u[:32, BLK:])
            u_st[1, i] = u
            f_st[HALO + TG + i] = jnp.broadcast_to(u[:, :1], u.shape)
            l_st[HALO + TG + i] = jnp.broadcast_to(u[:, BLK - 1 :], u.shape)

    @pl.when(s >= groups)
    def _():
        for i in range(TG):
            f_st[HALO + TG + i] = jnp.zeros((32, BLK), jnp.float32)
            l_st[HALO + TG + i] = jnp.zeros((32, BLK), jnp.float32)

    @pl.when(s - 1 >= finals)
    def _():
        base = (s - 1) * TG + PAD - HALO

        def advance(which, j, west, east):
            st, r = (f_st, 0) if which == "f" else (l_st, 2)
            return st[j] + coef_ref[r, base + j] * west + coef_ref[r + 1, base + j] * east

        l1 = {j: advance("l", j, l_st[j - 1], f_st[j + 1]) for j in range(1, HALO + TG)}
        f1 = {j: advance("f", j, l_st[j - 1], f_st[j + 1]) for j in range(HALO, HALO + TG + 2)}
        outs = []
        for i in range(TG):
            j = HALO + i
            west = advance("l", j - 1, l1[j - 2], f1[j])
            east = advance("f", j + 1, l1[j], f1[j + 2])
            value = u_st[0, i] + a_ref[i : i + 1, :] * west + b_ref[i : i + 1, :] * east
            value = value.astype(jnp.bfloat16)
            out_ref[:, i * BLK : (i + 1) * BLK] = value
            outs.append(value)
        ends = jnp.dot(
            yw_ref[...], jnp.concatenate(outs, axis=1), preferred_element_type=jnp.float32
        )
        part_ref[...] = ends[0:2] + ends[8:10]

    @pl.when(step == pl.num_programs(0) - 1)
    def _():
        u_out[...] = u_st[1]
        f_out[...] = f_st[...]
        l_out[...] = l_st[...]


def run_rows(first, stop, groups, state, kinds, coefs, own, got, w, tables, mask, bg, inv, a, b, yw):
    ends_here = stop == groups
    steps = stop - first + (1 if ends_here else 0)
    finals = 0 if first == 0 else first - 1
    n_final = (stop if ends_here else stop - 1) - finals
    carried = state is not None
    count = stop - first
    here = lambda l: jnp.minimum(l, count - 1)
    done = lambda l: jnp.clip(l + first - 1, finals, finals + n_final - 1)
    full = lambda *shape: pl.BlockSpec(shape, lambda l, *_: (0,) * len(shape))
    wide = lambda off: pl.BlockSpec((32, GW), lambda l, *_: (0, here(l) + off))
    edge = lambda off: pl.BlockSpec((32, BLK), lambda l, *_: (0, (here(l) + off + 1) * TG))
    in_specs = [wide(first), wide(0), wide(0), wide(0), edge(first), edge(0), edge(0), edge(0)]
    in_specs += [
        full(64, BLK),
        pl.BlockSpec((TG, 2 * BLK, BLK), lambda l, *_: (here(l) + first, 0, 0)),
        wide(first),
        wide(first),
        pl.BlockSpec((TG, BLK, 2 * BLK), lambda l, *_: (here(l) + first, 0, 0)),
        pl.BlockSpec((TG, BLK), lambda l, *_: (done(l), 0)),
        pl.BlockSpec((TG, BLK), lambda l, *_: (done(l), 0)),
        full(16, 32),
    ]
    keep = [
        jax.ShapeDtypeStruct((TG, 32, BLK), jnp.float32),
        jax.ShapeDtypeStruct((HALO + 2 * TG, 32, BLK), jnp.float32),
        jax.ShapeDtypeStruct((HALO + 2 * TG, 32, BLK), jnp.float32),
    ]
    operands = [kinds, coefs, own, *got, own, *got, w, tables, mask, bg, inv, a, b, yw]
    if carried:
        in_specs += [full(*k.shape) for k in keep]
        operands += list(state)
    grid_spec = pltpu.PrefetchScalarGridSpec(
        num_scalar_prefetch=2,
        grid=(steps,),
        in_specs=in_specs,
        out_specs=[
            pl.BlockSpec((32, GW), lambda l, *_: (0, done(l) - finals)),
            pl.BlockSpec((2, GW), lambda l, *_: (0, done(l) - finals)),
            *[full(*k.shape) for k in keep],
        ],
        scratch_shapes=[
            pltpu.VMEM((2, 32, GW + BLK), jnp.bfloat16),
            pltpu.VMEM((2, TG, 32, BLK), jnp.float32),
            pltpu.VMEM((HALO + 2 * TG, 32, BLK), jnp.float32),
            pltpu.VMEM((HALO + 2 * TG, 32, BLK), jnp.float32),
        ],
    )
    outs = pl.pallas_call(
        functools.partial(rows_kernel, first, groups, finals, carried),
        grid_spec=grid_spec,
        out_shape=[
            jax.ShapeDtypeStruct((32, n_final * GW), jnp.bfloat16),
            jax.ShapeDtypeStruct((2, n_final * GW), jnp.float32),
            *keep,
        ],
        compiler_params=pltpu.CompilerParams(vmem_limit_bytes=VMEM_LIMIT),
    )(*operands)
    return outs[0], outs[1], tuple(outs[2:])


def columns_kernel(w_ref, ends_ref, e0, e1, e2, e3, n0, n1, *rest):
    out_ref = rest[-1]
    rows = jnp.concatenate([e0[...], e1[...], e2[...], e3[...]], axis=0)
    both = jnp.dot(w_ref[...], rows, preferred_element_type=jnp.float32)
    forced = n0[...] + n1[...]
    value = both[:32] + both[32:]
    value = value + ends_ref[:, 0:1] * forced[0:1, :] + ends_ref[:, 1:2] * forced[1:2, :]
    out_ref[...] = value


def run_columns(start, width, total, w, ends, pieces, near, far, so_far):
    cw = GW
    steps = width // cw
    full = lambda *shape: pl.BlockSpec(shape, lambda l: (0,) * len(shape))
    part = lambda rows: pl.BlockSpec((rows, cw), lambda l: (0, l))
    operands = [w, ends, *pieces, near, far]
    in_specs = [full(64, BLK), full(32, 2), *[part(32)] * 4, part(2), part(2)]
    aliases = {}
    if so_far is not None:
        operands.append(so_far)
        in_specs.append(pl.BlockSpec(memory_space=pl.ANY))
        aliases = {8: 0}
    return pl.pallas_call(
        columns_kernel,
        grid=(steps,),
        in_specs=in_specs,
        out_specs=pl.BlockSpec((32, cw), lambda l: (0, l + start // cw)),
        out_shape=jax.ShapeDtypeStruct((32, total), jnp.float32),
        input_output_aliases=aliases,
        compiler_params=pltpu.CompilerParams(vmem_limit_bytes=VMEM_LIMIT),
    )(*operands)


def body(
    panels,
    void_mask,
    background,
    row_offset,
    row_frac,
    tile_kind,
    tile_shift,
    tile_frac,
    inverse_x,
    couple_x,
    inverse_y,
    couple_y,
):
    rows = row_offset.shape[0]
    width = background.shape[1]
    groups = width // GW
    n_wide = lax.axis_size("wide")
    mine = lax.axis_index("band")
    block = lax.axis_index("wide")
    across = [(d, d ^ 2) for d in range(4)]
    sibling = [(d, d ^ 1) for d in range(4)]
    swap = lambda value, pairs: lax.ppermute(value, "band", pairs)

    near = swap(panels, sibling)
    bounds = [(SPLITS[i], SPLITS[i + 1]) for i in range(len(SPLITS) - 1)]
    gathered = []
    for first, stop in bounds:
        cols = slice(first * GW, stop * GW + BLK)
        far = swap(panels[:, cols], across)
        gathered.append((near[:, cols], far, swap(far, sibling)))

    order = ((jnp.arange(4, dtype=jnp.int32) ^ mine)[:, None] * rows + jnp.arange(rows)[None, :]).reshape(-1)
    w = jnp.concatenate(
        [
            row_matrix(row_offset, row_frac, order, linear_terms),
            row_matrix(row_offset, row_frac, order, cubic_terms),
        ],
        axis=0,
    )
    kinds = (tile_kind == 1).astype(jnp.int32)
    tables = column_tables(tile_kind, tile_shift, tile_frac)
    inv_xt = jnp.concatenate(table_hi_lo(jnp.swapaxes(inverse_x, 1, 2)), axis=2)
    a_x = couple_x[0][:, None] * inverse_x[:, :, 0]
    b_x = couple_x[1][:, None] * inverse_x[:, :, -1]
    coefs = jnp.stack([a_x[:, 0], b_x[:, 0], a_x[:, -1], b_x[:, -1]])
    coefs = jnp.pad(coefs, ((0, 0), (PAD, 2 * PAD)))

    a_y = couple_y[0][:, None] * inverse_y[:, :, 0]
    b_y = couple_y[1][:, None] * inverse_y[:, :, -1]
    corner = jnp.pad(
        jnp.stack([a_y[:, 0], b_y[:, 0], a_y[:, -1], b_y[:, -1]]), ((0, 0), (HALO, HALO))
    )
    corner = lax.dynamic_slice_in_dim(corner, block, 2 * HALO + 1, 1)
    own_inv = lax.dynamic_index_in_dim(inverse_y, block, 0, keepdims=False)
    at = mine * rows
    own_rows = lax.dynamic_slice_in_dim(own_inv, at, rows, 0)
    shuffled = jnp.concatenate(
        [lax.dynamic_slice_in_dim(own_rows, (q ^ mine) * rows, rows, 1) for q in range(4)], axis=1
    )
    w_y = jnp.concatenate(table_hi_lo(shuffled), axis=0)
    ends_y = jnp.stack(
        [
            couple_y[0, block] * own_rows[:, 0],
            couple_y[1, block] * own_rows[:, -1],
        ],
        axis=1,
    )
    end_rows = lax.dynamic_slice_in_dim(jnp.stack([own_inv[0], own_inv[-1]]), at, rows, 1)
    end_hi, end_lo = table_hi_lo(end_rows)
    gap = jnp.zeros((6, rows), jnp.bfloat16)
    yw = jnp.concatenate([end_hi, gap, end_lo, gap], axis=0)

    def neighbour(value, k):
        pairs = [(i + k, i) for i in range(n_wide) if 0 <= i + k < n_wide]
        return lax.ppermute(value, "wide", pairs)

    state = None
    result = None
    position = 0
    for (first, stop), got in zip(bounds, gathered):
        got = (got[0], got[1], got[2])
        east_west, part, state = run_rows(
            first, stop, groups, state, kinds, coefs, panels, got, w, tables,
            void_mask, background, inv_xt, a_x, b_x, yw,
        )
        far = swap(east_west, across)
        close = swap(east_west, sibling)
        f, l = {0: part[0:1]}, {0: part[1:2]}
        for k in (-1, 1):
            pair = neighbour(part, k)
            f[k], l[k] = pair[0:1], pair[1:2]
        for k in (2, 3):
            l[-k] = neighbour(part[1:2], -k)
            f[k] = neighbour(part[0:1], k)
        af, cf, al, cl = [{k: corner[r, HALO + k] for k in range(-HALO, HALO + 1)} for r in range(4)]
        l_m2 = l[-2] + al[-2] * l[-3] + cl[-2] * f[-1]
        f_0 = f[0] + af[0] * l[-1] + cf[0] * f[1]
        l_0 = l[0] + al[0] * l[-1] + cl[0] * f[1]
        f_p2 = f[2] + af[2] * l[1] + cf[2] * f[3]
        south = l[-1] + al[-1] * l_m2 + cl[-1] * f_0
        north = f[1] + af[1] * l_0 + cf[1] * f_p2
        forced = jnp.concatenate([south, north], axis=0)
        forced = forced + swap(forced, across)
        other = swap(forced, sibling)
        pieces = (east_west, close, far, swap(far, sibling))
        result = run_columns(
            position, east_west.shape[1], width, w_y, ends_y, pieces, forced, other, result
        )
        position += east_west.shape[1]
    return result


def solution(mesh):
    placed = (
        P(("wide", "band"), None),
        P(("wide", "band"), None),
        P(("wide", "band"), None),
        P(("wide", "band")),
        P(("wide", "band")),
        P(),
        P(),
        P(),
        P(),
        P(),
        P(),
        P(),
    )
    return jax.shard_map(
        body, mesh=mesh, in_specs=placed, out_specs=P(("wide", "band"), None), check_vma=False
    )
```

```python
import functools

import jax
import jax.numpy as jnp
from jax import lax
from jax.experimental import pallas as pl
from jax.experimental.pallas import tpu as pltpu
from jax.sharding import PartitionSpec as P

BLK = 128
TG = 8
GW = TG * BLK
HALO = 3
PAD = 8
CW = 2048
SPLITS = (0, 16)
VMEM_LIMIT = 48 * 1024 * 1024


def cubic_terms(frac):
    f2 = frac * frac
    f3 = f2 * frac
    return [
        -0.5 * f3 + f2 - 0.5 * frac,
        1.5 * f3 - 2.5 * f2 + 1.0,
        -1.5 * f3 + 2.0 * f2 + 0.5 * frac,
        0.5 * f3 - 0.5 * f2,
    ]


def linear_terms(frac):
    zeros = jnp.zeros_like(frac)
    return [zeros, 1.0 - frac, frac, zeros]


def row_matrix(offsets, fracs, columns, terms):
    total = jnp.zeros((offsets.shape[0], columns.shape[0]), jnp.float32)
    for index, weight in enumerate(terms(fracs)):
        hit = (columns[None, :] == offsets[:, None] + index).astype(jnp.float32)
        total = total + weight[:, None] * hit
    return total.astype(jnp.bfloat16)


def tap_weights(kind, frac):
    taps = [
        jnp.where(kind == 1, wc, wl)
        for wc, wl in zip(cubic_terms(frac), linear_terms(frac))
    ]
    return lax.reduce_precision(jnp.stack(taps), 8, 7)


def tables_kernel(shift_ref, tap_ref, couple_ref, inv_ref, t_ref, pair_ref, a_ref, b_ref):
    step = pl.program_id(0)
    shape = (2 * BLK, BLK)
    delta = lax.broadcasted_iota(jnp.int32, shape, 0) - lax.broadcasted_iota(jnp.int32, shape, 1)
    for i in range(TG):
        tile = step * TG + i
        tap = delta - shift_ref[tile]
        total = jnp.zeros(shape, jnp.float32)
        for k in range(4):
            total = jnp.where(tap == k, tap_ref[k, tile], total)
        t_ref[i] = total.astype(jnp.bfloat16)
        turned = inv_ref[i].T
        hi, lo = split_hi_lo(turned)
        pair_ref[i, :, :BLK] = hi
        pair_ref[i, :, BLK:] = lo
        a_ref[i : i + 1, :] = couple_ref[0, tile] * turned[0:1, :]
        b_ref[i : i + 1, :] = couple_ref[1, tile] * turned[BLK - 1 :, :]


def run_tables(shift, taps, couple, inverse):
    tiles = inverse.shape[0]
    cube = lambda *shape: pl.BlockSpec((TG, *shape), lambda l, *_: (l,) + (0,) * len(shape))
    return pl.pallas_call(
        tables_kernel,
        grid_spec=pltpu.PrefetchScalarGridSpec(
            num_scalar_prefetch=3,
            grid=(tiles // TG,),
            in_specs=[cube(BLK, BLK)],
            out_specs=[cube(2 * BLK, BLK), cube(BLK, 2 * BLK), cube(BLK), cube(BLK)],
        ),
        out_shape=[
            jax.ShapeDtypeStruct((tiles, 2 * BLK, BLK), jnp.bfloat16),
            jax.ShapeDtypeStruct((tiles, BLK, 2 * BLK), jnp.bfloat16),
            jax.ShapeDtypeStruct((tiles, BLK), jnp.float32),
            jax.ShapeDtypeStruct((tiles, BLK), jnp.float32),
        ],
        compiler_params=pltpu.CompilerParams(vmem_limit_bytes=VMEM_LIMIT),
    )(shift, taps, couple, inverse)


def table_hi_lo(value):
    hi = lax.reduce_precision(value, 8, 7)
    return hi.astype(jnp.bfloat16), (value - hi).astype(jnp.bfloat16)


def split_hi_lo(value):
    hi = value.astype(jnp.bfloat16)
    lo = (value - hi.astype(jnp.float32)).astype(jnp.bfloat16)
    return hi, lo


def rows_kernel(first, groups, finals, carried, *refs):
    kind_ref, coef_ref = refs[:2]
    refs = refs[2:]
    (p0, p1, p2, p3, q0, q1, q2, q3, w_ref, t_ref, mask_ref, bg_ref, inv_ref) = refs[:13]
    refs = refs[13:]
    a_ref, b_ref, yw_ref = refs[:3]
    refs = refs[3:]
    if carried:
        u_in, f_in, l_in = refs[:3]
        refs = refs[3:]
    out_ref, part_ref, u_out, f_out, l_out, sec, u_st, f_st, l_st = refs
    step = pl.program_id(0)
    s = step + first

    @pl.when(step == 0)
    def _():
        if carried:
            u_st[0] = u_in[...]
            f_st[...] = f_in[...]
            l_st[...] = l_in[...]
        else:
            u_st[...] = jnp.zeros_like(u_st)
            f_st[...] = jnp.zeros_like(f_st)
            l_st[...] = jnp.zeros_like(l_st)

    @pl.when(step > 0)
    def _():
        u_st[0] = u_st[1]

    for st in (f_st, l_st):
        for i in range(HALO + TG):
            st[i] = st[i + TG]

    @pl.when(s < groups)
    def _():
        rows = jnp.concatenate([p0[...], p1[...], p2[...], p3[...]], axis=0)
        edge = jnp.concatenate([q0[...], q1[...], q2[...], q3[...]], axis=0)
        w = w_ref[...]
        both = jnp.dot(w, rows, preferred_element_type=jnp.float32).astype(jnp.bfloat16)
        tail = jnp.dot(w, edge, preferred_element_type=jnp.float32).astype(jnp.bfloat16)
        for k in range(2):
            sec[k, :, :GW] = both[k * 32 : (k + 1) * 32]
            sec[k, :, GW:] = tail[k * 32 : (k + 1) * 32]
        ests = []
        for i in range(TG):
            kind = kind_ref[s * TG + i]
            taken = sec[kind, :, i * BLK : (i + 2) * BLK]
            ests.append(jnp.dot(taken, t_ref[i], preferred_element_type=jnp.float32))
        sides = []
        for i in range(TG):
            cols = slice(i * BLK, (i + 1) * BLK)
            misfit = mask_ref[:, cols].astype(jnp.float32) * (ests[i] - bg_ref[:, cols])
            sides.append(jnp.concatenate(split_hi_lo(misfit), axis=0))
        solved = [
            jnp.dot(sides[i], inv_ref[i], preferred_element_type=jnp.float32) for i in range(TG)
        ]
        for i in range(TG):
            u = solved[i][:32, :BLK] + (solved[i][32:, :BLK] + solved[i][:32, BLK:])
            u_st[1, i] = u
            f_st[HALO + TG + i] = jnp.broadcast_to(u[:, :1], u.shape)
            l_st[HALO + TG + i] = jnp.broadcast_to(u[:, BLK - 1 :], u.shape)

    @pl.when(s >= groups)
    def _():
        for i in range(TG):
            f_st[HALO + TG + i] = jnp.zeros((32, BLK), jnp.float32)
            l_st[HALO + TG + i] = jnp.zeros((32, BLK), jnp.float32)

    @pl.when(s - 1 >= finals)
    def _():
        base = (s - 1) * TG + PAD - HALO

        def advance(which, j, west, east):
            st, r = (f_st, 0) if which == "f" else (l_st, 2)
            return st[j] + coef_ref[r, base + j] * west + coef_ref[r + 1, base + j] * east

        l1 = {j: advance("l", j, l_st[j - 1], f_st[j + 1]) for j in range(1, HALO + TG)}
        f1 = {j: advance("f", j, l_st[j - 1], f_st[j + 1]) for j in range(HALO, HALO + TG + 2)}
        outs = []
        for i in range(TG):
            j = HALO + i
            west = advance("l", j - 1, l1[j - 2], f1[j])
            east = advance("f", j + 1, l1[j], f1[j + 2])
            value = u_st[0, i] + a_ref[i : i + 1, :] * west + b_ref[i : i + 1, :] * east
            value = value.astype(jnp.bfloat16)
            out_ref[:, i * BLK : (i + 1) * BLK] = value
            outs.append(value)
        ends = jnp.dot(
            yw_ref[...], jnp.concatenate(outs, axis=1), preferred_element_type=jnp.float32
        )
        ends = ends[0:8] + ends[8:16]
        for i in range(TG):
            for k in range(2):
                part_ref[k, i : i + 1, :] = ends[k : k + 1, i * BLK : (i + 1) * BLK]

    @pl.when(step == pl.num_programs(0) - 1)
    def _():
        u_out[...] = u_st[1]
        f_out[...] = f_st[...]
        l_out[...] = l_st[...]


def run_rows(first, stop, groups, state, kinds, coefs, own, got, w, tables, mask, bg, inv, a, b, yw):
    ends_here = stop == groups
    steps = stop - first + (1 if ends_here else 0)
    finals = 0 if first == 0 else first - 1
    n_final = (stop if ends_here else stop - 1) - finals
    carried = state is not None
    count = stop - first
    here = lambda l: jnp.minimum(l, count - 1)
    done = lambda l: jnp.clip(l + first - 1, finals, finals + n_final - 1)
    full = lambda *shape: pl.BlockSpec(shape, lambda l, *_: (0,) * len(shape))
    wide = lambda off: pl.BlockSpec((32, GW), lambda l, *_: (0, here(l) + off))
    edge = lambda off: pl.BlockSpec((32, BLK), lambda l, *_: (0, (here(l) + off + 1) * TG))
    in_specs = [wide(first), wide(0), wide(0), wide(0), edge(first), edge(0), edge(0), edge(0)]
    in_specs += [
        full(64, BLK),
        pl.BlockSpec((TG, 2 * BLK, BLK), lambda l, *_: (here(l) + first, 0, 0)),
        wide(first),
        wide(first),
        pl.BlockSpec((TG, BLK, 2 * BLK), lambda l, *_: (here(l) + first, 0, 0)),
        pl.BlockSpec((TG, BLK), lambda l, *_: (done(l), 0)),
        pl.BlockSpec((TG, BLK), lambda l, *_: (done(l), 0)),
        full(16, 32),
    ]
    keep = [
        jax.ShapeDtypeStruct((TG, 32, BLK), jnp.float32),
        jax.ShapeDtypeStruct((HALO + 2 * TG, 32, BLK), jnp.float32),
        jax.ShapeDtypeStruct((HALO + 2 * TG, 32, BLK), jnp.float32),
    ]
    operands = [kinds, coefs, own, *got, own, *got, w, tables, mask, bg, inv, a, b, yw]
    if carried:
        in_specs += [full(*k.shape) for k in keep]
        operands += list(state)
    grid_spec = pltpu.PrefetchScalarGridSpec(
        num_scalar_prefetch=2,
        grid=(steps,),
        in_specs=in_specs,
        out_specs=[
            pl.BlockSpec((32, GW), lambda l, *_: (0, done(l) - finals)),
            pl.BlockSpec((2, TG, BLK), lambda l, *_: (0, done(l) - finals, 0)),
            *[full(*k.shape) for k in keep],
        ],
        scratch_shapes=[
            pltpu.VMEM((2, 32, GW + BLK), jnp.bfloat16),
            pltpu.VMEM((2, TG, 32, BLK), jnp.float32),
            pltpu.VMEM((HALO + 2 * TG, 32, BLK), jnp.float32),
            pltpu.VMEM((HALO + 2 * TG, 32, BLK), jnp.float32),
        ],
    )
    outs = pl.pallas_call(
        functools.partial(rows_kernel, first, groups, finals, carried),
        grid_spec=grid_spec,
        out_shape=[
            jax.ShapeDtypeStruct((32, n_final * GW), jnp.bfloat16),
            jax.ShapeDtypeStruct((2, n_final * TG, BLK), jnp.float32),
            *keep,
        ],
        compiler_params=pltpu.CompilerParams(vmem_limit_bytes=VMEM_LIMIT),
    )(*operands)
    return outs[0], outs[1], tuple(outs[2:])


def columns_kernel(w_ref, ends_ref, e0, e1, e2, e3, n0, n1, *rest):
    out_ref = rest[-1]
    rows = jnp.concatenate([e0[...], e1[...], e2[...], e3[...]], axis=0)
    both = jnp.dot(w_ref[...], rows, preferred_element_type=jnp.float32)
    value = both[:32] + both[32:]
    south, north = ends_ref[:, 0:1], ends_ref[:, 1:2]
    for i in range(CW // BLK):
        cols = slice(i * BLK, (i + 1) * BLK)
        row = [n0[k, i : i + 1, :] + n1[k, i : i + 1, :] for k in range(2)]
        out_ref[:, cols] = value[:, cols] + south * row[0] + north * row[1]


def run_columns(start, width, total, w, ends, pieces, near, far, so_far):
    cw = CW
    steps = width // cw
    full = lambda *shape: pl.BlockSpec(shape, lambda l: (0,) * len(shape))
    part = lambda rows: pl.BlockSpec((rows, cw), lambda l: (0, l))
    forced = pl.BlockSpec((2, cw // BLK, BLK), lambda l: (0, l + start // cw, 0))
    operands = [w, ends, *pieces, near, far]
    in_specs = [full(64, BLK), full(32, 2), *[part(32)] * 4, forced, forced]
    aliases = {}
    if so_far is not None:
        operands.append(so_far)
        in_specs.append(pl.BlockSpec(memory_space=pl.ANY))
        aliases = {8: 0}
    return pl.pallas_call(
        columns_kernel,
        grid=(steps,),
        in_specs=in_specs,
        out_specs=pl.BlockSpec((32, cw), lambda l: (0, l + start // cw)),
        out_shape=jax.ShapeDtypeStruct((32, total), jnp.float32),
        input_output_aliases=aliases,
        compiler_params=pltpu.CompilerParams(vmem_limit_bytes=VMEM_LIMIT),
    )(*operands)


def body(
    panels,
    void_mask,
    background,
    row_offset,
    row_frac,
    tile_kind,
    tile_shift,
    tile_frac,
    inverse_x,
    couple_x,
    inverse_y,
    couple_y,
):
    rows = row_offset.shape[0]
    width = background.shape[1]
    groups = width // GW
    n_wide = lax.axis_size("wide")
    mine = lax.axis_index("band")
    block = lax.axis_index("wide")
    across = [(d, d ^ 2) for d in range(4)]
    sibling = [(d, d ^ 1) for d in range(4)]
    swap = lambda value, pairs: lax.ppermute(value, "band", pairs)

    near = swap(panels, sibling)
    bounds = [(SPLITS[i], SPLITS[i + 1]) for i in range(len(SPLITS) - 1)]
    gathered = []
    for first, stop in bounds:
        cols = slice(first * GW, stop * GW + BLK)
        far = swap(panels[:, cols], across)
        gathered.append((near[:, cols], far, swap(far, sibling)))

    order = ((jnp.arange(4, dtype=jnp.int32) ^ mine)[:, None] * rows + jnp.arange(rows)[None, :]).reshape(-1)
    w = jnp.concatenate(
        [
            row_matrix(row_offset, row_frac, order, linear_terms),
            row_matrix(row_offset, row_frac, order, cubic_terms),
        ],
        axis=0,
    )
    kinds = (tile_kind == 1).astype(jnp.int32)
    tables, inv_xt, a_x, b_x = run_tables(
        tile_shift, tap_weights(tile_kind, tile_frac), couple_x, inverse_x
    )
    coefs = jnp.stack([a_x[:, 0], b_x[:, 0], a_x[:, -1], b_x[:, -1]])
    coefs = jnp.pad(coefs, ((0, 0), (PAD, 2 * PAD)))

    tips = inverse_y[:, :: BLK - 1, :: BLK - 1] * couple_y.T[:, None, :]
    corner = jnp.stack([tips[:, 0, 0], tips[:, 0, 1], tips[:, 1, 0], tips[:, 1, 1]])
    corner = jnp.pad(corner, ((0, 0), (HALO, HALO)))
    corner = lax.dynamic_slice_in_dim(corner, block, 2 * HALO + 1, 1)
    own_inv = lax.dynamic_index_in_dim(inverse_y, block, 0, keepdims=False)
    at = mine * rows
    own_rows = lax.dynamic_slice_in_dim(own_inv, at, rows, 0)
    shuffled = jnp.concatenate(
        [lax.dynamic_slice_in_dim(own_rows, (q ^ mine) * rows, rows, 1) for q in range(4)], axis=1
    )
    w_y = jnp.concatenate(table_hi_lo(shuffled), axis=0)
    ends_y = jnp.stack(
        [
            couple_y[0, block] * own_rows[:, 0],
            couple_y[1, block] * own_rows[:, -1],
        ],
        axis=1,
    )
    end_rows = lax.dynamic_slice_in_dim(jnp.stack([own_inv[0], own_inv[-1]]), at, rows, 1)
    end_hi, end_lo = table_hi_lo(end_rows)
    gap = jnp.zeros((6, rows), jnp.bfloat16)
    yw = jnp.concatenate([end_hi, gap, end_lo, gap], axis=0)

    state = None
    sent = []
    parts = []
    for (first, stop), got in zip(bounds, gathered):
        east_west, part, state = run_rows(
            first, stop, groups, state, kinds, coefs, panels, got, w, tables,
            void_mask, background, inv_xt, a_x, b_x, yw,
        )
        far = swap(east_west, across)
        sent.append((east_west, swap(east_west, sibling), far, swap(far, sibling)))
        parts.append(part)
    part = jnp.concatenate(parts, axis=1) if len(parts) > 1 else parts[0]

    every = [(d, k) for d in range(4) for k in range(n_wide)]
    at = lambda d, k: d * n_wide + k
    fetch = lambda db, dw: lax.ppermute(
        part, ("band", "wide"), [(at(d ^ db, k ^ dw), at(d, k)) for d, k in every]
    )
    second = block % 2
    own = part + fetch(2, 0)
    other = fetch(0, 1) + fetch(2, 1)
    even = jnp.where(second == 0, own, other)
    odd = jnp.where(second == 0, other, own)
    shifted = lambda value, k: lax.ppermute(
        value, "wide", [(i, i + 2 * k) for i in range(n_wide) if 0 <= i + 2 * k < n_wide]
    )
    before = shifted(jnp.stack([even[1], odd[0], odd[1]]), 1)
    after = shifted(jnp.stack([even[0], even[1], odd[0]]), -1)
    beyond = lax.ppermute(
        jnp.where(second == 0, odd[1], even[0]),
        "wide",
        [(i, j) for i in range(n_wide) for j in [i + 4 * (1 - 2 * (i % 2))] if 0 <= j < n_wide],
    )
    pick = lambda first, last: jnp.where(second == 0, first, last)
    f = {0: own[0], -1: pick(before[1], other[0]), 1: pick(other[0], after[0])}
    l = {0: own[1], -1: pick(before[2], other[1]), 1: pick(other[1], after[1])}
    l[-2], l[-3] = pick(before[0], before[2]), pick(beyond, before[0])
    f[2], f[3] = pick(after[0], after[2]), pick(after[2], beyond)
    af, cf, al, cl = [{k: corner[r, HALO + k] for k in range(-HALO, HALO + 1)} for r in range(4)]
    l_m2 = l[-2] + al[-2] * l[-3] + cl[-2] * f[-1]
    f_0 = f[0] + af[0] * l[-1] + cf[0] * f[1]
    l_0 = l[0] + al[0] * l[-1] + cl[0] * f[1]
    f_p2 = f[2] + af[2] * l[1] + cf[2] * f[3]
    south = l[-1] + al[-1] * l_m2 + cl[-1] * f_0
    north = f[1] + af[1] * l_0 + cf[1] * f_p2
    forced = jnp.stack([south, north])
    rest = swap(forced, sibling)

    result = None
    position = 0
    for pieces in sent:
        size = pieces[0].shape[1]
        result = run_columns(position, size, width, w_y, ends_y, pieces, forced, rest, result)
        position += size
    return result


def solution(mesh):
    placed = (
        P(("wide", "band"), None),
        P(("wide", "band"), None),
        P(("wide", "band"), None),
        P(("wide", "band")),
        P(("wide", "band")),
        P(),
        P(),
        P(),
        P(),
        P(),
        P(),
        P(),
    )
    return jax.shard_map(
        body, mesh=mesh, in_specs=placed, out_specs=P(("wide", "band"), None), check_vma=False
    )
```

```python
import functools

import jax
import jax.numpy as jnp
from jax import lax
from jax.experimental import pallas as pl
from jax.experimental.pallas import tpu as pltpu
from jax.sharding import PartitionSpec as P

BLK = 128
TG = 8
GW = TG * BLK
HALO = 3
CW = 1024
SPLITS = (0, 8, 16)
VMEM_LIMIT = 48 * 1024 * 1024


def cubic_terms(frac):
    f2 = frac * frac
    f3 = f2 * frac
    return [
        -0.5 * f3 + f2 - 0.5 * frac,
        1.5 * f3 - 2.5 * f2 + 1.0,
        -1.5 * f3 + 2.0 * f2 + 0.5 * frac,
        0.5 * f3 - 0.5 * f2,
    ]


def linear_terms(frac):
    zeros = jnp.zeros_like(frac)
    return [zeros, 1.0 - frac, frac, zeros]


def row_matrix(offsets, fracs, columns, terms):
    total = jnp.zeros((offsets.shape[0], columns.shape[0]), jnp.float32)
    for index, weight in enumerate(terms(fracs)):
        hit = (columns[None, :] == offsets[:, None] + index).astype(jnp.float32)
        total = total + weight[:, None] * hit
    return total.astype(jnp.bfloat16)


def tap_weights(kind, frac):
    taps = [
        jnp.where(kind == 1, wc, wl)
        for wc, wl in zip(cubic_terms(frac), linear_terms(frac))
    ]
    return lax.reduce_precision(jnp.stack(taps), 8, 7)


NT = (((1,), (1,)), ((), ()))


def tables_kernel(shift_ref, tap_ref, couple_ref, inv_ref, t_ref, corr_ref, a_ref, b_ref):
    step = pl.program_id(0)
    shape = (2 * BLK, BLK)
    delta = lax.broadcasted_iota(jnp.int32, shape, 0) - lax.broadcasted_iota(jnp.int32, shape, 1)
    place = lax.broadcasted_iota(jnp.int32, (16, BLK), 0) * (BLK - 1)
    units = (place == lax.broadcasted_iota(jnp.int32, (16, BLK), 1)).astype(jnp.bfloat16)
    row = lax.broadcasted_iota(jnp.int32, (2 * TG, BLK), 0)
    for i in range(TG):
        tile = step * TG + i
        tap = delta - shift_ref[tile]
        total = jnp.zeros(shape, jnp.float32)
        for k in range(4):
            total = jnp.where(tap == k, tap_ref[k, tile], total)
        t_ref[i] = total.astype(jnp.bfloat16)
        hi, lo = split_hi_lo(inv_ref[i])
        ends = lax.dot_general(units, hi, NT, preferred_element_type=jnp.float32)
        ends = ends + lax.dot_general(units, lo, NT, preferred_element_type=jnp.float32)
        a = couple_ref[0, tile] * ends[0:1, :]
        b = couple_ref[1, tile] * ends[1:2, :]
        a_ref[i : i + 1, :] = a
        b_ref[i : i + 1, :] = b
        both = jnp.where(row == i, a, jnp.where(row == TG + i, b, 0.0))
        corr_ref[0, :, i * BLK : (i + 1) * BLK] = both.astype(jnp.bfloat16)


def run_tables(shift, taps, couple, inverse):
    tiles = inverse.shape[0]
    cube = lambda *shape: pl.BlockSpec((TG, *shape), lambda l, *_: (l,) + (0,) * len(shape))
    return pl.pallas_call(
        tables_kernel,
        grid_spec=pltpu.PrefetchScalarGridSpec(
            num_scalar_prefetch=3,
            grid=(tiles // TG,),
            in_specs=[cube(BLK, BLK)],
            out_specs=[
                cube(2 * BLK, BLK),
                pl.BlockSpec((1, 2 * TG, GW), lambda l, *_: (l, 0, 0)),
                cube(BLK),
                cube(BLK),
            ],
        ),
        out_shape=[
            jax.ShapeDtypeStruct((tiles, 2 * BLK, BLK), jnp.bfloat16),
            jax.ShapeDtypeStruct((tiles // TG, 2 * TG, GW), jnp.bfloat16),
            jax.ShapeDtypeStruct((tiles, BLK), jnp.float32),
            jax.ShapeDtypeStruct((tiles, BLK), jnp.float32),
        ],
        compiler_params=pltpu.CompilerParams(vmem_limit_bytes=VMEM_LIMIT),
    )(shift, taps, couple, inverse)


def table_hi_lo(value):
    hi = lax.reduce_precision(value, 8, 7)
    return hi.astype(jnp.bfloat16), (value - hi).astype(jnp.bfloat16)


def split_hi_lo(value):
    hi = value.astype(jnp.bfloat16)
    lo = (value - hi.astype(jnp.float32)).astype(jnp.bfloat16)
    return hi, lo


def rows_kernel(first, groups, finals, carried, *refs):
    kind_ref, p0, p1, p2, p3, q0, q1, q2, q3, w_ref, t_ref, mask_ref, bg_ref, inv_ref = refs[:14]
    coef_ref, corr_ref, yw_ref = refs[14:17]
    refs = refs[17:]
    if carried:
        u_in, f_in, l_in = refs[:3]
        refs = refs[3:]
    out_ref, part_ref, u_out, f_out, l_out, sec, u_st, f_st, l_st = refs
    step = pl.program_id(0)
    s = step + first
    lane = lax.broadcasted_iota(jnp.int32, (32, BLK), 1)
    roll = lambda value, by: pltpu.roll(value, by % BLK, 1)

    @pl.when(step == 0)
    def _():
        if carried:
            u_st[1] = u_in[...]
            f_st[...] = f_in[...]
            l_st[...] = l_in[...]
        else:
            u_st[...] = jnp.zeros_like(u_st)
            f_st[...] = jnp.zeros_like(f_st)
            l_st[...] = jnp.zeros_like(l_st)

    u_st[0] = u_st[1]
    f_st[...] = jnp.where(lane < HALO + TG, roll(f_st[...], -TG), 0.0)
    l_st[...] = jnp.where(lane < HALO + TG, roll(l_st[...], -TG), 0.0)

    @pl.when(s < groups)
    def _():
        rows = jnp.concatenate([p0[...], p1[...], p2[...], p3[...]], axis=0)
        edge = jnp.concatenate([q0[...], q1[...], q2[...], q3[...]], axis=0)
        w = w_ref[...]
        both = jnp.dot(w, rows, preferred_element_type=jnp.float32).astype(jnp.bfloat16)
        tail = jnp.dot(w, edge, preferred_element_type=jnp.float32).astype(jnp.bfloat16)
        for k in range(2):
            sec[k, :, :GW] = both[k * 32 : (k + 1) * 32]
            sec[k, :, GW:] = tail[k * 32 : (k + 1) * 32]
        ests = []
        for i in range(TG):
            kind = kind_ref[s * TG + i]
            taken = sec[kind, :, i * BLK : (i + 2) * BLK]
            ests.append(jnp.dot(taken, t_ref[i], preferred_element_type=jnp.float32))
        sides = []
        for i in range(TG):
            cols = slice(i * BLK, (i + 1) * BLK)
            misfit = mask_ref[:, cols].astype(jnp.float32) * (ests[i] - bg_ref[:, cols])
            sides.append(jnp.concatenate(split_hi_lo(misfit), axis=0))
        solved = []
        for i in range(TG):
            pair = jnp.concatenate(split_hi_lo(inv_ref[i]), axis=0)
            solved.append(lax.dot_general(sides[i], pair, NT, preferred_element_type=jnp.float32))
        f, l = f_st[...], l_st[...]
        for i in range(TG):
            u = solved[i][:32, :BLK] + (solved[i][32:, :BLK] + solved[i][:32, BLK:])
            u_st[1, i] = u
            here = lane == HALO + TG + i
            f = jnp.where(here, u[:, :1], f)
            l = jnp.where(here, u[:, BLK - 1 :], l)
        f_st[...] = f
        l_st[...] = l

    @pl.when(s - 1 >= finals)
    def _():
        af, cf, al, cl = [coef_ref[r, pl.ds(s - 1, 1), :] for r in range(4)]
        f0, l0 = f_st[...], l_st[...]
        west, east = roll(l0, 1), roll(f0, -1)
        f1 = f0 + af * west + cf * east
        l1 = l0 + al * west + cl * east
        west, east = roll(l1, 1), roll(f1, -1)
        f2 = f0 + af * west + cf * east
        l2 = l0 + al * west + cl * east
        ends = jnp.where(lane < TG, roll(l2, 1 - HALO), roll(f2, TG - 1 - HALO))
        ends = ends[:, : 2 * TG].astype(jnp.bfloat16)
        fix = jnp.dot(ends, corr_ref[0], preferred_element_type=jnp.float32)
        outs = []
        for i in range(TG):
            cols = slice(i * BLK, (i + 1) * BLK)
            value = (u_st[0, i] + fix[:, cols]).astype(jnp.bfloat16)
            out_ref[:, cols] = value
            outs.append(value)
        tips = jnp.dot(
            yw_ref[...], jnp.concatenate(outs, axis=1), preferred_element_type=jnp.float32
        )
        tips = tips[0:8] + tips[8:16]
        for i in range(TG):
            for k in range(2):
                part_ref[k, i : i + 1, :] = tips[k : k + 1, i * BLK : (i + 1) * BLK]

    @pl.when(step == pl.num_programs(0) - 1)
    def _():
        u_out[...] = u_st[1]
        f_out[...] = f_st[...]
        l_out[...] = l_st[...]


def run_rows(first, stop, groups, state, kinds, own, got, w, tables, mask, bg, inv, coefs, corr, yw):
    ends_here = stop == groups
    steps = stop - first + (1 if ends_here else 0)
    finals = 0 if first == 0 else first - 1
    n_final = (stop if ends_here else stop - 1) - finals
    carried = state is not None
    count = stop - first
    near, far, away = got
    here = lambda l: jnp.minimum(l, count - 1)
    done = lambda l: jnp.clip(l + first - 1, finals, finals + n_final - 1)
    full = lambda *shape: pl.BlockSpec(shape, lambda l, *_: (0,) * len(shape))
    wide = lambda off: pl.BlockSpec((32, GW), lambda l, *_: (0, here(l) + off))
    edge = lambda off: pl.BlockSpec((32, BLK), lambda l, *_: (0, (here(l) + off + 1) * TG))
    cube = lambda *shape: pl.BlockSpec((TG, *shape), lambda l, *_: (here(l) + first, 0, 0))
    in_specs = [wide(first), wide(first), wide(0), wide(0)]
    in_specs += [edge(first), edge(first), edge(0), edge(0)]
    in_specs += [
        full(64, BLK),
        cube(2 * BLK, BLK),
        wide(first),
        wide(first),
        cube(BLK, BLK),
        full(*coefs.shape),
        pl.BlockSpec((1, 2 * TG, GW), lambda l, *_: (done(l), 0, 0)),
        full(16, 32),
    ]
    keep = [
        jax.ShapeDtypeStruct((TG, 32, BLK), jnp.float32),
        jax.ShapeDtypeStruct((32, BLK), jnp.float32),
        jax.ShapeDtypeStruct((32, BLK), jnp.float32),
    ]
    operands = [kinds, own, near, far, away, own, near, far, away, w, tables, mask, bg, inv]
    operands += [coefs, corr, yw]
    if carried:
        in_specs += [full(*k.shape) for k in keep]
        operands += list(state)
    grid_spec = pltpu.PrefetchScalarGridSpec(
        num_scalar_prefetch=1,
        grid=(steps,),
        in_specs=in_specs,
        out_specs=[
            pl.BlockSpec((32, GW), lambda l, *_: (0, done(l) - finals)),
            pl.BlockSpec((2, TG, BLK), lambda l, *_: (0, done(l) - finals, 0)),
            *[full(*k.shape) for k in keep],
        ],
        scratch_shapes=[
            pltpu.VMEM((2, 32, GW + BLK), jnp.bfloat16),
            pltpu.VMEM((2, TG, 32, BLK), jnp.float32),
            pltpu.VMEM((32, BLK), jnp.float32),
            pltpu.VMEM((32, BLK), jnp.float32),
        ],
    )
    outs = pl.pallas_call(
        functools.partial(rows_kernel, first, groups, finals, carried),
        grid_spec=grid_spec,
        out_shape=[
            jax.ShapeDtypeStruct((32, n_final * GW), jnp.bfloat16),
            jax.ShapeDtypeStruct((2, n_final * TG, BLK), jnp.float32),
            *keep,
        ],
        compiler_params=pltpu.CompilerParams(vmem_limit_bytes=VMEM_LIMIT),
    )(*operands)
    return outs[0], outs[1], tuple(outs[2:])


def ends_kernel(block_ref, corner_ref, own, other, before, after, beyond, out):
    block = block_ref[0]
    second = lax.rem(block, 2) == 1
    pick = lambda even, odd: jnp.where(second, odd, even)
    coef = lambda r, k: corner_ref[r, block + HALO + k]
    f = {0: own[0], -1: pick(before[1], other[0]), 1: pick(other[0], after[0])}
    l = {0: own[1], -1: pick(before[2], other[1]), 1: pick(other[1], after[1])}
    l[-2], l[-3] = pick(before[0], before[2]), pick(beyond[...], before[0])
    f[2], f[3] = pick(after[0], after[2]), pick(after[2], beyond[...])
    last = lambda k, west, east: l[k] + coef(2, k) * west + coef(3, k) * east
    head = lambda k, west, east: f[k] + coef(0, k) * west + coef(1, k) * east
    out[0] = last(-1, last(-2, l[-3], f[-1]), head(0, l[-1], f[1]))
    out[1] = head(1, last(0, l[-1], f[1]), head(2, l[1], f[3]))


def run_ends(block, corner, own, *others):
    smem = pl.BlockSpec(memory_space=pltpu.SMEM)
    vmem = pl.BlockSpec(memory_space=pltpu.VMEM)
    return pl.pallas_call(
        ends_kernel,
        in_specs=[smem, smem] + [vmem] * 5,
        out_specs=vmem,
        out_shape=jax.ShapeDtypeStruct(own.shape, own.dtype),
        compiler_params=pltpu.CompilerParams(vmem_limit_bytes=VMEM_LIMIT),
    )(block.reshape(1), corner, own, *others)


def columns_kernel(w_ref, ends_ref, e0, e1, e2, e3, n0, n1, *rest):
    out_ref = rest[-1]
    rows = jnp.concatenate([e0[...], e1[...], e2[...], e3[...]], axis=0)
    both = jnp.dot(w_ref[...], rows, preferred_element_type=jnp.float32)
    value = both[:32] + both[32:]
    south, north = ends_ref[:, 0:1], ends_ref[:, 1:2]
    for i in range(CW // BLK):
        cols = slice(i * BLK, (i + 1) * BLK)
        row = [n0[k, i : i + 1, :] + n1[k, i : i + 1, :] for k in range(2)]
        out_ref[:, cols] = value[:, cols] + south * row[0] + north * row[1]


def run_columns(start, width, total, w, ends, pieces, near, far, so_far):
    cw = CW
    steps = width // cw
    full = lambda *shape: pl.BlockSpec(shape, lambda l: (0,) * len(shape))
    part = lambda rows: pl.BlockSpec((rows, cw), lambda l: (0, l))
    forced = pl.BlockSpec((2, cw // BLK, BLK), lambda l: (0, l + start // cw, 0))
    operands = [w, ends, *pieces, near, far]
    in_specs = [full(64, BLK), full(32, 2), *[part(32)] * 4, forced, forced]
    aliases = {}
    if so_far is not None:
        operands.append(so_far)
        in_specs.append(pl.BlockSpec(memory_space=pl.ANY))
        aliases = {8: 0}
    return pl.pallas_call(
        columns_kernel,
        grid=(steps,),
        in_specs=in_specs,
        out_specs=pl.BlockSpec((32, cw), lambda l: (0, l + start // cw)),
        out_shape=jax.ShapeDtypeStruct((32, total), jnp.float32),
        input_output_aliases=aliases,
        compiler_params=pltpu.CompilerParams(vmem_limit_bytes=VMEM_LIMIT),
    )(*operands)


def body(
    panels,
    void_mask,
    background,
    row_offset,
    row_frac,
    tile_kind,
    tile_shift,
    tile_frac,
    inverse_x,
    couple_x,
    inverse_y,
    couple_y,
):
    rows = row_offset.shape[0]
    width = background.shape[1]
    groups = width // GW
    n_wide = lax.axis_size("wide")
    mine = lax.axis_index("band")
    block = lax.axis_index("wide")
    across = [(d, d ^ 2) for d in range(4)]
    sibling = [(d, d ^ 1) for d in range(4)]
    swap = lambda value, pairs: lax.ppermute(value, "band", pairs)

    near = swap(panels, sibling)
    bounds = [(SPLITS[i], SPLITS[i + 1]) for i in range(len(SPLITS) - 1)]
    gathered = []
    for first, stop in bounds:
        far = swap(panels[:, first * GW : stop * GW + BLK], across)
        gathered.append((near, far, swap(far, sibling)))

    order = ((jnp.arange(4, dtype=jnp.int32) ^ mine)[:, None] * rows + jnp.arange(rows)[None, :]).reshape(-1)
    w = jnp.concatenate(
        [
            row_matrix(row_offset, row_frac, order, linear_terms),
            row_matrix(row_offset, row_frac, order, cubic_terms),
        ],
        axis=0,
    )
    kinds = (tile_kind == 1).astype(jnp.int32)
    tables, corr, a_x, b_x = run_tables(
        tile_shift, tap_weights(tile_kind, tile_frac), couple_x, inverse_x
    )
    coefs = jnp.stack([a_x[:, 0], b_x[:, 0], a_x[:, -1], b_x[:, -1]])
    coefs = jnp.pad(coefs, ((0, 0), (HALO, 2 * TG - HALO))).reshape(4, groups + 2, TG)
    coefs = jnp.concatenate([coefs[:, k : k + groups] for k in range(3)], axis=2)
    coefs = jnp.pad(coefs, ((0, 0), (0, 0), (0, BLK - 3 * TG)))

    tips = inverse_y[:, :: BLK - 1, :: BLK - 1] * couple_y.T[:, None, :]
    corner = jnp.stack([tips[:, 0, 0], tips[:, 0, 1], tips[:, 1, 0], tips[:, 1, 1]])
    corner = jnp.pad(corner, ((0, 0), (HALO, HALO)))
    own_inv = lax.dynamic_index_in_dim(inverse_y, block, 0, keepdims=False)
    at = mine * rows
    own_rows = lax.dynamic_slice_in_dim(own_inv, at, rows, 0)
    shuffled = jnp.concatenate(
        [lax.dynamic_slice_in_dim(own_rows, (q ^ mine) * rows, rows, 1) for q in range(4)], axis=1
    )
    w_y = jnp.concatenate(table_hi_lo(shuffled), axis=0)
    ends_y = jnp.stack(
        [
            couple_y[0, block] * own_rows[:, 0],
            couple_y[1, block] * own_rows[:, -1],
        ],
        axis=1,
    )
    end_rows = lax.dynamic_slice_in_dim(jnp.stack([own_inv[0], own_inv[-1]]), at, rows, 1)
    end_hi, end_lo = table_hi_lo(end_rows)
    gap = jnp.zeros((6, rows), jnp.bfloat16)
    yw = jnp.concatenate([end_hi, gap, end_lo, gap], axis=0)

    state = None
    sent = []
    parts = []
    for (first, stop), got in zip(bounds, gathered):
        east_west, part, state = run_rows(
            first, stop, groups, state, kinds, panels, got, w, tables,
            void_mask, background, inverse_x, coefs, corr, yw,
        )
        far = swap(east_west, across)
        sent.append([east_west, swap(east_west, sibling), far])
        parts.append(part)
    part = jnp.concatenate(parts, axis=1) if len(parts) > 1 else parts[0]

    every = [(d, k) for d in range(4) for k in range(n_wide)]
    at = lambda d, k: d * n_wide + k
    fetch = lambda db, dw: lax.ppermute(
        part, ("band", "wide"), [(at(d ^ db, k ^ dw), at(d, k)) for d, k in every]
    )
    second = block % 2
    own = part + fetch(2, 0)
    other = fetch(0, 1) + fetch(2, 1)
    even = jnp.where(second == 0, own, other)
    odd = jnp.where(second == 0, other, own)
    shifted = lambda value, k: lax.ppermute(
        value, "wide", [(i, i + 2 * k) for i in range(n_wide) if 0 <= i + 2 * k < n_wide]
    )
    before = shifted(jnp.stack([even[1], odd[0], odd[1]]), 1)
    after = shifted(jnp.stack([even[0], even[1], odd[0]]), -1)
    beyond = lax.ppermute(
        jnp.where(second == 0, odd[1], even[0]),
        "wide",
        [(i, j) for i in range(n_wide) for j in [i + 4 * (1 - 2 * (i % 2))] if 0 <= j < n_wide],
    )
    forced = run_ends(block, corner, own, other, before, after, beyond)
    rest = swap(forced, sibling)
    sent[-1][2], rest = lax.optimization_barrier((sent[-1][2], rest))

    result = None
    position = 0
    for pieces in sent:
        size = pieces[0].shape[1]
        pieces = (*pieces, swap(pieces[2], sibling))
        result = run_columns(position, size, width, w_y, ends_y, pieces, forced, rest, result)
        position += size
    return result


def solution(mesh):
    placed = (
        P(("wide", "band"), None),
        P(("wide", "band"), None),
        P(("wide", "band"), None),
        P(("wide", "band")),
        P(("wide", "band")),
        P(),
        P(),
        P(),
        P(),
        P(),
        P(),
        P(),
    )
    return jax.shard_map(
        body, mesh=mesh, in_specs=placed, out_specs=P(("wide", "band"), None), check_vma=False
    )
```

```python
import functools

import jax
import jax.numpy as jnp
from jax import lax
from jax.experimental import pallas as pl
from jax.experimental.pallas import tpu as pltpu
from jax.sharding import PartitionSpec as P

BLK = 128
TG = 32
GW = TG * BLK
SUB = 8
SW = SUB * BLK
HALO = 3
SPLITS = (0, 2, 4)
VMEM_LIMIT = 48 * 1024 * 1024


def cubic_terms(frac):
    f2 = frac * frac
    f3 = f2 * frac
    return [
        -0.5 * f3 + f2 - 0.5 * frac,
        1.5 * f3 - 2.5 * f2 + 1.0,
        -1.5 * f3 + 2.0 * f2 + 0.5 * frac,
        0.5 * f3 - 0.5 * f2,
    ]


def linear_terms(frac):
    zeros = jnp.zeros_like(frac)
    return [zeros, 1.0 - frac, frac, zeros]


def row_matrix(offsets, fracs, columns, terms):
    total = jnp.zeros((offsets.shape[0], columns.shape[0]), jnp.float32)
    for index, weight in enumerate(terms(fracs)):
        hit = (columns[None, :] == offsets[:, None] + index).astype(jnp.float32)
        total = total + weight[:, None] * hit
    return total.astype(jnp.bfloat16)


def tap_weights(kind, frac):
    taps = [
        jnp.where(kind == 1, wc, wl)
        for wc, wl in zip(cubic_terms(frac), linear_terms(frac))
    ]
    return lax.reduce_precision(jnp.stack(taps), 8, 7)


NT = (((1,), (1,)), ((), ()))


def tables_kernel(shift_ref, tap_ref, couple_ref, inv_ref, t_ref, corr_ref, a_ref, b_ref):
    step = pl.program_id(0)
    shape = (2 * BLK, BLK)
    delta = lax.broadcasted_iota(jnp.int32, shape, 0) - lax.broadcasted_iota(jnp.int32, shape, 1)
    place = lax.broadcasted_iota(jnp.int32, (16, BLK), 0) * (BLK - 1)
    units = (place == lax.broadcasted_iota(jnp.int32, (16, BLK), 1)).astype(jnp.bfloat16)
    row = lax.broadcasted_iota(jnp.int32, (2 * SUB, BLK), 0)
    for i in range(TG):
        tile = step * TG + i
        tap = delta - shift_ref[tile]
        total = jnp.zeros(shape, jnp.float32)
        for k in range(4):
            total = jnp.where(tap == k, tap_ref[k, tile], total)
        t_ref[i] = total.astype(jnp.bfloat16)
        hi, lo = split_hi_lo(inv_ref[i])
        ends = lax.dot_general(units, hi, NT, preferred_element_type=jnp.float32)
        ends = ends + lax.dot_general(units, lo, NT, preferred_element_type=jnp.float32)
        a = couple_ref[0, tile] * ends[0:1, :]
        b = couple_ref[1, tile] * ends[1:2, :]
        a_ref[i : i + 1, :] = a
        b_ref[i : i + 1, :] = b
        q, r = divmod(i, SUB)
        both = jnp.where(row == r, a, jnp.where(row == SUB + r, b, 0.0))
        corr_ref[q, :, r * BLK : (r + 1) * BLK] = both.astype(jnp.bfloat16)


def run_tables(shift, taps, couple, inverse):
    tiles = inverse.shape[0]
    cube = lambda *shape: pl.BlockSpec((TG, *shape), lambda l, *_: (l,) + (0,) * len(shape))
    return pl.pallas_call(
        tables_kernel,
        grid_spec=pltpu.PrefetchScalarGridSpec(
            num_scalar_prefetch=3,
            grid=(tiles // TG,),
            in_specs=[cube(BLK, BLK)],
            out_specs=[
                cube(2 * BLK, BLK),
                pl.BlockSpec((TG // SUB, 2 * SUB, SW), lambda l, *_: (l, 0, 0)),
                cube(BLK),
                cube(BLK),
            ],
        ),
        out_shape=[
            jax.ShapeDtypeStruct((tiles, 2 * BLK, BLK), jnp.bfloat16),
            jax.ShapeDtypeStruct((tiles // SUB, 2 * SUB, SW), jnp.bfloat16),
            jax.ShapeDtypeStruct((tiles, BLK), jnp.float32),
            jax.ShapeDtypeStruct((tiles, BLK), jnp.float32),
        ],
        compiler_params=pltpu.CompilerParams(vmem_limit_bytes=VMEM_LIMIT),
    )(shift, taps, couple, inverse)


def table_hi_lo(value):
    hi = lax.reduce_precision(value, 8, 7)
    return hi.astype(jnp.bfloat16), (value - hi).astype(jnp.bfloat16)


def split_hi_lo(value):
    hi = value.astype(jnp.bfloat16)
    lo = (value - hi.astype(jnp.float32)).astype(jnp.bfloat16)
    return hi, lo


def rows_kernel(first, groups, carried, *refs):
    kind_ref, p0, p1, p2, p3, q0, q1, q2, q3, w_ref, t_ref, mask_ref, bg_ref, inv_ref = refs[:14]
    coef_ref, corr_ref, yw_ref = refs[14:17]
    refs = refs[17:]
    if carried:
        u_in, f_in, l_in = refs[:3]
        refs = refs[3:]
    out_ref, part_ref, u_out, f_out, l_out, sec, u_st, f_st, l_st = refs
    step = pl.program_id(0)
    s = step + first
    lane = lax.broadcasted_iota(jnp.int32, (32, BLK), 1)
    roll = lambda value, by: pltpu.roll(value, by % BLK, 1)

    @pl.when(step == 0)
    def _():
        if carried:
            u_st[TG:] = u_in[...]
            f_st[...] = f_in[...]
            l_st[...] = l_in[...]
        else:
            u_st[...] = jnp.zeros_like(u_st)
            f_st[...] = jnp.zeros_like(f_st)
            l_st[...] = jnp.zeros_like(l_st)

    u_st[:SUB] = u_st[TG:]
    rows = jnp.concatenate([p0[...], p1[...], p2[...], p3[...]], axis=0)
    edge = jnp.concatenate([q0[...], q1[...], q2[...], q3[...]], axis=0)
    w = w_ref[...]
    both = jnp.dot(w, rows, preferred_element_type=jnp.float32).astype(jnp.bfloat16)
    tail = jnp.dot(w, edge, preferred_element_type=jnp.float32).astype(jnp.bfloat16)
    for k in range(2):
        sec[k, :, :GW] = both[k * 32 : (k + 1) * 32]
        sec[k, :, GW:] = tail[k * 32 : (k + 1) * 32]
    f = jnp.where(lane < HALO + SUB, roll(f_st[...], -TG), 0.0)
    l = jnp.where(lane < HALO + SUB, roll(l_st[...], -TG), 0.0)
    for at in range(0, TG, SUB):
        tiles = range(at, at + SUB)
        ests = []
        for i in tiles:
            kind = kind_ref[s * TG + i]
            taken = sec[kind, :, i * BLK : (i + 2) * BLK]
            ests.append(jnp.dot(taken, t_ref[i], preferred_element_type=jnp.float32))
        sides = []
        for i in tiles:
            cols = slice(i * BLK, (i + 1) * BLK)
            misfit = mask_ref[:, cols].astype(jnp.float32) * (ests[i - at] - bg_ref[:, cols])
            sides.append(jnp.concatenate(split_hi_lo(misfit), axis=0))
        solved = []
        for i in tiles:
            pair = jnp.concatenate(split_hi_lo(inv_ref[i]), axis=0)
            solved.append(
                lax.dot_general(sides[i - at], pair, NT, preferred_element_type=jnp.float32)
            )
        for i in tiles:
            u = solved[i - at]
            u = u[:32, :BLK] + (u[32:, :BLK] + u[:32, BLK:])
            u_st[SUB + i] = u
            here = lane == HALO + SUB + i
            f = jnp.where(here, u[:, :1], f)
            l = jnp.where(here, u[:, BLK - 1 :], l)
    f_st[...] = f
    l_st[...] = l

    af, cf, al, cl = [coef_ref[r, pl.ds(s, 1), :] for r in range(4)]

    def sweep(f, l):
        west, east = roll(l, 1), roll(f, -1)
        return f_st[...] + af * west + cf * east, l_st[...] + al * west + cl * east

    f2, l2 = sweep(*sweep(f, l))

    def finish(q):
        low = HALO + q * SUB
        ends = jnp.where(lane < SUB, roll(l2, 1 - low), roll(f2, SUB - 1 - low))
        ends = ends[:, : 2 * SUB].astype(jnp.bfloat16)
        sub = s * (TG // SUB) - 1 + q
        fix = jnp.dot(ends, corr_ref[sub], preferred_element_type=jnp.float32)
        spot = step * (TG // SUB) + q - (0 if carried else 1)
        outs = []
        for i in range(SUB):
            cols = slice(i * BLK, (i + 1) * BLK)
            outs.append((u_st[q * SUB + i] + fix[:, cols]).astype(jnp.bfloat16))
        value = jnp.concatenate(outs, axis=1)
        out_ref[:, pl.ds(pl.multiple_of(spot * SW, SW), SW)] = value
        tips = jnp.dot(yw_ref[...], value, preferred_element_type=jnp.float32)
        tips = tips[0:8] + tips[8:16]
        for k in range(2):
            lines = [tips[k : k + 1, i * BLK : (i + 1) * BLK] for i in range(SUB)]
            place = pl.ds(pl.multiple_of(spot * SUB, SUB), SUB)
            part_ref[k, place, :] = jnp.concatenate(lines, axis=0)

    if carried:
        finish(0)
    else:
        pl.when(step > 0)(lambda: finish(0))
    for q in range(1, TG // SUB):
        finish(q)
    pl.when(s == groups - 1)(lambda: finish(TG // SUB))

    @pl.when(step == pl.num_programs(0) - 1)
    def _():
        u_out[...] = u_st[TG:]
        f_out[...] = f_st[...]
        l_out[...] = l_st[...]


def run_rows(first, stop, groups, state, kinds, own, got, w, tables, mask, bg, inv, coefs, corr, yw):
    carried = state is not None
    steps = stop - first
    width = steps * GW - (0 if carried else SW) + (SW if stop == groups else 0)
    near, far, away = got
    full = lambda *shape: pl.BlockSpec(shape, lambda l, *_: (0,) * len(shape))
    wide = lambda off: pl.BlockSpec((32, GW), lambda l, *_: (0, l + off))
    edge = lambda off: pl.BlockSpec((32, BLK), lambda l, *_: (0, (l + off + 1) * TG))
    cube = lambda *shape: pl.BlockSpec((TG, *shape), lambda l, *_: (l + first, 0, 0))
    in_specs = [wide(first), wide(first), wide(0), wide(0)]
    in_specs += [edge(first), edge(first), edge(0), edge(0)]
    in_specs += [
        full(64, BLK),
        cube(2 * BLK, BLK),
        wide(first),
        wide(first),
        cube(BLK, BLK),
        full(*coefs.shape),
        full(*corr.shape),
        full(16, 32),
    ]
    keep = [
        jax.ShapeDtypeStruct((SUB, 32, BLK), jnp.float32),
        jax.ShapeDtypeStruct((32, BLK), jnp.float32),
        jax.ShapeDtypeStruct((32, BLK), jnp.float32),
    ]
    operands = [kinds, own, near, far, away, own, near, far, away, w, tables, mask, bg, inv]
    operands += [coefs, corr, yw]
    if carried:
        in_specs += [full(*k.shape) for k in keep]
        operands += list(state)
    grid_spec = pltpu.PrefetchScalarGridSpec(
        num_scalar_prefetch=1,
        grid=(steps,),
        in_specs=in_specs,
        out_specs=[full(32, width), full(2, width // BLK, BLK), *[full(*k.shape) for k in keep]],
        scratch_shapes=[
            pltpu.VMEM((2, 32, GW + BLK), jnp.bfloat16),
            pltpu.VMEM((SUB + TG, 32, BLK), jnp.float32),
            pltpu.VMEM((32, BLK), jnp.float32),
            pltpu.VMEM((32, BLK), jnp.float32),
        ],
    )
    outs = pl.pallas_call(
        functools.partial(rows_kernel, first, groups, carried),
        grid_spec=grid_spec,
        out_shape=[
            jax.ShapeDtypeStruct((32, width), jnp.bfloat16),
            jax.ShapeDtypeStruct((2, width // BLK, BLK), jnp.float32),
            *keep,
        ],
        compiler_params=pltpu.CompilerParams(vmem_limit_bytes=VMEM_LIMIT),
    )(*operands)
    return outs[0], outs[1], tuple(outs[2:])


def ends_kernel(blocks, block_ref, corner_ref, own, other, below, above, distant, out):
    block = block_ref[0]
    pair = block // 2
    before = jnp.where(pair > 0, below[...], 0.0)
    after = jnp.where(pair < blocks // 2 - 1, above[...], 0.0)
    inside = jnp.where(lax.rem(block, 2) == 1, pair < blocks // 2 - 2, pair > 1)
    beyond = jnp.where(inside, distant[...], 0.0)
    second = lax.rem(block, 2) == 1
    pick = lambda even, odd: jnp.where(second, odd, even)
    coef = lambda r, k: corner_ref[r, block + HALO + k]
    f = {0: own[0], -1: pick(before[1], other[0]), 1: pick(other[0], after[0])}
    l = {0: own[1], -1: pick(before[2], other[1]), 1: pick(other[1], after[1])}
    l[-2], l[-3] = pick(before[0], before[2]), pick(beyond, before[0])
    f[2], f[3] = pick(after[0], after[2]), pick(after[2], beyond)
    last = lambda k, west, east: l[k] + coef(2, k) * west + coef(3, k) * east
    head = lambda k, west, east: f[k] + coef(0, k) * west + coef(1, k) * east
    out[0] = last(-1, last(-2, l[-3], f[-1]), head(0, l[-1], f[1]))
    out[1] = head(1, last(0, l[-1], f[1]), head(2, l[1], f[3]))


def run_ends(blocks, block, corner, own, *others):
    smem = pl.BlockSpec(memory_space=pltpu.SMEM)
    vmem = pl.BlockSpec(memory_space=pltpu.VMEM)
    return pl.pallas_call(
        functools.partial(ends_kernel, blocks),
        in_specs=[smem, smem] + [vmem] * 5,
        out_specs=vmem,
        out_shape=jax.ShapeDtypeStruct(own.shape, own.dtype),
        compiler_params=pltpu.CompilerParams(vmem_limit_bytes=VMEM_LIMIT),
    )(block.reshape(1), corner, own, *others)


def columns_kernel(start, w_ref, ends_ref, e0, e1, e2, e3, n0, n1, *rest):
    out_ref, held, sems = rest[-3:]
    south, north = ends_ref[:, 0:1], ends_ref[:, 1:2]
    copies = []
    for at in range(0, held.shape[1], SW):
        cols = slice(at, at + SW)
        rows = jnp.concatenate([e[:, cols] for e in (e0, e1, e2, e3)], axis=0)
        both = jnp.dot(w_ref[...], rows, preferred_element_type=jnp.float32)
        value = both[:32] + both[32:]
        for i in range(SUB):
            line = (start + at) // BLK + i
            row = [n0[k, line : line + 1, :] + n1[k, line : line + 1, :] for k in range(2)]
            here = slice(i * BLK, (i + 1) * BLK)
            held[:, at + i * BLK : at + (i + 1) * BLK] = (
                value[:, here] + south * row[0] + north * row[1]
            )
        copy = pltpu.make_async_copy(
            held.at[:, cols], out_ref.at[:, start + at : start + at + SW], sems.at[at // SW]
        )
        copy.start()
        copies.append(copy)
    for copy in copies:
        copy.wait()


def run_columns(start, total, w, ends, pieces, near, far, so_far):
    width = pieces[0].shape[1]
    vmem = pl.BlockSpec(memory_space=pltpu.VMEM)
    operands = [w, ends, *pieces, near, far]
    in_specs = [vmem] * 8
    aliases = {}
    if so_far is not None:
        operands.append(so_far)
        in_specs.append(pl.BlockSpec(memory_space=pl.ANY))
        aliases = {8: 0}
    return pl.pallas_call(
        functools.partial(columns_kernel, start),
        in_specs=in_specs,
        out_specs=pl.BlockSpec(memory_space=pl.ANY),
        out_shape=jax.ShapeDtypeStruct((32, total), jnp.float32),
        scratch_shapes=[
            pltpu.VMEM((32, width), jnp.float32),
            pltpu.SemaphoreType.DMA((width // SW,)),
        ],
        input_output_aliases=aliases,
        compiler_params=pltpu.CompilerParams(vmem_limit_bytes=VMEM_LIMIT),
    )(*operands)


def body(
    panels,
    void_mask,
    background,
    row_offset,
    row_frac,
    tile_kind,
    tile_shift,
    tile_frac,
    inverse_x,
    couple_x,
    inverse_y,
    couple_y,
):
    rows = row_offset.shape[0]
    width = background.shape[1]
    groups = width // GW
    n_wide = lax.axis_size("wide")
    mine = lax.axis_index("band")
    block = lax.axis_index("wide")
    across = [(d, d ^ 2) for d in range(4)]
    sibling = [(d, d ^ 1) for d in range(4)]
    swap = lambda value, pairs: lax.ppermute(value, "band", pairs)

    near = swap(panels, sibling)
    bounds = [(SPLITS[i], SPLITS[i + 1]) for i in range(len(SPLITS) - 1)]
    gathered = []
    for first, stop in bounds:
        far = swap(panels[:, first * GW : stop * GW + BLK], across)
        gathered.append(far)

    order = ((jnp.arange(4, dtype=jnp.int32) ^ mine)[:, None] * rows + jnp.arange(rows)[None, :]).reshape(-1)
    w = jnp.concatenate(
        [
            row_matrix(row_offset, row_frac, order, linear_terms),
            row_matrix(row_offset, row_frac, order, cubic_terms),
        ],
        axis=0,
    )
    kinds = (tile_kind == 1).astype(jnp.int32)
    tables, corr, a_x, b_x = run_tables(
        tile_shift, tap_weights(tile_kind, tile_frac), couple_x, inverse_x
    )
    coefs = jnp.stack([a_x[:, 0], b_x[:, 0], a_x[:, -1], b_x[:, -1]])
    coefs = jnp.pad(coefs, ((0, 0), (SUB + HALO, TG - SUB - HALO))).reshape(4, groups + 1, TG)
    coefs = jnp.concatenate([coefs[:, :-1], coefs[:, 1:]], axis=2)
    coefs = jnp.pad(coefs, ((0, 0), (0, 0), (0, BLK - 2 * TG)))

    tips = inverse_y[:, :: BLK - 1, :: BLK - 1] * couple_y.T[:, None, :]
    corner = jnp.stack([tips[:, 0, 0], tips[:, 0, 1], tips[:, 1, 0], tips[:, 1, 1]])
    corner = jnp.pad(corner, ((0, 0), (HALO, HALO)))
    own_inv = lax.dynamic_index_in_dim(inverse_y, block, 0, keepdims=False)
    at = mine * rows
    own_rows = lax.dynamic_slice_in_dim(own_inv, at, rows, 0)
    shuffled = jnp.concatenate(
        [lax.dynamic_slice_in_dim(own_rows, (q ^ mine) * rows, rows, 1) for q in range(4)], axis=1
    )
    w_y = jnp.concatenate(table_hi_lo(shuffled), axis=0)
    ends_y = jnp.stack(
        [
            couple_y[0, block] * own_rows[:, 0],
            couple_y[1, block] * own_rows[:, -1],
        ],
        axis=1,
    )
    end_rows = lax.dynamic_slice_in_dim(jnp.stack([own_inv[0], own_inv[-1]]), at, rows, 1)
    end_hi, end_lo = table_hi_lo(end_rows)
    gap = jnp.zeros((6, rows), jnp.bfloat16)
    yw = jnp.concatenate([end_hi, gap, end_lo, gap], axis=0)

    state = None
    sent = []
    parts = []
    for (first, stop), far in zip(bounds, gathered):
        if state is not None:
            far, state = lax.optimization_barrier((far, state))
        got = (near, far, swap(far, sibling))
        east_west, part, state = run_rows(
            first, stop, groups, state, kinds, panels, got, w, tables,
            void_mask, background, inverse_x, coefs, corr, yw,
        )
        far = swap(east_west, across)
        sent.append([east_west, swap(east_west, sibling), far])
        parts.append(part)
    part = jnp.concatenate(parts, axis=1) if len(parts) > 1 else parts[0]
    if len(sent) > 1:
        part, sent[0][2] = lax.optimization_barrier((part, sent[0][2]))

    every = [(d, k) for d in range(4) for k in range(n_wide)]
    at = lambda d, k: d * n_wide + k
    fetch = lambda db, dw: lax.ppermute(
        part, ("band", "wide"), [(at(d ^ db, k ^ dw), at(d, k)) for d, k in every]
    )
    second = block % 2
    own = part + fetch(2, 0)
    other = fetch(0, 1) + fetch(2, 1)
    even = jnp.where(second == 0, own, other)
    odd = jnp.where(second == 0, other, own)
    shifted = lambda value, k: lax.ppermute(
        value, "wide", [(i, (i + 2 * k) % n_wide) for i in range(n_wide)]
    )
    before = shifted(jnp.stack([even[1], odd[0], odd[1]]), 1)
    after = shifted(jnp.stack([even[0], even[1], odd[0]]), -1)
    beyond = lax.ppermute(
        jnp.where(second == 0, odd[1], even[0]),
        "wide",
        [(i, (i + 4 * (1 - 2 * (i % 2))) % n_wide) for i in range(n_wide)],
    )
    forced = run_ends(n_wide, block, corner, own, other, before, after, beyond)
    rest = swap(forced, sibling)
    sent[-1][2], rest = lax.optimization_barrier((sent[-1][2], rest))

    result = None
    position = 0
    for pieces in sent:
        pieces = (*pieces, swap(pieces[2], sibling))
        result = run_columns(position, width, w_y, ends_y, pieces, forced, rest, result)
        position += pieces[0].shape[1]
    return result


def solution(mesh):
    placed = (
        P(("wide", "band"), None),
        P(("wide", "band"), None),
        P(("wide", "band"), None),
        P(("wide", "band")),
        P(("wide", "band")),
        P(),
        P(),
        P(),
        P(),
        P(),
        P(),
        P(),
    )
    return jax.shard_map(
        body, mesh=mesh, in_specs=placed, out_specs=P(("wide", "band"), None), check_vma=False
    )
```

```python
import functools

import jax
import jax.numpy as jnp
from jax import lax
from jax.experimental import pallas as pl
from jax.experimental.pallas import tpu as pltpu
from jax.sharding import PartitionSpec as P

BLK = 128
TG = 32
GW = TG * BLK
SUB = 8
SW = SUB * BLK
HALO = 3
SPLITS = (0, 2, 4)
VMEM_LIMIT = 48 * 1024 * 1024


def cubic_terms(frac):
    f2 = frac * frac
    f3 = f2 * frac
    return [
        -0.5 * f3 + f2 - 0.5 * frac,
        1.5 * f3 - 2.5 * f2 + 1.0,
        -1.5 * f3 + 2.0 * f2 + 0.5 * frac,
        0.5 * f3 - 0.5 * f2,
    ]


def linear_terms(frac):
    zeros = jnp.zeros_like(frac)
    return [zeros, 1.0 - frac, frac, zeros]


def row_matrix(offsets, fracs, columns, terms):
    total = jnp.zeros((offsets.shape[0], columns.shape[0]), jnp.float32)
    for index, weight in enumerate(terms(fracs)):
        hit = (columns[None, :] == offsets[:, None] + index).astype(jnp.float32)
        total = total + weight[:, None] * hit
    return total.astype(jnp.bfloat16)


def tap_weights(kind, frac):
    taps = [
        jnp.where(kind == 1, wc, wl)
        for wc, wl in zip(cubic_terms(frac), linear_terms(frac))
    ]
    return lax.reduce_precision(jnp.stack(taps), 8, 7)


NT = (((1,), (1,)), ((), ()))


def tables_kernel(here_ref, shift_ref, tap_ref, inv_ref, couple_ref, *outs):
    t_ref, w_ref, ends_ref, yw_ref, corner_ref = outs
    step = pl.program_id(0)
    block, mine = here_ref[0], here_ref[1]
    shape = (2 * BLK, BLK)
    delta = lax.broadcasted_iota(jnp.int32, shape, 0) - lax.broadcasted_iota(jnp.int32, shape, 1)
    for i in range(TG):
        tile = step * TG + i
        tap = delta - shift_ref[tile]
        total = jnp.zeros(shape, jnp.float32)
        for k in range(4):
            total = jnp.where(tap == k, tap_ref[k, tile], total)
        t_ref[i] = total.astype(jnp.bfloat16)

    @pl.when(step == 0)
    def _():
        lane = lax.broadcasted_iota(jnp.int32, (32, BLK), 1)
        odd, high = lax.rem(mine, 2) == 1, mine > 1
        own = inv_ref[block, pl.ds(pl.multiple_of(mine * 32, 32), 32), :]
        swapped = jnp.where(lax.rem(lane // 32, 2) == 0, pltpu.roll(own, 96, 1), pltpu.roll(own, 32, 1))
        turned = jnp.where(odd, swapped, own)
        turned = jnp.where(high, pltpu.roll(turned, 64, 1), turned)
        w_ref[...] = jnp.concatenate(split_hi_lo(turned), axis=0)
        pair = jnp.where(lane == 0, own[:, :1], own[:, BLK - 1 :])
        couple = couple_ref[pl.ds(block, 1), :]
        ends_ref[...] = pair * jnp.where(lane == 0, couple[:, :1], couple[:, 1:2])
        row = lax.broadcasted_iota(jnp.int32, (8, BLK), 0)
        tips = jnp.where(row == 0, inv_ref[block, 0:1, :], inv_ref[block, BLK - 1 :, :])
        tips = jnp.where(row < 2, tips, 0.0)
        tips = jnp.where(odd, pltpu.roll(tips, 96, 1), tips)
        tips = jnp.where(high, pltpu.roll(tips, 64, 1), tips)
        yw_ref[...] = jnp.concatenate(split_hi_lo(tips), axis=0)[:, :32]
        top, bottom = inv_ref[:, 0, :], inv_ref[:, BLK - 1, :]
        west, east = couple_ref[:, 0:1], couple_ref[:, 1:2]
        values = (top[:, :1] * west, top[:, BLK - 1 :] * east, bottom[:, :1] * west, bottom[:, BLK - 1 :] * east)
        total = jnp.zeros((32, BLK), jnp.float32)
        for k, value in enumerate(values):
            total = jnp.where(lane == k, value, total)
        corner_ref[...] = total


def run_tables(here, shift, taps, inverse_y, couple_y):
    tiles = shift.shape[0]
    full = lambda *shape: pl.BlockSpec(shape, lambda l, *_: (0,) * len(shape))
    return pl.pallas_call(
        tables_kernel,
        grid_spec=pltpu.PrefetchScalarGridSpec(
            num_scalar_prefetch=3,
            grid=(tiles // TG,),
            in_specs=[full(*inverse_y.shape), full(*couple_y.shape)],
            out_specs=[
                pl.BlockSpec((TG, 2 * BLK, BLK), lambda l, *_: (l, 0, 0)),
                full(64, BLK),
                full(32, BLK),
                full(16, 32),
                full(32, BLK),
            ],
        ),
        out_shape=[
            jax.ShapeDtypeStruct((tiles, 2 * BLK, BLK), jnp.bfloat16),
            jax.ShapeDtypeStruct((64, BLK), jnp.bfloat16),
            jax.ShapeDtypeStruct((32, BLK), jnp.float32),
            jax.ShapeDtypeStruct((16, 32), jnp.bfloat16),
            jax.ShapeDtypeStruct((32, BLK), jnp.float32),
        ],
        compiler_params=pltpu.CompilerParams(vmem_limit_bytes=VMEM_LIMIT),
    )(here, shift, taps, inverse_y, couple_y)


def split_hi_lo(value):
    hi = value.astype(jnp.bfloat16)
    lo = (value - hi.astype(jnp.float32)).astype(jnp.bfloat16)
    return hi, lo


def rows_kernel(first, groups, carried, *refs):
    kind_ref, couple_ref, p0, p1, p2, p3, q0, q1, q2, q3, w_ref, t_ref = refs[:12]
    mask_ref, bg_ref, inv_ref, lanes_ref, yw_ref = refs[12:17]
    refs = refs[17:]
    if carried:
        u_in, f_in, l_in, c_in = refs[:4]
        refs = refs[4:]
    out_ref, part_ref, u_out, f_out, l_out, c_out, sec, u_st, f_st, l_st, c_st = refs
    step = pl.program_id(0)
    s = step + first
    tall = (40, BLK)
    tall_lane = lax.broadcasted_iota(jnp.int32, tall, 1)
    lane = lax.broadcasted_iota(jnp.int32, (32, BLK), 1)
    row = lax.broadcasted_iota(jnp.int32, (2 * SUB, BLK), 0)
    units = row * (BLK - 1) == lax.broadcasted_iota(jnp.int32, (2 * SUB, BLK), 1)
    units = units.astype(jnp.float32).astype(jnp.bfloat16)
    roll = lambda value, by: pltpu.roll(value, by % BLK, 1)

    @pl.when(step == 0)
    def _():
        if carried:
            u_st[TG:] = u_in[...]
            f_st[...] = f_in[...]
            l_st[...] = l_in[...]
            c_st[TG // SUB] = c_in[...]
        else:
            c_st[...] = jnp.zeros_like(c_st)
            u_st[...] = jnp.zeros_like(u_st)
            f_st[...] = jnp.zeros_like(f_st)
            l_st[...] = jnp.zeros_like(l_st)

    u_st[:SUB] = u_st[TG:]
    c_st[0] = c_st[TG // SUB]
    rows = jnp.concatenate([p0[...], p1[...], p2[...], p3[...]], axis=0)
    edge = jnp.concatenate([q0[...], q1[...], q2[...], q3[...]], axis=0)
    w = w_ref[...]
    both = jnp.dot(w, rows, preferred_element_type=jnp.float32).astype(jnp.bfloat16)
    tail = jnp.dot(w, edge, preferred_element_type=jnp.float32).astype(jnp.bfloat16)
    for k in range(2):
        sec[k, :, :GW] = both[k * 32 : (k + 1) * 32]
        sec[k, :, GW:] = tail[k * 32 : (k + 1) * 32]
    f = jnp.where(tall_lane < HALO + SUB, roll(f_st[...], -TG), 0.0)
    l = jnp.where(tall_lane < HALO + SUB, roll(l_st[...], -TG), 0.0)
    for at in range(0, TG, SUB):
        tiles = range(at, at + SUB)
        ests = []
        for i in tiles:
            kind = kind_ref[s * TG + i]
            taken = sec[kind, :, i * BLK : (i + 2) * BLK]
            ests.append(jnp.dot(taken, t_ref[i], preferred_element_type=jnp.float32))
        sides = []
        for i in tiles:
            cols = slice(i * BLK, (i + 1) * BLK)
            misfit = mask_ref[:, cols].astype(jnp.float32) * (ests[i - at] - bg_ref[:, cols])
            sides.append(jnp.concatenate([*split_hi_lo(misfit), units], axis=0))
        solved = []
        for i in tiles:
            pair = jnp.concatenate(split_hi_lo(inv_ref[i]), axis=0)
            solved.append(
                lax.dot_general(sides[i - at], pair, NT, preferred_element_type=jnp.float32)
            )
        for i in tiles:
            u = solved[i - at]
            tips = u[64:72, :BLK] + u[64:72, BLK:]
            u = u[:32, :BLK] + (u[32:64, :BLK] + u[:32, BLK:])
            u_st[SUB + i] = u
            tile = s * TG + i
            west, east = couple_ref[0, tile] * tips[0:1], couple_ref[1, tile] * tips[1:2]
            both = jnp.where(row == i - at, west, jnp.where(row == SUB + i - at, east, 0.0))
            spot = (i - at) * BLK
            c_st[at // SUB + 1, :, spot : spot + BLK] = both.astype(jnp.bfloat16)
            u = jnp.concatenate([u, tips], axis=0)
            here = tall_lane == HALO + SUB + i
            f = jnp.where(here, u[:, :1], f)
            l = jnp.where(here, u[:, BLK - 1 :], l)
    f_st[...] = f
    l_st[...] = l

    west, east = lanes_ref[0, pl.ds(s, 1), :], lanes_ref[1, pl.ds(s, 1), :]
    af, cf, al, cl = f[32:33] * west, f[33:34] * east, l[32:33] * west, l[33:34] * east
    f0, l0 = f[:32], l[:32]

    def sweep(f, l):
        west, east = roll(l, 1), roll(f, -1)
        return f0 + af * west + cf * east, l0 + al * west + cl * east

    f2, l2 = sweep(*sweep(f0, l0))

    def finish(q):
        low = HALO + q * SUB
        ends = jnp.where(lane < SUB, roll(l2, 1 - low), roll(f2, SUB - 1 - low))
        ends = ends[:, : 2 * SUB].astype(jnp.bfloat16)
        fix = jnp.dot(ends, c_st[q], preferred_element_type=jnp.float32)
        spot = step * (TG // SUB) + q - (0 if carried else 1)
        outs = []
        for i in range(SUB):
            cols = slice(i * BLK, (i + 1) * BLK)
            outs.append((u_st[q * SUB + i] + fix[:, cols]).astype(jnp.bfloat16))
        value = jnp.concatenate(outs, axis=1)
        out_ref[:, pl.ds(pl.multiple_of(spot * SW, SW), SW)] = value
        tips = jnp.dot(yw_ref[...], value, preferred_element_type=jnp.float32)
        tips = tips[0:8] + tips[8:16]
        for k in range(2):
            lines = [tips[k : k + 1, i * BLK : (i + 1) * BLK] for i in range(SUB)]
            place = pl.ds(pl.multiple_of(spot * SUB, SUB), SUB)
            part_ref[k, place, :] = jnp.concatenate(lines, axis=0)

    if carried:
        finish(0)
    else:
        pl.when(step > 0)(lambda: finish(0))
    for q in range(1, TG // SUB):
        finish(q)
    pl.when(s == groups - 1)(lambda: finish(TG // SUB))

    @pl.when(step == pl.num_programs(0) - 1)
    def _():
        u_out[...] = u_st[TG:]
        f_out[...] = f_st[...]
        l_out[...] = l_st[...]
        c_out[...] = c_st[TG // SUB]


def run_rows(first, stop, groups, state, kinds, couple, own, got, w, tables, mask, bg, inv, lanes, yw):
    carried = state is not None
    steps = stop - first
    width = steps * GW - (0 if carried else SW) + (SW if stop == groups else 0)
    near, far, away = got
    full = lambda *shape: pl.BlockSpec(shape, lambda l, *_: (0,) * len(shape))
    wide = lambda off: pl.BlockSpec((32, GW), lambda l, *_: (0, l + off))
    edge = lambda off: pl.BlockSpec((32, BLK), lambda l, *_: (0, (l + off + 1) * TG))
    cube = lambda *shape: pl.BlockSpec((TG, *shape), lambda l, *_: (l + first, 0, 0))
    in_specs = [wide(first), wide(first), wide(0), wide(0)]
    in_specs += [edge(first), edge(first), edge(0), edge(0)]
    in_specs += [
        full(64, BLK),
        cube(2 * BLK, BLK),
        wide(first),
        wide(first),
        cube(BLK, BLK),
        full(*lanes.shape),
        full(16, 32),
    ]
    keep = [
        jax.ShapeDtypeStruct((SUB, 32, BLK), jnp.float32),
        jax.ShapeDtypeStruct((40, BLK), jnp.float32),
        jax.ShapeDtypeStruct((40, BLK), jnp.float32),
        jax.ShapeDtypeStruct((2 * SUB, SW), jnp.bfloat16),
    ]
    operands = [kinds, couple, own, near, far, away, own, near, far, away, w, tables, mask, bg]
    operands += [inv, lanes, yw]
    if carried:
        in_specs += [full(*k.shape) for k in keep]
        operands += list(state)
    grid_spec = pltpu.PrefetchScalarGridSpec(
        num_scalar_prefetch=2,
        grid=(steps,),
        in_specs=in_specs,
        out_specs=[full(32, width), full(2, width // BLK, BLK), *[full(*k.shape) for k in keep]],
        scratch_shapes=[
            pltpu.VMEM((2, 32, GW + BLK), jnp.bfloat16),
            pltpu.VMEM((SUB + TG, 32, BLK), jnp.float32),
            pltpu.VMEM((40, BLK), jnp.float32),
            pltpu.VMEM((40, BLK), jnp.float32),
            pltpu.VMEM((TG // SUB + 1, 2 * SUB, SW), jnp.bfloat16),
        ],
    )
    outs = pl.pallas_call(
        functools.partial(rows_kernel, first, groups, carried),
        grid_spec=grid_spec,
        out_shape=[
            jax.ShapeDtypeStruct((32, width), jnp.bfloat16),
            jax.ShapeDtypeStruct((2, width // BLK, BLK), jnp.float32),
            *keep,
        ],
        compiler_params=pltpu.CompilerParams(vmem_limit_bytes=VMEM_LIMIT),
    )(*operands)
    return outs[0], outs[1], tuple(outs[2:])


def ends_kernel(blocks, block_ref, corner_ref, own, other, below, above, distant, out):
    block = block_ref[0]
    pair = block // 2
    value = lambda ref: ref[...].astype(jnp.float32)
    before = jnp.where(pair > 0, value(below), 0.0)
    after = jnp.where(pair < blocks // 2 - 1, value(above), 0.0)
    inside = jnp.where(lax.rem(block, 2) == 1, pair < blocks // 2 - 2, pair > 1)
    beyond = jnp.where(inside, value(distant), 0.0)
    second = lax.rem(block, 2) == 1
    pick = lambda even, odd: jnp.where(second, odd, even)

    def coef(r, k):
        at = block + k
        return jnp.where((at >= 0) & (at < blocks), corner_ref[jnp.clip(at, 0, blocks - 1), r], 0.0)

    f = {0: own[0], -1: pick(before[1], other[0]), 1: pick(other[0], after[0])}
    l = {0: own[1], -1: pick(before[2], other[1]), 1: pick(other[1], after[1])}
    l[-2], l[-3] = pick(before[0], before[2]), pick(beyond, before[0])
    f[2], f[3] = pick(after[0], after[2]), pick(after[2], beyond)
    last = lambda k, west, east: l[k] + coef(2, k) * west + coef(3, k) * east
    head = lambda k, west, east: f[k] + coef(0, k) * west + coef(1, k) * east
    out[0] = last(-1, last(-2, l[-3], f[-1]), head(0, l[-1], f[1]))
    out[1] = head(1, last(0, l[-1], f[1]), head(2, l[1], f[3]))


def run_ends(blocks, block, corner, own, *others):
    smem = pl.BlockSpec(memory_space=pltpu.SMEM)
    vmem = pl.BlockSpec(memory_space=pltpu.VMEM)
    return pl.pallas_call(
        functools.partial(ends_kernel, blocks),
        in_specs=[smem, smem] + [vmem] * 5,
        out_specs=vmem,
        out_shape=jax.ShapeDtypeStruct(own.shape, own.dtype),
        compiler_params=pltpu.CompilerParams(vmem_limit_bytes=VMEM_LIMIT),
    )(block.reshape(1), corner, own, *others)


def columns_kernel(start, w_ref, ends_ref, e0, e1, e2, e3, n0, n1, *rest):
    out_ref, held, sems = rest[-3:]
    south, north = ends_ref[:, 0:1], ends_ref[:, 1:2]
    copies = []
    for at in range(0, held.shape[1], SW):
        cols = slice(at, at + SW)
        rows = jnp.concatenate([e[:, cols] for e in (e0, e1, e2, e3)], axis=0)
        both = jnp.dot(w_ref[...], rows, preferred_element_type=jnp.float32)
        value = both[:32] + both[32:]
        for i in range(SUB):
            line = (start + at) // BLK + i
            row = [n0[k, line : line + 1, :] + n1[k, line : line + 1, :] for k in range(2)]
            here = slice(i * BLK, (i + 1) * BLK)
            held[:, at + i * BLK : at + (i + 1) * BLK] = (
                value[:, here] + south * row[0] + north * row[1]
            )
        copy = pltpu.make_async_copy(
            held.at[:, cols], out_ref.at[:, start + at : start + at + SW], sems.at[at // SW]
        )
        copy.start()
        copies.append(copy)
    for copy in copies:
        copy.wait()


def run_columns(start, total, w, ends, pieces, near, far, so_far):
    width = pieces[0].shape[1]
    vmem = pl.BlockSpec(memory_space=pltpu.VMEM)
    operands = [w, ends, *pieces, near, far]
    in_specs = [vmem] * 8
    aliases = {}
    if so_far is not None:
        operands.append(so_far)
        in_specs.append(pl.BlockSpec(memory_space=pl.ANY))
        aliases = {8: 0}
    return pl.pallas_call(
        functools.partial(columns_kernel, start),
        in_specs=in_specs,
        out_specs=pl.BlockSpec(memory_space=pl.ANY),
        out_shape=jax.ShapeDtypeStruct((32, total), jnp.float32),
        scratch_shapes=[
            pltpu.VMEM((32, width), jnp.float32),
            pltpu.SemaphoreType.DMA((width // SW,)),
        ],
        input_output_aliases=aliases,
        compiler_params=pltpu.CompilerParams(vmem_limit_bytes=VMEM_LIMIT),
    )(*operands)


def body(
    panels,
    void_mask,
    background,
    row_offset,
    row_frac,
    tile_kind,
    tile_shift,
    tile_frac,
    inverse_x,
    couple_x,
    inverse_y,
    couple_y,
):
    rows = row_offset.shape[0]
    width = background.shape[1]
    groups = width // GW
    n_wide = lax.axis_size("wide")
    mine = lax.axis_index("band")
    block = lax.axis_index("wide")
    across = [(d, d ^ 2) for d in range(4)]
    sibling = [(d, d ^ 1) for d in range(4)]
    swap = lambda value, pairs: lax.ppermute(value, "band", pairs)

    near = swap(panels, sibling)
    bounds = [(SPLITS[i], SPLITS[i + 1]) for i in range(len(SPLITS) - 1)]
    gathered = []
    for first, stop in bounds:
        far = swap(panels[:, first * GW : stop * GW + BLK], across)
        gathered.append(far)

    order = ((jnp.arange(4, dtype=jnp.int32) ^ mine)[:, None] * rows + jnp.arange(rows)[None, :]).reshape(-1)
    w = jnp.concatenate(
        [
            row_matrix(row_offset, row_frac, order, linear_terms),
            row_matrix(row_offset, row_frac, order, cubic_terms),
        ],
        axis=0,
    )
    kinds = (tile_kind == 1).astype(jnp.int32)
    tables, w_y, ends_y, yw, corner = run_tables(
        jnp.stack([block, mine]), tile_shift, tap_weights(tile_kind, tile_frac), inverse_y, couple_y.T
    )
    lanes = jnp.pad(couple_x, ((0, 0), (SUB + HALO, TG - SUB - HALO))).reshape(2, groups + 1, TG)
    lanes = jnp.concatenate([lanes[:, :-1], lanes[:, 1:]], axis=2)
    lanes = jnp.pad(lanes, ((0, 0), (0, 0), (0, BLK - 2 * TG)))

    state = None
    sent = []
    parts = []
    for (first, stop), far in zip(bounds, gathered):
        if state is not None:
            far, state = lax.optimization_barrier((far, state))
        got = (near, far, swap(far, sibling))
        east_west, part, state = run_rows(
            first, stop, groups, state, kinds, couple_x, panels, got, w, tables,
            void_mask, background, inverse_x, lanes, yw,
        )
        far = swap(east_west, across)
        sent.append([east_west, swap(east_west, sibling), far])
        parts.append(part)
    together = lax.optimization_barrier
    part = jnp.concatenate(parts, axis=1) if len(parts) > 1 else parts[0]
    for pieces in sent[:-1]:
        part, pieces[1], pieces[2] = together((part, pieces[1], pieces[2]))

    every = [(d, k) for d in range(4) for k in range(n_wide)]
    at = lambda d, k: d * n_wide + k
    half = part.astype(jnp.bfloat16)
    fetch = lambda db, dw: lax.ppermute(
        half, ("band", "wide"), [(at(d ^ db, k ^ dw), at(d, k)) for d, k in every]
    ).astype(jnp.float32)
    second = block % 2
    own = part + fetch(2, 0)
    other = fetch(0, 1) + fetch(2, 1)
    for pieces in sent[:-1]:
        pieces.append(swap(pieces[2], sibling))
        own, pieces[3] = together((own, pieces[3]))
    even = jnp.where(second == 0, own, other).astype(jnp.bfloat16)
    odd = jnp.where(second == 0, other, own).astype(jnp.bfloat16)
    shifted = lambda value, k: lax.ppermute(
        value, "wide", [(i, (i + 2 * k) % n_wide) for i in range(n_wide)]
    )
    before = shifted(jnp.stack([even[1], odd[0], odd[1]]), 1)
    after = shifted(jnp.stack([even[0], even[1], odd[0]]), -1)
    beyond = lax.ppermute(
        jnp.where(second == 0, odd[1], even[0]),
        "wide",
        [(i, (i + 4 * (1 - 2 * (i % 2))) % n_wide) for i in range(n_wide)],
    )
    before, sent[-1][1] = together((before, sent[-1][1]))
    forced = run_ends(n_wide, block, corner, own, other, before, after, beyond)
    rest = swap(forced, sibling)

    result = None
    position = 0
    for pieces in sent:
        if len(pieces) == 3:
            if result is None:
                pieces[2], rest = together((pieces[2], rest))
            else:
                pieces[2], result = together((pieces[2], result))
            pieces.append(swap(pieces[2], sibling))
        result = run_columns(position, width, w_y, ends_y, pieces, forced, rest, result)
        position += pieces[0].shape[1]
    return result


def solution(mesh):
    placed = (
        P(("wide", "band"), None),
        P(("wide", "band"), None),
        P(("wide", "band"), None),
        P(("wide", "band")),
        P(("wide", "band")),
        P(),
        P(),
        P(),
        P(),
        P(),
        P(),
        P(),
    )
    return jax.shard_map(
        body, mesh=mesh, in_specs=placed, out_specs=P(("wide", "band"), None), check_vma=False
    )
```

```python
import functools

import jax
import jax.numpy as jnp
from jax import lax
from jax.experimental import pallas as pl
from jax.experimental.pallas import tpu as pltpu
from jax.sharding import PartitionSpec as P

BLK = 128
TG = 32
GW = TG * BLK
SUB = 8
SW = SUB * BLK
HALO = 3
SPLITS = (0, 2, 4)
LATE = 1
VMEM_LIMIT = 32 * 1024 * 1024


def cubic_terms(frac):
    f2 = frac * frac
    f3 = f2 * frac
    return [
        -0.5 * f3 + f2 - 0.5 * frac,
        1.5 * f3 - 2.5 * f2 + 1.0,
        -1.5 * f3 + 2.0 * f2 + 0.5 * frac,
        0.5 * f3 - 0.5 * f2,
    ]


def linear_terms(frac):
    zeros = jnp.zeros_like(frac)
    return [zeros, 1.0 - frac, frac, zeros]


def row_matrix(offsets, fracs, columns, terms):
    total = jnp.zeros((offsets.shape[0], columns.shape[0]), jnp.float32)
    for index, weight in enumerate(terms(fracs)):
        hit = (columns[None, :] == offsets[:, None] + index).astype(jnp.float32)
        total = total + weight[:, None] * hit
    return total.astype(jnp.bfloat16)


def tap_weights(kind, frac):
    taps = [
        jnp.where(kind == 1, wc, wl)
        for wc, wl in zip(cubic_terms(frac), linear_terms(frac))
    ]
    return lax.reduce_precision(jnp.stack(taps), 8, 7)


NT = (((1,), (1,)), ((), ()))


def tables_kernel(here_ref, shift_ref, tap_ref, inv_ref, first_ref, last_ref, couple_ref, *outs):
    t_ref, w_ref, ends_ref, yw_ref, corner_ref = outs
    step = pl.program_id(0)
    block, mine = here_ref[0], here_ref[1]
    shape = (2 * BLK, BLK)
    delta = lax.broadcasted_iota(jnp.int32, shape, 0) - lax.broadcasted_iota(jnp.int32, shape, 1)
    for i in range(TG):
        tile = step * TG + i
        tap = delta - shift_ref[tile]
        total = jnp.zeros(shape, jnp.float32)
        for k in range(4):
            total = jnp.where(tap == k, tap_ref[k, tile], total)
        t_ref[i] = total.astype(jnp.bfloat16)

    @pl.when(step == 0)
    def _():
        lane = lax.broadcasted_iota(jnp.int32, (32, BLK), 1)
        odd, high = lax.rem(mine, 2) == 1, mine > 1
        own = inv_ref[0, pl.ds(pl.multiple_of(mine * 32, 32), 32), :]
        swapped = jnp.where(lax.rem(lane // 32, 2) == 0, pltpu.roll(own, 96, 1), pltpu.roll(own, 32, 1))
        turned = jnp.where(odd, swapped, own)
        turned = jnp.where(high, pltpu.roll(turned, 64, 1), turned)
        w_ref[...] = jnp.concatenate(split_hi_lo(turned), axis=0)
        pair = jnp.where(lane == 0, own[:, :1], own[:, BLK - 1 :])
        couple = couple_ref[pl.ds(block, 1), :]
        ends_ref[...] = pair * jnp.where(lane == 0, couple[:, :1], couple[:, 1:2])
        row = lax.broadcasted_iota(jnp.int32, (8, BLK), 0)
        tips = jnp.where(row == 0, inv_ref[0, 0:1, :], inv_ref[0, BLK - 1 :, :])
        tips = jnp.where(row < 2, tips, 0.0)
        tips = jnp.where(odd, pltpu.roll(tips, 96, 1), tips)
        tips = jnp.where(high, pltpu.roll(tips, 64, 1), tips)
        yw_ref[...] = jnp.concatenate(split_hi_lo(tips), axis=0)[:, :32]
        top, bottom = first_ref[:, 0, :], last_ref[:, 7, :]
        west, east = couple_ref[:, 0:1], couple_ref[:, 1:2]
        values = (top[:, :1] * west, top[:, BLK - 1 :] * east, bottom[:, :1] * west, bottom[:, BLK - 1 :] * east)
        total = jnp.zeros((32, BLK), jnp.float32)
        for k, value in enumerate(values):
            total = jnp.where(lane == k, value, total)
        corner_ref[...] = total


def run_tables(here, shift, taps, inverse_y, couple_y):
    tiles = shift.shape[0]
    full = lambda *shape: pl.BlockSpec(shape, lambda l, *_: (0,) * len(shape))
    return pl.pallas_call(
        tables_kernel,
        grid_spec=pltpu.PrefetchScalarGridSpec(
            num_scalar_prefetch=3,
            grid=(tiles // TG,),
            in_specs=[
                pl.BlockSpec((1, BLK, BLK), lambda l, here, *_: (here[0], 0, 0)),
                pl.BlockSpec((inverse_y.shape[0], 8, BLK), lambda l, *_: (0, 0, 0)),
                pl.BlockSpec((inverse_y.shape[0], 8, BLK), lambda l, *_: (0, BLK // 8 - 1, 0)),
                full(*couple_y.shape),
            ],
            out_specs=[
                pl.BlockSpec((TG, 2 * BLK, BLK), lambda l, *_: (l, 0, 0)),
                full(64, BLK),
                full(32, BLK),
                full(16, 32),
                full(32, BLK),
            ],
        ),
        out_shape=[
            jax.ShapeDtypeStruct((tiles, 2 * BLK, BLK), jnp.bfloat16),
            jax.ShapeDtypeStruct((64, BLK), jnp.bfloat16),
            jax.ShapeDtypeStruct((32, BLK), jnp.float32),
            jax.ShapeDtypeStruct((16, 32), jnp.bfloat16),
            jax.ShapeDtypeStruct((32, BLK), jnp.float32),
        ],
        compiler_params=pltpu.CompilerParams(vmem_limit_bytes=VMEM_LIMIT),
    )(here, shift, taps, inverse_y, inverse_y, inverse_y, couple_y)


def split_hi_lo(value):
    hi = value.astype(jnp.bfloat16)
    lo = (value - hi.astype(jnp.float32)).astype(jnp.bfloat16)
    return hi, lo


def rows_kernel(first, groups, carried, *refs):
    kind_ref, couple_ref, p0, p1, p2, p3, q0, q1, q2, q3, w_ref, t_ref = refs[:12]
    mask_ref, bg_ref, inv_ref, lanes_ref, yw_ref = refs[12:17]
    refs = refs[17:]
    if carried:
        u_in, f_in, l_in, c_in = refs[:4]
        refs = refs[4:]
    out_ref, part_ref, u_out, f_out, l_out, c_out, sec, u_st, f_st, l_st, c_st = refs
    step = pl.program_id(0)
    s = step + first
    tall = (40, BLK)
    tall_lane = lax.broadcasted_iota(jnp.int32, tall, 1)
    lane = lax.broadcasted_iota(jnp.int32, (32, BLK), 1)
    row = lax.broadcasted_iota(jnp.int32, (2 * SUB, BLK), 0)
    units = row * (BLK - 1) == lax.broadcasted_iota(jnp.int32, (2 * SUB, BLK), 1)
    units = units.astype(jnp.float32).astype(jnp.bfloat16)
    roll = lambda value, by: pltpu.roll(value, by % BLK, 1)

    @pl.when(step == 0)
    def _():
        if carried:
            u_st[TG:] = u_in[...]
            f_st[...] = f_in[...]
            l_st[...] = l_in[...]
            c_st[TG // SUB] = c_in[...]
        else:
            c_st[...] = jnp.zeros_like(c_st)
            u_st[...] = jnp.zeros_like(u_st)
            f_st[...] = jnp.zeros_like(f_st)
            l_st[...] = jnp.zeros_like(l_st)

    u_st[:SUB] = u_st[TG:]
    c_st[0] = c_st[TG // SUB]
    rows = jnp.concatenate([p0[...], p1[...], p2[...], p3[...]], axis=0)
    edge = jnp.concatenate([q0[...], q1[...], q2[...], q3[...]], axis=0)
    w = w_ref[...]
    both = jnp.dot(w, rows, preferred_element_type=jnp.float32).astype(jnp.bfloat16)
    tail = jnp.dot(w, edge, preferred_element_type=jnp.float32).astype(jnp.bfloat16)
    for k in range(2):
        sec[k, :, :GW] = both[k * 32 : (k + 1) * 32]
        sec[k, :, GW:] = tail[k * 32 : (k + 1) * 32]
    f = jnp.where(tall_lane < HALO + SUB, roll(f_st[...], -TG), 0.0)
    l = jnp.where(tall_lane < HALO + SUB, roll(l_st[...], -TG), 0.0)
    for at in range(0, TG, SUB):
        tiles = range(at, at + SUB)
        ests = []
        for i in tiles:
            kind = kind_ref[s * TG + i]
            taken = sec[kind, :, i * BLK : (i + 2) * BLK]
            ests.append(jnp.dot(taken, t_ref[i], preferred_element_type=jnp.float32))
        sides = []
        for i in tiles:
            cols = slice(i * BLK, (i + 1) * BLK)
            misfit = mask_ref[:, cols].astype(jnp.float32) * (ests[i - at] - bg_ref[:, cols])
            sides.append(jnp.concatenate([*split_hi_lo(misfit), units], axis=0))
        solved = []
        for i in tiles:
            pair = jnp.concatenate(split_hi_lo(inv_ref[i]), axis=0)
            solved.append(
                lax.dot_general(sides[i - at], pair, NT, preferred_element_type=jnp.float32)
            )
        for i in tiles:
            u = solved[i - at]
            tips = u[64:72, :BLK] + u[64:72, BLK:]
            u = u[:32, :BLK] + (u[32:64, :BLK] + u[:32, BLK:])
            u_st[SUB + i] = u
            tile = s * TG + i
            west, east = couple_ref[0, tile] * tips[0:1], couple_ref[1, tile] * tips[1:2]
            both = jnp.where(row == i - at, west, jnp.where(row == SUB + i - at, east, 0.0))
            spot = (i - at) * BLK
            c_st[at // SUB + 1, :, spot : spot + BLK] = both.astype(jnp.bfloat16)
            u = jnp.concatenate([u, tips], axis=0)
            here = tall_lane == HALO + SUB + i
            f = jnp.where(here, u[:, :1], f)
            l = jnp.where(here, u[:, BLK - 1 :], l)
    f_st[...] = f
    l_st[...] = l

    west, east = lanes_ref[0, pl.ds(s, 1), :], lanes_ref[1, pl.ds(s, 1), :]
    af, cf, al, cl = f[32:33] * west, f[33:34] * east, l[32:33] * west, l[33:34] * east
    f0, l0 = f[:32], l[:32]

    def sweep(f, l):
        west, east = roll(l, 1), roll(f, -1)
        return f0 + af * west + cf * east, l0 + al * west + cl * east

    f2, l2 = sweep(*sweep(f0, l0))

    def finish(q):
        low = HALO + q * SUB
        ends = jnp.where(lane < SUB, roll(l2, 1 - low), roll(f2, SUB - 1 - low))
        ends = ends[:, : 2 * SUB].astype(jnp.bfloat16)
        fix = jnp.dot(ends, c_st[q], preferred_element_type=jnp.float32)
        spot = step * (TG // SUB) + q - (0 if carried else 1)
        outs = []
        for i in range(SUB):
            cols = slice(i * BLK, (i + 1) * BLK)
            outs.append((u_st[q * SUB + i] + fix[:, cols]).astype(jnp.bfloat16))
        value = jnp.concatenate(outs, axis=1)
        out_ref[:, pl.ds(pl.multiple_of(spot * SW, SW), SW)] = value
        tips = jnp.dot(yw_ref[...], value, preferred_element_type=jnp.float32)
        tips = tips[0:8] + tips[8:16]
        for k in range(2):
            lines = [tips[k : k + 1, i * BLK : (i + 1) * BLK] for i in range(SUB)]
            place = pl.ds(pl.multiple_of(spot * SUB, SUB), SUB)
            part_ref[k, place, :] = jnp.concatenate(lines, axis=0)

    if carried:
        finish(0)
    else:
        pl.when(step > 0)(lambda: finish(0))
    for q in range(1, TG // SUB):
        finish(q)
    pl.when(s == groups - 1)(lambda: finish(TG // SUB))

    @pl.when(step == pl.num_programs(0) - 1)
    def _():
        u_out[...] = u_st[TG:]
        f_out[...] = f_st[...]
        l_out[...] = l_st[...]
        c_out[...] = c_st[TG // SUB]


def run_rows(first, stop, groups, state, kinds, couple, own, got, w, tables, mask, bg, inv, lanes, yw):
    carried = state is not None
    steps = stop - first
    width = steps * GW - (0 if carried else SW) + (SW if stop == groups else 0)
    near, far, away = got
    full = lambda *shape: pl.BlockSpec(shape, lambda l, *_: (0,) * len(shape))
    wide = lambda off: pl.BlockSpec((32, GW), lambda l, *_: (0, l + off))
    edge = lambda off: pl.BlockSpec((32, BLK), lambda l, *_: (0, (l + off + 1) * TG))
    cube = lambda *shape: pl.BlockSpec((TG, *shape), lambda l, *_: (l + first, 0, 0))
    in_specs = [wide(first), wide(first), wide(0), wide(0)]
    in_specs += [edge(first), edge(first), edge(0), edge(0)]
    in_specs += [
        full(64, BLK),
        cube(2 * BLK, BLK),
        wide(first),
        wide(first),
        cube(BLK, BLK),
        full(*lanes.shape),
        full(16, 32),
    ]
    keep = [
        jax.ShapeDtypeStruct((SUB, 32, BLK), jnp.float32),
        jax.ShapeDtypeStruct((40, BLK), jnp.float32),
        jax.ShapeDtypeStruct((40, BLK), jnp.float32),
        jax.ShapeDtypeStruct((2 * SUB, SW), jnp.bfloat16),
    ]
    operands = [kinds, couple, own, near, far, away, own, near, far, away, w, tables, mask, bg]
    operands += [inv, lanes, yw]
    if carried:
        in_specs += [full(*k.shape) for k in keep]
        operands += list(state)
    grid_spec = pltpu.PrefetchScalarGridSpec(
        num_scalar_prefetch=2,
        grid=(steps,),
        in_specs=in_specs,
        out_specs=[full(32, width), full(2, width // BLK, BLK), *[full(*k.shape) for k in keep]],
        scratch_shapes=[
            pltpu.VMEM((2, 32, GW + BLK), jnp.bfloat16),
            pltpu.VMEM((SUB + TG, 32, BLK), jnp.float32),
            pltpu.VMEM((40, BLK), jnp.float32),
            pltpu.VMEM((40, BLK), jnp.float32),
            pltpu.VMEM((TG // SUB + 1, 2 * SUB, SW), jnp.bfloat16),
        ],
    )
    outs = pl.pallas_call(
        functools.partial(rows_kernel, first, groups, carried),
        grid_spec=grid_spec,
        out_shape=[
            jax.ShapeDtypeStruct((32, width), jnp.bfloat16),
            jax.ShapeDtypeStruct((2, width // BLK, BLK), jnp.float32),
            *keep,
        ],
        compiler_params=pltpu.CompilerParams(vmem_limit_bytes=VMEM_LIMIT),
    )(*operands)
    return outs[0], outs[1], tuple(outs[2:])


def ends_kernel(blocks, block_ref, corner_ref, own, other, below, above, distant, out):
    block = block_ref[0]
    pair = block // 2
    value = lambda ref: ref[...].astype(jnp.float32)
    before = jnp.where(pair > 0, value(below), 0.0)
    after = jnp.where(pair < blocks // 2 - 1, value(above), 0.0)
    inside = jnp.where(lax.rem(block, 2) == 1, pair < blocks // 2 - 2, pair > 1)
    beyond = jnp.where(inside, value(distant), 0.0)
    second = lax.rem(block, 2) == 1
    pick = lambda even, odd: jnp.where(second, odd, even)

    def coef(r, k):
        at = block + k
        return jnp.where((at >= 0) & (at < blocks), corner_ref[jnp.clip(at, 0, blocks - 1), r], 0.0)

    f = {0: own[0], -1: pick(before[1], other[0]), 1: pick(other[0], after[0])}
    l = {0: own[1], -1: pick(before[2], other[1]), 1: pick(other[1], after[1])}
    l[-2], l[-3] = pick(before[0], before[2]), pick(beyond, before[0])
    f[2], f[3] = pick(after[0], after[2]), pick(after[2], beyond)
    last = lambda k, west, east: l[k] + coef(2, k) * west + coef(3, k) * east
    head = lambda k, west, east: f[k] + coef(0, k) * west + coef(1, k) * east
    out[0] = last(-1, last(-2, l[-3], f[-1]), head(0, l[-1], f[1]))
    out[1] = head(1, last(0, l[-1], f[1]), head(2, l[1], f[3]))


def run_ends(blocks, block, corner, own, *others):
    smem = pl.BlockSpec(memory_space=pltpu.SMEM)
    vmem = pl.BlockSpec(memory_space=pltpu.VMEM)
    return pl.pallas_call(
        functools.partial(ends_kernel, blocks),
        in_specs=[smem, smem] + [vmem] * 5,
        out_specs=vmem,
        out_shape=jax.ShapeDtypeStruct(own.shape, own.dtype),
        compiler_params=pltpu.CompilerParams(vmem_limit_bytes=VMEM_LIMIT),
    )(block.reshape(1), corner, own, *others)


def columns_kernel(start, w_ref, ends_ref, n0, n1, *rest):
    out_ref, held, sems = rest[-3:]
    south, north = ends_ref[:, 0:1], ends_ref[:, 1:2]
    copies = []
    at = 0
    for chunk in range(0, (len(rest) - 3) // 4 * 4, 4):
        pieces = rest[chunk : chunk + 4]
        for within in range(0, pieces[0].shape[1], SW):
            rows = jnp.concatenate([e[:, within : within + SW] for e in pieces], axis=0)
            both = jnp.dot(w_ref[...], rows, preferred_element_type=jnp.float32)
            value = both[:32] + both[32:]
            for i in range(SUB):
                line = (start + at) // BLK + i
                row = [n0[k, line : line + 1, :] + n1[k, line : line + 1, :] for k in range(2)]
                here = slice(i * BLK, (i + 1) * BLK)
                held[:, at + i * BLK : at + (i + 1) * BLK] = (
                    value[:, here] + south * row[0] + north * row[1]
                )
            copy = pltpu.make_async_copy(
                held.at[:, at : at + SW],
                out_ref.at[:, start + at : start + at + SW],
                sems.at[at // SW],
            )
            copy.start()
            copies.append(copy)
            at += SW
    for copy in copies:
        copy.wait()


def run_columns(start, total, w, ends, chunks, near, far, so_far):
    width = sum(pieces[0].shape[1] for pieces in chunks)
    vmem = pl.BlockSpec(memory_space=pltpu.VMEM)
    operands = [w, ends, near, far] + [piece for pieces in chunks for piece in pieces]
    in_specs = [vmem] * len(operands)
    aliases = {}
    if so_far is not None:
        aliases = {len(operands): 0}
        operands.append(so_far)
        in_specs.append(pl.BlockSpec(memory_space=pl.ANY))
    return pl.pallas_call(
        functools.partial(columns_kernel, start),
        in_specs=in_specs,
        out_specs=pl.BlockSpec(memory_space=pl.ANY),
        out_shape=jax.ShapeDtypeStruct((32, total), jnp.float32),
        scratch_shapes=[
            pltpu.VMEM((32, width), jnp.float32),
            pltpu.SemaphoreType.DMA((width // SW,)),
        ],
        input_output_aliases=aliases,
        compiler_params=pltpu.CompilerParams(vmem_limit_bytes=VMEM_LIMIT),
    )(*operands)


def body(
    panels,
    void_mask,
    background,
    row_offset,
    row_frac,
    tile_kind,
    tile_shift,
    tile_frac,
    inverse_x,
    couple_x,
    inverse_y,
    couple_y,
):
    rows = row_offset.shape[0]
    width = background.shape[1]
    groups = width // GW
    n_wide = lax.axis_size("wide")
    mine = lax.axis_index("band")
    block = lax.axis_index("wide")
    across = [(d, d ^ 2) for d in range(4)]
    sibling = [(d, d ^ 1) for d in range(4)]
    swap = lambda value, pairs: lax.ppermute(value, "band", pairs)

    bounds = [(SPLITS[i], SPLITS[i + 1]) for i in range(len(SPLITS) - 1)]
    gathered = []
    near = swap(panels, sibling)
    for first, stop in bounds:
        gathered.append(swap(panels[:, first * GW : stop * GW + BLK], across))

    order = ((jnp.arange(4, dtype=jnp.int32) ^ mine)[:, None] * rows + jnp.arange(rows)[None, :]).reshape(-1)
    w = jnp.concatenate(
        [
            row_matrix(row_offset, row_frac, order, linear_terms),
            row_matrix(row_offset, row_frac, order, cubic_terms),
        ],
        axis=0,
    )
    kinds = (tile_kind == 1).astype(jnp.int32)
    tables, w_y, ends_y, yw, corner = run_tables(
        jnp.stack([block, mine]), tile_shift, tap_weights(tile_kind, tile_frac), inverse_y, couple_y.T
    )
    lanes = jnp.pad(couple_x, ((0, 0), (SUB + HALO, TG - SUB - HALO))).reshape(2, groups + 1, TG)
    lanes = jnp.concatenate([lanes[:, :-1], lanes[:, 1:]], axis=2)
    lanes = jnp.pad(lanes, ((0, 0), (0, 0), (0, BLK - 2 * TG)))

    state = None
    sent = []
    parts = []
    early = len(bounds) - LATE
    for (first, stop), far in zip(bounds, gathered):
        if state is not None:
            far, state = lax.optimization_barrier((far, state))
        got = (near, far, swap(far, sibling))
        east_west, part, state = run_rows(
            first, stop, groups, state, kinds, couple_x, panels, got, w, tables,
            void_mask, background, inverse_x, lanes, yw,
        )
        far = swap(east_west, across) if len(sent) < early else None
        sent.append([east_west, swap(east_west, sibling), far])
        parts.append(part)
    together = lax.optimization_barrier
    part = jnp.concatenate(parts, axis=1) if len(parts) > 1 else parts[0]
    for pieces in sent[:early]:
        part, pieces[1], pieces[2] = together((part, pieces[1], pieces[2]))

    every = [(d, k) for d in range(4) for k in range(n_wide)]
    at = lambda d, k: d * n_wide + k
    half = part.astype(jnp.bfloat16)
    fetch = lambda db, dw: lax.ppermute(
        half, ("band", "wide"), [(at(d ^ db, k ^ dw), at(d, k)) for d, k in every]
    ).astype(jnp.float32)
    second = block % 2
    own = part + fetch(2, 0)
    other = fetch(0, 1) + fetch(2, 1)
    for pieces in sent[early:]:
        last, own, other = together((pieces[0], own, other))
        pieces[2] = swap(last, across)
    even = jnp.where(second == 0, own, other).astype(jnp.bfloat16)
    odd = jnp.where(second == 0, other, own).astype(jnp.bfloat16)
    shifted = lambda value, k: lax.ppermute(
        value, "wide", [(i, (i + 2 * k) % n_wide) for i in range(n_wide)]
    )
    before = shifted(jnp.stack([even[1], odd[0], odd[1]]), 1)
    after = shifted(jnp.stack([even[0], even[1], odd[0]]), -1)
    beyond = lax.ppermute(
        jnp.where(second == 0, odd[1], even[0]),
        "wide",
        [(i, j) for i in range(n_wide) for j in [i + 4 * (1 - 2 * (i % 2))] if 0 <= j < n_wide],
    )
    for pieces in sent[early:]:
        before, pieces[1] = together((before, pieces[1]))
    for pieces in sent[:early]:
        pieces.append(swap(pieces[2], sibling))
        before, pieces[3] = together((before, pieces[3]))
    forced = run_ends(n_wide, block, corner, own, other, before, after, beyond)
    for pieces in sent[early:]:
        pieces[2], forced = together((pieces[2], forced))
    rest = swap(forced, sibling)
    for pieces in sent[early:]:
        pieces.append(swap(pieces[2], sibling))

    return run_columns(0, width, w_y, ends_y, sent, forced, rest, None)


def solution(mesh):
    placed = (
        P(("wide", "band"), None),
        P(("wide", "band"), None),
        P(("wide", "band"), None),
        P(("wide", "band")),
        P(("wide", "band")),
        P(),
        P(),
        P(),
        P(),
        P(),
        P(),
        P(),
    )
    return jax.shard_map(
        body, mesh=mesh, in_specs=placed, out_specs=P(("wide", "band"), None), check_vma=False
    )
```

```python
import functools

import jax
import jax.numpy as jnp
from jax import lax
from jax.experimental import pallas as pl
from jax.experimental.pallas import tpu as pltpu
from jax.sharding import PartitionSpec as P

BLK = 128
TG = 32
GW = TG * BLK
SUB = 8
SW = SUB * BLK
HALO = 3
SPLITS = (0, 2, 4)
LATE = 1
VMEM_LIMIT = 32 * 1024 * 1024


def cubic_terms(frac):
    f2 = frac * frac
    f3 = f2 * frac
    return [
        -0.5 * f3 + f2 - 0.5 * frac,
        1.5 * f3 - 2.5 * f2 + 1.0,
        -1.5 * f3 + 2.0 * f2 + 0.5 * frac,
        0.5 * f3 - 0.5 * f2,
    ]


def linear_terms(frac):
    zeros = jnp.zeros_like(frac)
    return [zeros, 1.0 - frac, frac, zeros]


def row_matrix(offsets, fracs, columns, terms):
    total = jnp.zeros((offsets.shape[0], columns.shape[0]), jnp.float32)
    for index, weight in enumerate(terms(fracs)):
        hit = (columns[None, :] == offsets[:, None] + index).astype(jnp.float32)
        total = total + weight[:, None] * hit
    return total.astype(jnp.bfloat16)


def tap_weights(kind, frac):
    taps = [
        jnp.where(kind == 1, wc, wl)
        for wc, wl in zip(cubic_terms(frac), linear_terms(frac))
    ]
    return lax.reduce_precision(jnp.stack(taps), 8, 7)


NT = (((1,), (1,)), ((), ()))


def tables_kernel(here_ref, shift_ref, tap_ref, inv_ref, first_ref, last_ref, couple_ref, *outs):
    t_ref, w_ref, ends_ref, yw_ref, corner_ref = outs
    step = pl.program_id(0)
    block, mine = here_ref[0], here_ref[1]
    shape = (2 * BLK, BLK)
    delta = lax.broadcasted_iota(jnp.int32, shape, 0) - lax.broadcasted_iota(jnp.int32, shape, 1)
    for i in range(TG):
        tile = step * TG + i
        tap = delta - shift_ref[tile]
        total = jnp.zeros(shape, jnp.float32)
        for k in range(4):
            total = jnp.where(tap == k, tap_ref[k, tile], total)
        t_ref[i] = total.astype(jnp.bfloat16)

    @pl.when(step == 0)
    def _():
        lane = lax.broadcasted_iota(jnp.int32, (32, BLK), 1)
        odd, high = lax.rem(mine, 2) == 1, mine > 1
        own = inv_ref[0, pl.ds(pl.multiple_of(mine * 32, 32), 32), :]
        swapped = jnp.where(lax.rem(lane // 32, 2) == 0, pltpu.roll(own, 96, 1), pltpu.roll(own, 32, 1))
        turned = jnp.where(odd, swapped, own)
        turned = jnp.where(high, pltpu.roll(turned, 64, 1), turned)
        w_ref[...] = jnp.concatenate(split_hi_lo(turned), axis=0)
        pair = jnp.where(lane == 0, own[:, :1], own[:, BLK - 1 :])
        couple = couple_ref[pl.ds(block, 1), :]
        ends_ref[...] = pair * jnp.where(lane == 0, couple[:, :1], couple[:, 1:2])
        row = lax.broadcasted_iota(jnp.int32, (8, BLK), 0)
        tips = jnp.where(row == 0, inv_ref[0, 0:1, :], inv_ref[0, BLK - 1 :, :])
        tips = jnp.where(row < 2, tips, 0.0)
        tips = jnp.where(odd, pltpu.roll(tips, 96, 1), tips)
        tips = jnp.where(high, pltpu.roll(tips, 64, 1), tips)
        yw_ref[...] = jnp.concatenate(split_hi_lo(tips), axis=0)[:, :32]
        top, bottom = first_ref[:, 0, :], last_ref[:, 7, :]
        west, east = couple_ref[:, 0:1], couple_ref[:, 1:2]
        values = (top[:, :1] * west, top[:, BLK - 1 :] * east, bottom[:, :1] * west, bottom[:, BLK - 1 :] * east)
        total = jnp.zeros((32, BLK), jnp.float32)
        for k, value in enumerate(values):
            total = jnp.where(lane == k, value, total)
        corner_ref[...] = total


def run_tables(here, shift, taps, inverse_y, couple_y):
    tiles = shift.shape[0]
    full = lambda *shape: pl.BlockSpec(shape, lambda l, *_: (0,) * len(shape))
    return pl.pallas_call(
        tables_kernel,
        grid_spec=pltpu.PrefetchScalarGridSpec(
            num_scalar_prefetch=3,
            grid=(tiles // TG,),
            in_specs=[
                pl.BlockSpec((1, BLK, BLK), lambda l, here, *_: (here[0], 0, 0)),
                pl.BlockSpec((inverse_y.shape[0], 8, BLK), lambda l, *_: (0, 0, 0)),
                pl.BlockSpec((inverse_y.shape[0], 8, BLK), lambda l, *_: (0, BLK // 8 - 1, 0)),
                full(*couple_y.shape),
            ],
            out_specs=[
                pl.BlockSpec((TG, 2 * BLK, BLK), lambda l, *_: (l, 0, 0)),
                full(64, BLK),
                full(32, BLK),
                full(16, 32),
                full(32, BLK),
            ],
        ),
        out_shape=[
            jax.ShapeDtypeStruct((tiles, 2 * BLK, BLK), jnp.bfloat16),
            jax.ShapeDtypeStruct((64, BLK), jnp.bfloat16),
            jax.ShapeDtypeStruct((32, BLK), jnp.float32),
            jax.ShapeDtypeStruct((16, 32), jnp.bfloat16),
            jax.ShapeDtypeStruct((32, BLK), jnp.float32),
        ],
        compiler_params=pltpu.CompilerParams(vmem_limit_bytes=VMEM_LIMIT),
    )(here, shift, taps, inverse_y, inverse_y, inverse_y, couple_y)


def split_hi_lo(value):
    hi = value.astype(jnp.bfloat16)
    lo = (value - hi.astype(jnp.float32)).astype(jnp.bfloat16)
    return hi, lo


def rows_kernel(first, groups, carried, *refs):
    kind_ref, couple_ref, p0, p1, p2, p3, q0, q1, q2, q3, w_ref, t_ref = refs[:12]
    mask_ref, bg_ref, inv_ref, lanes_ref, yw_ref = refs[12:17]
    refs = refs[17:]
    if carried:
        u_in, f_in, l_in, c_in = refs[:4]
        refs = refs[4:]
    out_ref, part_ref, u_out, f_out, l_out, c_out, sec, u_st, f_st, l_st, c_st = refs
    step = pl.program_id(0)
    s = step + first
    tall = (40, BLK)
    tall_lane = lax.broadcasted_iota(jnp.int32, tall, 1)
    lane = lax.broadcasted_iota(jnp.int32, (32, BLK), 1)
    row = lax.broadcasted_iota(jnp.int32, (2 * SUB, BLK), 0)
    units = row * (BLK - 1) == lax.broadcasted_iota(jnp.int32, (2 * SUB, BLK), 1)
    units = units.astype(jnp.float32).astype(jnp.bfloat16)
    roll = lambda value, by: pltpu.roll(value, by % BLK, 1)

    @pl.when(step == 0)
    def _():
        if carried:
            u_st[TG:] = u_in[...]
            f_st[...] = f_in[...]
            l_st[...] = l_in[...]
            c_st[TG // SUB] = c_in[...]
        else:
            c_st[...] = jnp.zeros_like(c_st)
            u_st[...] = jnp.zeros_like(u_st)
            f_st[...] = jnp.zeros_like(f_st)
            l_st[...] = jnp.zeros_like(l_st)

    u_st[:SUB] = u_st[TG:]
    c_st[0] = c_st[TG // SUB]
    rows = jnp.concatenate([p0[...], p1[...], p2[...], p3[...]], axis=0)
    edge = jnp.concatenate([q0[...], q1[...], q2[...], q3[...]], axis=0)
    w = w_ref[...]
    both = jnp.dot(w, rows, preferred_element_type=jnp.float32).astype(jnp.bfloat16)
    tail = jnp.dot(w, edge, preferred_element_type=jnp.float32).astype(jnp.bfloat16)
    for k in range(2):
        sec[k, :, :GW] = both[k * 32 : (k + 1) * 32]
        sec[k, :, GW:] = tail[k * 32 : (k + 1) * 32]
    f = jnp.where(tall_lane < HALO + SUB, roll(f_st[...], -TG), 0.0)
    l = jnp.where(tall_lane < HALO + SUB, roll(l_st[...], -TG), 0.0)
    for at in range(0, TG, SUB):
        tiles = range(at, at + SUB)
        ests = []
        for i in tiles:
            kind = kind_ref[s * TG + i]
            taken = sec[kind, :, i * BLK : (i + 2) * BLK]
            ests.append(jnp.dot(taken, t_ref[i], preferred_element_type=jnp.float32))
        sides = []
        for i in tiles:
            cols = slice(i * BLK, (i + 1) * BLK)
            misfit = mask_ref[:, cols].astype(jnp.float32) * (ests[i - at] - bg_ref[:, cols])
            sides.append(jnp.concatenate([*split_hi_lo(misfit), units], axis=0))
        solved = []
        for i in tiles:
            pair = jnp.concatenate(split_hi_lo(inv_ref[i]), axis=0)
            solved.append(
                lax.dot_general(sides[i - at], pair, NT, preferred_element_type=jnp.float32)
            )
        for i in tiles:
            u = solved[i - at]
            tips = u[64:72, :BLK] + u[64:72, BLK:]
            u = u[:32, :BLK] + (u[32:64, :BLK] + u[:32, BLK:])
            u_st[SUB + i] = u
            tile = s * TG + i
            west, east = couple_ref[0, tile] * tips[0:1], couple_ref[1, tile] * tips[1:2]
            both = jnp.where(row == i - at, west, jnp.where(row == SUB + i - at, east, 0.0))
            spot = (i - at) * BLK
            c_st[at // SUB + 1, :, spot : spot + BLK] = both.astype(jnp.bfloat16)
            u = jnp.concatenate([u, tips], axis=0)
            here = tall_lane == HALO + SUB + i
            f = jnp.where(here, u[:, :1], f)
            l = jnp.where(here, u[:, BLK - 1 :], l)
    f_st[...] = f
    l_st[...] = l

    west, east = lanes_ref[0, pl.ds(s, 1), :], lanes_ref[1, pl.ds(s, 1), :]
    af, cf, al, cl = f[32:33] * west, f[33:34] * east, l[32:33] * west, l[33:34] * east
    f0, l0 = f[:32], l[:32]

    def sweep(f, l):
        west, east = roll(l, 1), roll(f, -1)
        return f0 + af * west + cf * east, l0 + al * west + cl * east

    f2, l2 = sweep(*sweep(f0, l0))

    def finish(q):
        low = HALO + q * SUB
        ends = jnp.where(lane < SUB, roll(l2, 1 - low), roll(f2, SUB - 1 - low))
        ends = ends[:, : 2 * SUB].astype(jnp.bfloat16)
        fix = jnp.dot(ends, c_st[q], preferred_element_type=jnp.float32)
        spot = step * (TG // SUB) + q - (0 if carried else 1)
        outs = []
        for i in range(SUB):
            cols = slice(i * BLK, (i + 1) * BLK)
            outs.append((u_st[q * SUB + i] + fix[:, cols]).astype(jnp.bfloat16))
        value = jnp.concatenate(outs, axis=1)
        out_ref[:, pl.ds(pl.multiple_of(spot * SW, SW), SW)] = value
        tips = jnp.dot(yw_ref[...], value, preferred_element_type=jnp.float32)
        tips = tips[0:8] + tips[8:16]
        for k in range(2):
            lines = [tips[k : k + 1, i * BLK : (i + 1) * BLK] for i in range(SUB)]
            place = pl.ds(pl.multiple_of(spot * SUB, SUB), SUB)
            part_ref[k, place, :] = jnp.concatenate(lines, axis=0)

    if carried:
        finish(0)
    else:
        pl.when(step > 0)(lambda: finish(0))
    for q in range(1, TG // SUB):
        finish(q)
    pl.when(s == groups - 1)(lambda: finish(TG // SUB))

    @pl.when(step == pl.num_programs(0) - 1)
    def _():
        u_out[...] = u_st[TG:]
        f_out[...] = f_st[...]
        l_out[...] = l_st[...]
        c_out[...] = c_st[TG // SUB]


def run_rows(first, stop, groups, state, kinds, couple, own, got, w, tables, mask, bg, inv, lanes, yw):
    carried = state is not None
    steps = stop - first
    width = steps * GW - (0 if carried else SW) + (SW if stop == groups else 0)
    near, far, away = got
    full = lambda *shape: pl.BlockSpec(shape, lambda l, *_: (0,) * len(shape))
    wide = lambda off: pl.BlockSpec((32, GW), lambda l, *_: (0, l + off))
    edge = lambda off: pl.BlockSpec((32, BLK), lambda l, *_: (0, (l + off + 1) * TG))
    cube = lambda *shape: pl.BlockSpec((TG, *shape), lambda l, *_: (l + first, 0, 0))
    in_specs = [wide(first), wide(first), wide(0), wide(0)]
    in_specs += [edge(first), edge(first), edge(0), edge(0)]
    in_specs += [
        full(64, BLK),
        cube(2 * BLK, BLK),
        wide(first),
        wide(first),
        cube(BLK, BLK),
        full(*lanes.shape),
        full(16, 32),
    ]
    keep = [
        jax.ShapeDtypeStruct((SUB, 32, BLK), jnp.float32),
        jax.ShapeDtypeStruct((40, BLK), jnp.float32),
        jax.ShapeDtypeStruct((40, BLK), jnp.float32),
        jax.ShapeDtypeStruct((2 * SUB, SW), jnp.bfloat16),
    ]
    operands = [kinds, couple, own, near, far, away, own, near, far, away, w, tables, mask, bg]
    operands += [inv, lanes, yw]
    if carried:
        in_specs += [full(*k.shape) for k in keep]
        operands += list(state)
    grid_spec = pltpu.PrefetchScalarGridSpec(
        num_scalar_prefetch=2,
        grid=(steps,),
        in_specs=in_specs,
        out_specs=[full(32, width), full(2, width // BLK, BLK), *[full(*k.shape) for k in keep]],
        scratch_shapes=[
            pltpu.VMEM((2, 32, GW + BLK), jnp.bfloat16),
            pltpu.VMEM((SUB + TG, 32, BLK), jnp.float32),
            pltpu.VMEM((40, BLK), jnp.float32),
            pltpu.VMEM((40, BLK), jnp.float32),
            pltpu.VMEM((TG // SUB + 1, 2 * SUB, SW), jnp.bfloat16),
        ],
    )
    outs = pl.pallas_call(
        functools.partial(rows_kernel, first, groups, carried),
        grid_spec=grid_spec,
        out_shape=[
            jax.ShapeDtypeStruct((32, width), jnp.bfloat16),
            jax.ShapeDtypeStruct((2, width // BLK, BLK), jnp.float32),
            *keep,
        ],
        compiler_params=pltpu.CompilerParams(vmem_limit_bytes=VMEM_LIMIT),
    )(*operands)
    return outs[0], outs[1], tuple(outs[2:])


def ends_kernel(blocks, block_ref, corner_ref, own, other, below, above, distant, out):
    block = block_ref[0]
    pair = block // 2
    value = lambda ref: ref[...].astype(jnp.float32)
    before = jnp.where(pair > 0, value(below), 0.0)
    after = jnp.where(pair < blocks // 2 - 1, value(above), 0.0)
    inside = jnp.where(lax.rem(block, 2) == 1, pair < blocks // 2 - 2, pair > 1)
    beyond = jnp.where(inside, value(distant), 0.0)
    second = lax.rem(block, 2) == 1
    pick = lambda even, odd: jnp.where(second, odd, even)

    def coef(r, k):
        at = block + k
        return jnp.where((at >= 0) & (at < blocks), corner_ref[jnp.clip(at, 0, blocks - 1), r], 0.0)

    f = {0: own[0], -1: pick(before[1], other[0]), 1: pick(other[0], after[0])}
    l = {0: own[1], -1: pick(before[2], other[1]), 1: pick(other[1], after[1])}
    l[-2], l[-3] = pick(before[0], before[2]), pick(beyond, before[0])
    f[2], f[3] = pick(after[0], after[2]), pick(after[2], beyond)
    last = lambda k, west, east: l[k] + coef(2, k) * west + coef(3, k) * east
    head = lambda k, west, east: f[k] + coef(0, k) * west + coef(1, k) * east
    out[0] = last(-1, last(-2, l[-3], f[-1]), head(0, l[-1], f[1]))
    out[1] = head(1, last(0, l[-1], f[1]), head(2, l[1], f[3]))


def run_ends(blocks, block, corner, own, *others):
    smem = pl.BlockSpec(memory_space=pltpu.SMEM)
    vmem = pl.BlockSpec(memory_space=pltpu.VMEM)
    return pl.pallas_call(
        functools.partial(ends_kernel, blocks),
        in_specs=[smem, smem] + [vmem] * 5,
        out_specs=vmem,
        out_shape=jax.ShapeDtypeStruct(own.shape, own.dtype),
        compiler_params=pltpu.CompilerParams(vmem_limit_bytes=VMEM_LIMIT),
    )(block.reshape(1), corner, own, *others)


def columns_kernel(start, w_ref, ends_ref, n0, n1, *rest):
    out_ref, held, sems = rest[-3:]
    south, north = ends_ref[:, 0:1], ends_ref[:, 1:2]
    copies = []
    at = 0
    for chunk in range(0, (len(rest) - 3) // 4 * 4, 4):
        pieces = rest[chunk : chunk + 4]
        for within in range(0, pieces[0].shape[1], SW):
            rows = jnp.concatenate([e[:, within : within + SW] for e in pieces], axis=0)
            both = jnp.dot(w_ref[...], rows, preferred_element_type=jnp.float32)
            value = both[:32] + both[32:]
            for i in range(SUB):
                line = (start + at) // BLK + i
                row = [n0[k, line : line + 1, :] + n1[k, line : line + 1, :] for k in range(2)]
                here = slice(i * BLK, (i + 1) * BLK)
                held[:, at + i * BLK : at + (i + 1) * BLK] = (
                    value[:, here] + south * row[0] + north * row[1]
                )
            copy = pltpu.make_async_copy(
                held.at[:, at : at + SW],
                out_ref.at[:, start + at : start + at + SW],
                sems.at[at // SW],
            )
            copy.start()
            copies.append(copy)
            at += SW
    for copy in copies:
        copy.wait()


def run_columns(start, total, w, ends, chunks, near, far, so_far):
    width = sum(pieces[0].shape[1] for pieces in chunks)
    vmem = pl.BlockSpec(memory_space=pltpu.VMEM)
    operands = [w, ends, near, far] + [piece for pieces in chunks for piece in pieces]
    in_specs = [vmem] * len(operands)
    aliases = {}
    if so_far is not None:
        aliases = {len(operands): 0}
        operands.append(so_far)
        in_specs.append(pl.BlockSpec(memory_space=pl.ANY))
    return pl.pallas_call(
        functools.partial(columns_kernel, start),
        in_specs=in_specs,
        out_specs=pl.BlockSpec(memory_space=pl.ANY),
        out_shape=jax.ShapeDtypeStruct((32, total), jnp.float32),
        scratch_shapes=[
            pltpu.VMEM((32, width), jnp.float32),
            pltpu.SemaphoreType.DMA((width // SW,)),
        ],
        input_output_aliases=aliases,
        compiler_params=pltpu.CompilerParams(vmem_limit_bytes=VMEM_LIMIT),
    )(*operands)


def body(
    panels,
    void_mask,
    background,
    row_offset,
    row_frac,
    tile_kind,
    tile_shift,
    tile_frac,
    inverse_x,
    couple_x,
    inverse_y,
    couple_y,
):
    rows = row_offset.shape[0]
    width = background.shape[1]
    groups = width // GW
    n_wide = lax.axis_size("wide")
    mine = lax.axis_index("band")
    block = lax.axis_index("wide")
    across = [(d, d ^ 2) for d in range(4)]
    sibling = [(d, d ^ 1) for d in range(4)]
    swap = lambda value, pairs: lax.ppermute(value, "band", pairs)

    bounds = [(SPLITS[i], SPLITS[i + 1]) for i in range(len(SPLITS) - 1)]
    gathered = []
    near = swap(panels, sibling)
    for first, stop in bounds:
        gathered.append(swap(panels[:, first * GW : stop * GW + BLK], across))

    order = ((jnp.arange(4, dtype=jnp.int32) ^ mine)[:, None] * rows + jnp.arange(rows)[None, :]).reshape(-1)
    w = jnp.concatenate(
        [
            row_matrix(row_offset, row_frac, order, linear_terms),
            row_matrix(row_offset, row_frac, order, cubic_terms),
        ],
        axis=0,
    )
    kinds = (tile_kind == 1).astype(jnp.int32)
    tables, w_y, ends_y, yw, corner = run_tables(
        jnp.stack([block, mine]), tile_shift, tap_weights(tile_kind, tile_frac), inverse_y, couple_y.T
    )
    lanes = jnp.pad(couple_x, ((0, 0), (SUB + HALO, TG - SUB - HALO))).reshape(2, groups + 1, TG)
    lanes = jnp.concatenate([lanes[:, :-1], lanes[:, 1:]], axis=2)
    lanes = jnp.pad(lanes, ((0, 0), (0, 0), (0, BLK - 2 * TG)))

    state = None
    sent = []
    parts = []
    early = len(bounds) - LATE
    for (first, stop), far in zip(bounds, gathered):
        if state is not None:
            far, state, sent[-1][1] = lax.optimization_barrier((far, state, sent[-1][1]))
        got = (near, far, swap(far, sibling))
        east_west, part, state = run_rows(
            first, stop, groups, state, kinds, couple_x, panels, got, w, tables,
            void_mask, background, inverse_x, lanes, yw,
        )
        far = swap(east_west, across) if len(sent) < early else None
        sent.append([east_west, swap(east_west, sibling), far])
        parts.append(part)
    together = lax.optimization_barrier
    part = jnp.concatenate(parts, axis=1) if len(parts) > 1 else parts[0]

    every = [(d, k) for d in range(4) for k in range(n_wide)]
    at = lambda d, k: d * n_wide + k
    half = part.astype(jnp.bfloat16)
    fetch = lambda db, dw: lax.ppermute(
        half, ("band", "wide"), [(at(d ^ db, k ^ dw), at(d, k)) for d, k in every]
    ).astype(jnp.float32)
    second = block % 2
    own = part + fetch(2, 0)
    other = fetch(0, 1) + fetch(2, 1)
    for pieces in sent[:early]:
        own, pieces[2] = together((own, pieces[2]))
        pieces.append(swap(pieces[2], sibling))
    for pieces in sent[early:]:
        last, own, other = together((pieces[0], own, other))
        pieces[2] = swap(last, across)
    even = jnp.where(second == 0, own, other).astype(jnp.bfloat16)
    odd = jnp.where(second == 0, other, own).astype(jnp.bfloat16)
    shifted = lambda value, k: lax.ppermute(
        value, "wide", [(i, (i + 2 * k) % n_wide) for i in range(n_wide)]
    )
    before = shifted(jnp.stack([even[1], odd[0], odd[1]]), 1)
    after = shifted(jnp.stack([even[0], even[1], odd[0]]), -1)
    beyond = lax.ppermute(
        jnp.where(second == 0, odd[1], even[0]),
        "wide",
        [(i, j) for i in range(n_wide) for j in [i + 4 * (1 - 2 * (i % 2))] if 0 <= j < n_wide],
    )
    for pieces in sent[early:]:
        before, pieces[1] = together((before, pieces[1]))
    forced = run_ends(n_wide, block, corner, own, other, before, after, beyond)
    for pieces in sent[early:]:
        pieces[2], forced = together((pieces[2], forced))
    rest = swap(forced, sibling)
    for pieces in sent[early:]:
        pieces.append(swap(pieces[2], sibling))

    return run_columns(0, width, w_y, ends_y, sent, forced, rest, None)


def solution(mesh):
    placed = (
        P(("wide", "band"), None),
        P(("wide", "band"), None),
        P(("wide", "band"), None),
        P(("wide", "band")),
        P(("wide", "band")),
        P(),
        P(),
        P(),
        P(),
        P(),
        P(),
        P(),
    )
    return jax.shard_map(
        body, mesh=mesh, in_specs=placed, out_specs=P(("wide", "band"), None), check_vma=False
    )
```

```python
import functools

import jax
import jax.numpy as jnp
from jax import lax
from jax.experimental import pallas as pl
from jax.experimental.pallas import tpu as pltpu
from jax.sharding import PartitionSpec as P

BLK = 128
TG = 32
GW = TG * BLK
SUB = 8
SW = SUB * BLK
HALO = 3
SPLITS = (0, 2, 4)
LATE = 1
VMEM_LIMIT = 32 * 1024 * 1024


def cubic_terms(frac):
    f2 = frac * frac
    f3 = f2 * frac
    return [
        -0.5 * f3 + f2 - 0.5 * frac,
        1.5 * f3 - 2.5 * f2 + 1.0,
        -1.5 * f3 + 2.0 * f2 + 0.5 * frac,
        0.5 * f3 - 0.5 * f2,
    ]


def linear_terms(frac):
    zeros = jnp.zeros_like(frac)
    return [zeros, 1.0 - frac, frac, zeros]


def row_matrix(offsets, fracs, columns, terms):
    total = jnp.zeros((offsets.shape[0], columns.shape[0]), jnp.float32)
    for index, weight in enumerate(terms(fracs)):
        hit = (columns[None, :] == offsets[:, None] + index).astype(jnp.float32)
        total = total + weight[:, None] * hit
    return total.astype(jnp.bfloat16)


def tap_weights(kind, frac):
    taps = [
        jnp.where(kind == 1, wc, wl)
        for wc, wl in zip(cubic_terms(frac), linear_terms(frac))
    ]
    return lax.reduce_precision(jnp.stack(taps), 8, 7)


NT = (((1,), (1,)), ((), ()))


def tables_kernel(here_ref, shift_ref, tap_ref, inv_ref, first_ref, last_ref, couple_ref, *outs):
    t_ref, w_ref, ends_ref, yw_ref, corner_ref = outs
    step = pl.program_id(0)
    block, mine = here_ref[0], here_ref[1]
    shape = (2 * BLK, BLK)
    delta = lax.broadcasted_iota(jnp.int32, shape, 0) - lax.broadcasted_iota(jnp.int32, shape, 1)
    for i in range(TG):
        tile = step * TG + i
        tap = delta - shift_ref[tile]
        total = jnp.zeros(shape, jnp.float32)
        for k in range(4):
            total = jnp.where(tap == k, tap_ref[k, tile], total)
        t_ref[i] = total.astype(jnp.bfloat16)

    @pl.when(step == 0)
    def _():
        lane = lax.broadcasted_iota(jnp.int32, (32, BLK), 1)
        odd, high = lax.rem(mine, 2) == 1, mine > 1
        own = inv_ref[0, pl.ds(pl.multiple_of(mine * 32, 32), 32), :]
        swapped = jnp.where(lax.rem(lane // 32, 2) == 0, pltpu.roll(own, 96, 1), pltpu.roll(own, 32, 1))
        turned = jnp.where(odd, swapped, own)
        turned = jnp.where(high, pltpu.roll(turned, 64, 1), turned)
        w_ref[...] = jnp.concatenate(split_hi_lo(turned), axis=0)
        pair = jnp.where(lane == 0, own[:, :1], own[:, BLK - 1 :])
        couple = couple_ref[pl.ds(block, 1), :]
        ends_ref[...] = pair * jnp.where(lane == 0, couple[:, :1], couple[:, 1:2])
        row = lax.broadcasted_iota(jnp.int32, (8, BLK), 0)
        tips = jnp.where(row == 0, inv_ref[0, 0:1, :], inv_ref[0, BLK - 1 :, :])
        tips = jnp.where(row < 2, tips, 0.0)
        tips = jnp.where(odd, pltpu.roll(tips, 96, 1), tips)
        tips = jnp.where(high, pltpu.roll(tips, 64, 1), tips)
        yw_ref[...] = jnp.concatenate(split_hi_lo(tips), axis=0)[:, :32]
        top, bottom = first_ref[:, 0, :], last_ref[:, 7, :]
        west, east = couple_ref[:, 0:1], couple_ref[:, 1:2]
        values = (top[:, :1] * west, top[:, BLK - 1 :] * east, bottom[:, :1] * west, bottom[:, BLK - 1 :] * east)
        total = jnp.zeros((32, BLK), jnp.float32)
        for k, value in enumerate(values):
            total = jnp.where(lane == k, value, total)
        corner_ref[...] = total


def cut_kernel(bounds, source, *rest):
    outs, sems = rest[:-1], rest[-1]
    copies = []
    for k, (start, stop) in enumerate(bounds):
        copies.append(pltpu.make_async_copy(source.at[:, start:stop], outs[k], sems.at[k]))
        copies[-1].start()
    for copy in copies:
        copy.wait()


def run_cut(source, bounds):
    anywhere = pl.BlockSpec(memory_space=pl.ANY)
    return pl.pallas_call(
        functools.partial(cut_kernel, bounds),
        in_specs=[pl.BlockSpec(memory_space=pltpu.HBM)],
        out_specs=[anywhere] * len(bounds),
        out_shape=[jax.ShapeDtypeStruct((32, stop - start), source.dtype) for start, stop in bounds],
        scratch_shapes=[pltpu.SemaphoreType.DMA((len(bounds),))],
        compiler_params=pltpu.CompilerParams(vmem_limit_bytes=VMEM_LIMIT),
    )(source)


def run_tables(here, shift, taps, inverse_y, couple_y):
    tiles = shift.shape[0]
    full = lambda *shape: pl.BlockSpec(shape, lambda l, *_: (0,) * len(shape))
    return pl.pallas_call(
        tables_kernel,
        grid_spec=pltpu.PrefetchScalarGridSpec(
            num_scalar_prefetch=3,
            grid=(tiles // TG,),
            in_specs=[
                pl.BlockSpec((1, BLK, BLK), lambda l, here, *_: (here[0], 0, 0)),
                pl.BlockSpec((inverse_y.shape[0], 8, BLK), lambda l, *_: (0, 0, 0)),
                pl.BlockSpec((inverse_y.shape[0], 8, BLK), lambda l, *_: (0, BLK // 8 - 1, 0)),
                full(*couple_y.shape),
            ],
            out_specs=[
                pl.BlockSpec((TG, 2 * BLK, BLK), lambda l, *_: (l, 0, 0)),
                full(64, BLK),
                full(32, BLK),
                full(16, 32),
                full(32, BLK),
            ],
        ),
        out_shape=[
            jax.ShapeDtypeStruct((tiles, 2 * BLK, BLK), jnp.bfloat16),
            jax.ShapeDtypeStruct((64, BLK), jnp.bfloat16),
            jax.ShapeDtypeStruct((32, BLK), jnp.float32),
            jax.ShapeDtypeStruct((16, 32), jnp.bfloat16),
            jax.ShapeDtypeStruct((32, BLK), jnp.float32),
        ],
        compiler_params=pltpu.CompilerParams(vmem_limit_bytes=VMEM_LIMIT),
    )(here, shift, taps, inverse_y, inverse_y, inverse_y, couple_y)


def split_hi_lo(value):
    hi = value.astype(jnp.bfloat16)
    lo = (value - hi.astype(jnp.float32)).astype(jnp.bfloat16)
    return hi, lo


def rows_kernel(first, groups, carried, *refs):
    kind_ref, couple_ref, p0, p1, p2, p3, q0, q1, q2, q3, w_ref, t_ref = refs[:12]
    mask_ref, bg_ref, inv_ref, lanes_ref, yw_ref = refs[12:17]
    refs = refs[17:]
    if carried:
        u_in, f_in, l_in, c_in = refs[:4]
        refs = refs[4:]
    out_ref, part_ref, u_out, f_out, l_out, c_out, sec, u_st, f_st, l_st, c_st = refs
    step = pl.program_id(0)
    s = step + first
    tall = (40, BLK)
    tall_lane = lax.broadcasted_iota(jnp.int32, tall, 1)
    lane = lax.broadcasted_iota(jnp.int32, (32, BLK), 1)
    row = lax.broadcasted_iota(jnp.int32, (2 * SUB, BLK), 0)
    units = row * (BLK - 1) == lax.broadcasted_iota(jnp.int32, (2 * SUB, BLK), 1)
    units = units.astype(jnp.float32).astype(jnp.bfloat16)
    roll = lambda value, by: pltpu.roll(value, by % BLK, 1)

    @pl.when(step == 0)
    def _():
        if carried:
            u_st[TG:] = u_in[...]
            f_st[...] = f_in[...]
            l_st[...] = l_in[...]
            c_st[TG // SUB] = c_in[...]
        else:
            c_st[...] = jnp.zeros_like(c_st)
            u_st[...] = jnp.zeros_like(u_st)
            f_st[...] = jnp.zeros_like(f_st)
            l_st[...] = jnp.zeros_like(l_st)

    u_st[:SUB] = u_st[TG:]
    c_st[0] = c_st[TG // SUB]
    rows = jnp.concatenate([p0[...], p1[...], p2[...], p3[...]], axis=0)
    edge = jnp.concatenate([q0[...], q1[...], q2[...], q3[...]], axis=0)
    w = w_ref[...]
    both = jnp.dot(w, rows, preferred_element_type=jnp.float32).astype(jnp.bfloat16)
    tail = jnp.dot(w, edge, preferred_element_type=jnp.float32).astype(jnp.bfloat16)
    for k in range(2):
        sec[k, :, :GW] = both[k * 32 : (k + 1) * 32]
        sec[k, :, GW:] = tail[k * 32 : (k + 1) * 32]
    f = jnp.where(tall_lane < HALO + SUB, roll(f_st[...], -TG), 0.0)
    l = jnp.where(tall_lane < HALO + SUB, roll(l_st[...], -TG), 0.0)
    for at in range(0, TG, SUB):
        tiles = range(at, at + SUB)
        ests = []
        for i in tiles:
            kind = kind_ref[s * TG + i]
            taken = sec[kind, :, i * BLK : (i + 2) * BLK]
            ests.append(jnp.dot(taken, t_ref[i], preferred_element_type=jnp.float32))
        sides = []
        for i in tiles:
            cols = slice(i * BLK, (i + 1) * BLK)
            misfit = mask_ref[:, cols].astype(jnp.float32) * (ests[i - at] - bg_ref[:, cols])
            sides.append(jnp.concatenate([*split_hi_lo(misfit), units], axis=0))
        solved = []
        for i in tiles:
            pair = jnp.concatenate(split_hi_lo(inv_ref[i]), axis=0)
            solved.append(
                lax.dot_general(sides[i - at], pair, NT, preferred_element_type=jnp.float32)
            )
        for i in tiles:
            u = solved[i - at]
            tips = u[64:72, :BLK] + u[64:72, BLK:]
            u = u[:32, :BLK] + (u[32:64, :BLK] + u[:32, BLK:])
            u_st[SUB + i] = u
            tile = s * TG + i
            west, east = couple_ref[0, tile] * tips[0:1], couple_ref[1, tile] * tips[1:2]
            both = jnp.where(row == i - at, west, jnp.where(row == SUB + i - at, east, 0.0))
            spot = (i - at) * BLK
            c_st[at // SUB + 1, :, spot : spot + BLK] = both.astype(jnp.bfloat16)
            u = jnp.concatenate([u, tips], axis=0)
            here = tall_lane == HALO + SUB + i
            f = jnp.where(here, u[:, :1], f)
            l = jnp.where(here, u[:, BLK - 1 :], l)
    f_st[...] = f
    l_st[...] = l

    west, east = lanes_ref[0, pl.ds(s, 1), :], lanes_ref[1, pl.ds(s, 1), :]
    af, cf, al, cl = f[32:33] * west, f[33:34] * east, l[32:33] * west, l[33:34] * east
    f0, l0 = f[:32], l[:32]

    def sweep(f, l):
        west, east = roll(l, 1), roll(f, -1)
        return f0 + af * west + cf * east, l0 + al * west + cl * east

    f2, l2 = sweep(*sweep(f0, l0))

    def finish(q):
        low = HALO + q * SUB
        ends = jnp.where(lane < SUB, roll(l2, 1 - low), roll(f2, SUB - 1 - low))
        ends = ends[:, : 2 * SUB].astype(jnp.bfloat16)
        fix = jnp.dot(ends, c_st[q], preferred_element_type=jnp.float32)
        spot = step * (TG // SUB) + q - (0 if carried else 1)
        outs = []
        for i in range(SUB):
            cols = slice(i * BLK, (i + 1) * BLK)
            outs.append((u_st[q * SUB + i] + fix[:, cols]).astype(jnp.bfloat16))
        value = jnp.concatenate(outs, axis=1)
        out_ref[:, pl.ds(pl.multiple_of(spot * SW, SW), SW)] = value
        tips = jnp.dot(yw_ref[...], value, preferred_element_type=jnp.float32)
        tips = tips[0:8] + tips[8:16]
        for k in range(2):
            lines = [tips[k : k + 1, i * BLK : (i + 1) * BLK] for i in range(SUB)]
            place = pl.ds(pl.multiple_of(spot * SUB, SUB), SUB)
            part_ref[k, place, :] = jnp.concatenate(lines, axis=0)

    if carried:
        finish(0)
    else:
        pl.when(step > 0)(lambda: finish(0))
    for q in range(1, TG // SUB):
        finish(q)
    pl.when(s == groups - 1)(lambda: finish(TG // SUB))

    @pl.when(step == pl.num_programs(0) - 1)
    def _():
        u_out[...] = u_st[TG:]
        f_out[...] = f_st[...]
        l_out[...] = l_st[...]
        c_out[...] = c_st[TG // SUB]


def run_rows(first, stop, groups, state, kinds, couple, own, got, w, tables, mask, bg, inv, lanes, yw):
    carried = state is not None
    steps = stop - first
    width = steps * GW - (0 if carried else SW) + (SW if stop == groups else 0)
    near, far, away = got
    full = lambda *shape: pl.BlockSpec(shape, lambda l, *_: (0,) * len(shape))
    wide = lambda off: pl.BlockSpec((32, GW), lambda l, *_: (0, l + off))
    edge = lambda off: pl.BlockSpec((32, BLK), lambda l, *_: (0, (l + off + 1) * TG))
    cube = lambda *shape: pl.BlockSpec((TG, *shape), lambda l, *_: (l + first, 0, 0))
    in_specs = [wide(first), wide(first), wide(0), wide(0)]
    in_specs += [edge(first), edge(first), edge(0), edge(0)]
    in_specs += [
        full(64, BLK),
        cube(2 * BLK, BLK),
        wide(first),
        wide(first),
        cube(BLK, BLK),
        full(*lanes.shape),
        full(16, 32),
    ]
    keep = [
        jax.ShapeDtypeStruct((SUB, 32, BLK), jnp.float32),
        jax.ShapeDtypeStruct((40, BLK), jnp.float32),
        jax.ShapeDtypeStruct((40, BLK), jnp.float32),
        jax.ShapeDtypeStruct((2 * SUB, SW), jnp.bfloat16),
    ]
    operands = [kinds, couple, own, near, far, away, own, near, far, away, w, tables, mask, bg]
    operands += [inv, lanes, yw]
    if carried:
        in_specs += [full(*k.shape) for k in keep]
        operands += list(state)
    grid_spec = pltpu.PrefetchScalarGridSpec(
        num_scalar_prefetch=2,
        grid=(steps,),
        in_specs=in_specs,
        out_specs=[full(32, width), full(2, width // BLK, BLK), *[full(*k.shape) for k in keep]],
        scratch_shapes=[
            pltpu.VMEM((2, 32, GW + BLK), jnp.bfloat16),
            pltpu.VMEM((SUB + TG, 32, BLK), jnp.float32),
            pltpu.VMEM((40, BLK), jnp.float32),
            pltpu.VMEM((40, BLK), jnp.float32),
            pltpu.VMEM((TG // SUB + 1, 2 * SUB, SW), jnp.bfloat16),
        ],
    )
    outs = pl.pallas_call(
        functools.partial(rows_kernel, first, groups, carried),
        grid_spec=grid_spec,
        out_shape=[
            jax.ShapeDtypeStruct((32, width), jnp.bfloat16),
            jax.ShapeDtypeStruct((2, width // BLK, BLK), jnp.float32),
            *keep,
        ],
        compiler_params=pltpu.CompilerParams(vmem_limit_bytes=VMEM_LIMIT),
    )(*operands)
    return outs[0], outs[1], tuple(outs[2:])


def ends_kernel(blocks, block_ref, corner_ref, own, other, below, above, distant, out):
    block = block_ref[0]
    pair = block // 2
    value = lambda ref: ref[...].astype(jnp.float32)
    before = jnp.where(pair > 0, value(below), 0.0)
    after = jnp.where(pair < blocks // 2 - 1, value(above), 0.0)
    inside = jnp.where(lax.rem(block, 2) == 1, pair < blocks // 2 - 2, pair > 1)
    beyond = jnp.where(inside, value(distant), 0.0)
    second = lax.rem(block, 2) == 1
    pick = lambda even, odd: jnp.where(second, odd, even)

    def coef(r, k):
        at = block + k
        return jnp.where((at >= 0) & (at < blocks), corner_ref[jnp.clip(at, 0, blocks - 1), r], 0.0)

    f = {0: own[0], -1: pick(before[1], other[0]), 1: pick(other[0], after[0])}
    l = {0: own[1], -1: pick(before[2], other[1]), 1: pick(other[1], after[1])}
    l[-2], l[-3] = pick(before[0], before[2]), pick(beyond, before[0])
    f[2], f[3] = pick(after[0], after[2]), pick(after[2], beyond)
    last = lambda k, west, east: l[k] + coef(2, k) * west + coef(3, k) * east
    head = lambda k, west, east: f[k] + coef(0, k) * west + coef(1, k) * east
    out[0] = last(-1, last(-2, l[-3], f[-1]), head(0, l[-1], f[1]))
    out[1] = head(1, last(0, l[-1], f[1]), head(2, l[1], f[3]))


def run_ends(blocks, block, corner, own, *others):
    smem = pl.BlockSpec(memory_space=pltpu.SMEM)
    vmem = pl.BlockSpec(memory_space=pltpu.VMEM)
    return pl.pallas_call(
        functools.partial(ends_kernel, blocks),
        in_specs=[smem, smem] + [vmem] * 5,
        out_specs=vmem,
        out_shape=jax.ShapeDtypeStruct(own.shape, own.dtype),
        compiler_params=pltpu.CompilerParams(vmem_limit_bytes=VMEM_LIMIT),
    )(block.reshape(1), corner, own, *others)


def columns_kernel(start, w_ref, ends_ref, n0, n1, *rest):
    out_ref, held, sems = rest[-3:]
    south, north = ends_ref[:, 0:1], ends_ref[:, 1:2]
    copies = []
    at = 0
    for chunk in range(0, (len(rest) - 3) // 4 * 4, 4):
        pieces = rest[chunk : chunk + 4]
        for within in range(0, pieces[0].shape[1], SW):
            rows = jnp.concatenate([e[:, within : within + SW] for e in pieces], axis=0)
            both = jnp.dot(w_ref[...], rows, preferred_element_type=jnp.float32)
            value = both[:32] + both[32:]
            for i in range(SUB):
                line = (start + at) // BLK + i
                row = [n0[k, line : line + 1, :] + n1[k, line : line + 1, :] for k in range(2)]
                here = slice(i * BLK, (i + 1) * BLK)
                held[:, at + i * BLK : at + (i + 1) * BLK] = (
                    value[:, here] + south * row[0] + north * row[1]
                )
            copy = pltpu.make_async_copy(
                held.at[:, at : at + SW],
                out_ref.at[:, start + at : start + at + SW],
                sems.at[at // SW],
            )
            copy.start()
            copies.append(copy)
            at += SW
    for copy in copies:
        copy.wait()


def run_columns(start, total, w, ends, chunks, near, far, so_far):
    width = sum(pieces[0].shape[1] for pieces in chunks)
    vmem = pl.BlockSpec(memory_space=pltpu.VMEM)
    operands = [w, ends, near, far] + [piece for pieces in chunks for piece in pieces]
    in_specs = [vmem] * len(operands)
    aliases = {}
    if so_far is not None:
        aliases = {len(operands): 0}
        operands.append(so_far)
        in_specs.append(pl.BlockSpec(memory_space=pl.ANY))
    return pl.pallas_call(
        functools.partial(columns_kernel, start),
        in_specs=in_specs,
        out_specs=pl.BlockSpec(memory_space=pl.ANY),
        out_shape=jax.ShapeDtypeStruct((32, total), jnp.float32),
        scratch_shapes=[
            pltpu.VMEM((32, width), jnp.float32),
            pltpu.SemaphoreType.DMA((width // SW,)),
        ],
        input_output_aliases=aliases,
        compiler_params=pltpu.CompilerParams(vmem_limit_bytes=VMEM_LIMIT),
    )(*operands)


def body(
    panels,
    void_mask,
    background,
    row_offset,
    row_frac,
    tile_kind,
    tile_shift,
    tile_frac,
    inverse_x,
    couple_x,
    inverse_y,
    couple_y,
):
    rows = row_offset.shape[0]
    width = background.shape[1]
    groups = width // GW
    n_wide = lax.axis_size("wide")
    mine = lax.axis_index("band")
    block = lax.axis_index("wide")
    across = [(d, d ^ 2) for d in range(4)]
    sibling = [(d, d ^ 1) for d in range(4)]
    swap = lambda value, pairs: lax.ppermute(value, "band", pairs)

    bounds = [(SPLITS[i], SPLITS[i + 1]) for i in range(len(SPLITS) - 1)]
    gathered = []
    near = swap(panels, sibling)
    for first, stop in bounds:
        (piece,) = run_cut(panels, [(first * GW, stop * GW + BLK)])
        gathered.append(swap(piece, across))

    order = ((jnp.arange(4, dtype=jnp.int32) ^ mine)[:, None] * rows + jnp.arange(rows)[None, :]).reshape(-1)
    w = jnp.concatenate(
        [
            row_matrix(row_offset, row_frac, order, linear_terms),
            row_matrix(row_offset, row_frac, order, cubic_terms),
        ],
        axis=0,
    )
    kinds = (tile_kind == 1).astype(jnp.int32)
    tables, w_y, ends_y, yw, corner = run_tables(
        jnp.stack([block, mine]), tile_shift, tap_weights(tile_kind, tile_frac), inverse_y, couple_y.T
    )
    lanes = jnp.pad(couple_x, ((0, 0), (SUB + HALO, TG - SUB - HALO))).reshape(2, groups + 1, TG)
    lanes = jnp.concatenate([lanes[:, :-1], lanes[:, 1:]], axis=2)
    lanes = jnp.pad(lanes, ((0, 0), (0, 0), (0, BLK - 2 * TG)))

    state = None
    sent = []
    parts = []
    early = len(bounds) - LATE
    for (first, stop), far in zip(bounds, gathered):
        if state is not None:
            far, state = lax.optimization_barrier((far, state))
        got = (near, far, swap(far, sibling))
        east_west, part, state = run_rows(
            first, stop, groups, state, kinds, couple_x, panels, got, w, tables,
            void_mask, background, inverse_x, lanes, yw,
        )
        far = swap(east_west, across) if len(sent) < early else None
        sent.append([east_west, swap(east_west, sibling), far])
        parts.append(part)
    together = lax.optimization_barrier
    part = jnp.concatenate(parts, axis=1) if len(parts) > 1 else parts[0]

    for pieces in sent[:early]:
        part, pieces[1] = together((part, pieces[1]))

    every = [(d, k) for d in range(4) for k in range(n_wide)]
    at = lambda d, k: d * n_wide + k
    half = part.astype(jnp.bfloat16)
    fetch = lambda db, dw: lax.ppermute(
        half, ("band", "wide"), [(at(d ^ db, k ^ dw), at(d, k)) for d, k in every]
    ).astype(jnp.float32)
    second = block % 2
    own = part + fetch(2, 0)
    other = fetch(0, 1) + fetch(2, 1)
    for pieces in sent[:early]:
        own, pieces[2] = together((own, pieces[2]))
        pieces.append(swap(pieces[2], sibling))
    for pieces in sent[early:]:
        last, own, other = together((pieces[0], own, other))
        pieces[2] = swap(last, across)
    even = jnp.where(second == 0, own, other).astype(jnp.bfloat16)
    odd = jnp.where(second == 0, other, own).astype(jnp.bfloat16)
    shifted = lambda value, k: lax.ppermute(
        value, "wide", [(i, (i + 2 * k) % n_wide) for i in range(n_wide)]
    )
    before = shifted(jnp.stack([even[1], odd[0], odd[1]]), 1)
    after = shifted(jnp.stack([even[0], even[1], odd[0]]), -1)
    beyond = lax.ppermute(
        jnp.where(second == 0, odd[1], even[0]),
        "wide",
        [(i, j) for i in range(n_wide) for j in [i + 4 * (1 - 2 * (i % 2))] if 0 <= j < n_wide],
    )
    for pieces in sent[early:]:
        before, pieces[1] = together((before, pieces[1]))
    forced = run_ends(n_wide, block, corner, own, other, before, after, beyond)
    for pieces in sent[early:]:
        pieces[2], forced = together((pieces[2], forced))
    rest = swap(forced, sibling)
    for pieces in sent[early:]:
        pieces.append(swap(pieces[2], sibling))

    return run_columns(0, width, w_y, ends_y, sent, forced, rest, None)


def solution(mesh):
    placed = (
        P(("wide", "band"), None),
        P(("wide", "band"), None),
        P(("wide", "band"), None),
        P(("wide", "band")),
        P(("wide", "band")),
        P(),
        P(),
        P(),
        P(),
        P(),
        P(),
        P(),
    )
    return jax.shard_map(
        body, mesh=mesh, in_specs=placed, out_specs=P(("wide", "band"), None), check_vma=False
    )
```

```python
import functools

import jax
import jax.numpy as jnp
from jax import lax
from jax.experimental import pallas as pl
from jax.experimental.pallas import tpu as pltpu
from jax.sharding import PartitionSpec as P

BLK = 128
TG = 32
GW = TG * BLK
SUB = 8
SW = SUB * BLK
HALO = 3
SPLITS = (0, 2, 4)
LATE = 1
VMEM_LIMIT = 32 * 1024 * 1024


def cubic_terms(frac):
    f2 = frac * frac
    f3 = f2 * frac
    return [
        -0.5 * f3 + f2 - 0.5 * frac,
        1.5 * f3 - 2.5 * f2 + 1.0,
        -1.5 * f3 + 2.0 * f2 + 0.5 * frac,
        0.5 * f3 - 0.5 * f2,
    ]


def linear_terms(frac):
    zeros = jnp.zeros_like(frac)
    return [zeros, 1.0 - frac, frac, zeros]


def row_matrix(offsets, fracs, columns, terms):
    total = jnp.zeros((offsets.shape[0], columns.shape[0]), jnp.float32)
    for index, weight in enumerate(terms(fracs)):
        hit = (columns[None, :] == offsets[:, None] + index).astype(jnp.float32)
        total = total + weight[:, None] * hit
    return total.astype(jnp.bfloat16)


def tap_weights(kind, frac):
    taps = [
        jnp.where(kind == 1, wc, wl)
        for wc, wl in zip(cubic_terms(frac), linear_terms(frac))
    ]
    return lax.reduce_precision(jnp.stack(taps), 8, 7)


NT = (((1,), (1,)), ((), ()))


def tables_kernel(here_ref, shift_ref, tap_ref, inv_ref, first_ref, last_ref, couple_ref, *outs):
    t_ref, w_ref, ends_ref, yw_ref, corner_ref = outs
    step = pl.program_id(0)
    block, mine = here_ref[0], here_ref[1]
    shape = (2 * BLK, BLK)
    delta = lax.broadcasted_iota(jnp.int32, shape, 0) - lax.broadcasted_iota(jnp.int32, shape, 1)
    for i in range(TG):
        tile = step * TG + i
        tap = delta - shift_ref[tile]
        total = jnp.zeros(shape, jnp.float32)
        for k in range(4):
            total = jnp.where(tap == k, tap_ref[k, tile], total)
        t_ref[i] = total.astype(jnp.bfloat16)

    @pl.when(step == 0)
    def _():
        lane = lax.broadcasted_iota(jnp.int32, (32, BLK), 1)
        odd, high = lax.rem(mine, 2) == 1, mine > 1
        own = inv_ref[0, pl.ds(pl.multiple_of(mine * 32, 32), 32), :]
        swapped = jnp.where(lax.rem(lane // 32, 2) == 0, pltpu.roll(own, 96, 1), pltpu.roll(own, 32, 1))
        turned = jnp.where(odd, swapped, own)
        turned = jnp.where(high, pltpu.roll(turned, 64, 1), turned)
        w_ref[...] = jnp.concatenate(split_hi_lo(turned), axis=0)
        pair = jnp.where(lane == 0, own[:, :1], own[:, BLK - 1 :])
        couple = couple_ref[pl.ds(block, 1), :]
        ends_ref[...] = pair * jnp.where(lane == 0, couple[:, :1], couple[:, 1:2])
        row = lax.broadcasted_iota(jnp.int32, (8, BLK), 0)
        tips = jnp.where(row == 0, inv_ref[0, 0:1, :], inv_ref[0, BLK - 1 :, :])
        tips = jnp.where(row < 2, tips, 0.0)
        tips = jnp.where(odd, pltpu.roll(tips, 96, 1), tips)
        tips = jnp.where(high, pltpu.roll(tips, 64, 1), tips)
        yw_ref[...] = jnp.concatenate(split_hi_lo(tips), axis=0)[:, :32]
        top, bottom = first_ref[:, 0, :], last_ref[:, 7, :]
        west, east = couple_ref[:, 0:1], couple_ref[:, 1:2]
        values = (top[:, :1] * west, top[:, BLK - 1 :] * east, bottom[:, :1] * west, bottom[:, BLK - 1 :] * east)
        total = jnp.zeros((32, BLK), jnp.float32)
        for k, value in enumerate(values):
            total = jnp.where(lane == k, value, total)
        corner_ref[...] = total


CUTS = 5


def cut_kernel(start, source, out, sems):
    size = out.shape[1] // CUTS
    copies = []
    for k in range(CUTS):
        at = k * size
        copies.append(
            pltpu.make_async_copy(
                source.at[:, start + at : start + at + size], out.at[:, at : at + size], sems.at[k]
            )
        )
        copies[-1].start()
    for copy in copies:
        copy.wait()


def run_cut(source, start, stop):
    return pl.pallas_call(
        functools.partial(cut_kernel, start),
        in_specs=[pl.BlockSpec(memory_space=pltpu.HBM)],
        out_specs=pl.BlockSpec(memory_space=pltpu.VMEM),
        out_shape=jax.ShapeDtypeStruct((32, stop - start), source.dtype),
        scratch_shapes=[pltpu.SemaphoreType.DMA((CUTS,))],
        compiler_params=pltpu.CompilerParams(vmem_limit_bytes=VMEM_LIMIT),
    )(source)


def run_tables(here, shift, taps, inverse_y, couple_y):
    tiles = shift.shape[0]
    full = lambda *shape: pl.BlockSpec(shape, lambda l, *_: (0,) * len(shape))
    return pl.pallas_call(
        tables_kernel,
        grid_spec=pltpu.PrefetchScalarGridSpec(
            num_scalar_prefetch=3,
            grid=(tiles // TG,),
            in_specs=[
                pl.BlockSpec((1, BLK, BLK), lambda l, here, *_: (here[0], 0, 0)),
                pl.BlockSpec((inverse_y.shape[0], 8, BLK), lambda l, *_: (0, 0, 0)),
                pl.BlockSpec((inverse_y.shape[0], 8, BLK), lambda l, *_: (0, BLK // 8 - 1, 0)),
                full(*couple_y.shape),
            ],
            out_specs=[
                pl.BlockSpec((TG, 2 * BLK, BLK), lambda l, *_: (l, 0, 0)),
                full(64, BLK),
                full(32, BLK),
                full(16, 32),
                full(32, BLK),
            ],
        ),
        out_shape=[
            jax.ShapeDtypeStruct((tiles, 2 * BLK, BLK), jnp.bfloat16),
            jax.ShapeDtypeStruct((64, BLK), jnp.bfloat16),
            jax.ShapeDtypeStruct((32, BLK), jnp.float32),
            jax.ShapeDtypeStruct((16, 32), jnp.bfloat16),
            jax.ShapeDtypeStruct((32, BLK), jnp.float32),
        ],
        compiler_params=pltpu.CompilerParams(vmem_limit_bytes=VMEM_LIMIT),
    )(here, shift, taps, inverse_y, inverse_y, inverse_y, couple_y)


def split_hi_lo(value):
    hi = value.astype(jnp.bfloat16)
    lo = (value - hi.astype(jnp.float32)).astype(jnp.bfloat16)
    return hi, lo


def rows_kernel(first, groups, carried, *refs):
    kind_ref, couple_ref, p0, p1, p2, p3, q0, q1, q2, q3, w_ref, t_ref = refs[:12]
    mask_ref, bg_ref, inv_ref, lanes_ref, yw_ref = refs[12:17]
    refs = refs[17:]
    if carried:
        u_in, f_in, l_in, c_in = refs[:4]
        refs = refs[4:]
    out_ref, part_ref, u_out, f_out, l_out, c_out, sec, u_st, f_st, l_st, c_st = refs
    step = pl.program_id(0)
    s = step + first
    tall = (40, BLK)
    tall_lane = lax.broadcasted_iota(jnp.int32, tall, 1)
    lane = lax.broadcasted_iota(jnp.int32, (32, BLK), 1)
    row = lax.broadcasted_iota(jnp.int32, (2 * SUB, BLK), 0)
    units = row * (BLK - 1) == lax.broadcasted_iota(jnp.int32, (2 * SUB, BLK), 1)
    units = units.astype(jnp.float32).astype(jnp.bfloat16)
    roll = lambda value, by: pltpu.roll(value, by % BLK, 1)

    @pl.when(step == 0)
    def _():
        if carried:
            u_st[TG:] = u_in[...]
            f_st[...] = f_in[...]
            l_st[...] = l_in[...]
            c_st[TG // SUB] = c_in[...]
        else:
            c_st[...] = jnp.zeros_like(c_st)
            u_st[...] = jnp.zeros_like(u_st)
            f_st[...] = jnp.zeros_like(f_st)
            l_st[...] = jnp.zeros_like(l_st)

    u_st[:SUB] = u_st[TG:]
    c_st[0] = c_st[TG // SUB]
    rows = jnp.concatenate([p0[...], p1[...], p2[...], p3[...]], axis=0)
    edge = jnp.concatenate([q0[...], q1[...], q2[...], q3[...]], axis=0)
    w = w_ref[...]
    both = jnp.dot(w, rows, preferred_element_type=jnp.float32).astype(jnp.bfloat16)
    tail = jnp.dot(w, edge, preferred_element_type=jnp.float32).astype(jnp.bfloat16)
    for k in range(2):
        sec[k, :, :GW] = both[k * 32 : (k + 1) * 32]
        sec[k, :, GW:] = tail[k * 32 : (k + 1) * 32]
    f = jnp.where(tall_lane < HALO + SUB, roll(f_st[...], -TG), 0.0)
    l = jnp.where(tall_lane < HALO + SUB, roll(l_st[...], -TG), 0.0)
    for at in range(0, TG, SUB):
        tiles = range(at, at + SUB)
        ests = []
        for i in tiles:
            kind = kind_ref[s * TG + i]
            taken = sec[kind, :, i * BLK : (i + 2) * BLK]
            ests.append(jnp.dot(taken, t_ref[i], preferred_element_type=jnp.float32))
        sides = []
        for i in tiles:
            cols = slice(i * BLK, (i + 1) * BLK)
            misfit = mask_ref[:, cols].astype(jnp.float32) * (ests[i - at] - bg_ref[:, cols])
            sides.append(jnp.concatenate([*split_hi_lo(misfit), units], axis=0))
        solved = []
        for i in tiles:
            pair = jnp.concatenate(split_hi_lo(inv_ref[i]), axis=0)
            solved.append(
                lax.dot_general(sides[i - at], pair, NT, preferred_element_type=jnp.float32)
            )
        for i in tiles:
            u = solved[i - at]
            tips = u[64:72, :BLK] + u[64:72, BLK:]
            u = u[:32, :BLK] + (u[32:64, :BLK] + u[:32, BLK:])
            u_st[SUB + i] = u
            tile = s * TG + i
            west, east = couple_ref[0, tile] * tips[0:1], couple_ref[1, tile] * tips[1:2]
            both = jnp.where(row == i - at, west, jnp.where(row == SUB + i - at, east, 0.0))
            spot = (i - at) * BLK
            c_st[at // SUB + 1, :, spot : spot + BLK] = both.astype(jnp.bfloat16)
            u = jnp.concatenate([u, tips], axis=0)
            here = tall_lane == HALO + SUB + i
            f = jnp.where(here, u[:, :1], f)
            l = jnp.where(here, u[:, BLK - 1 :], l)
    f_st[...] = f
    l_st[...] = l

    west, east = lanes_ref[0, pl.ds(s, 1), :], lanes_ref[1, pl.ds(s, 1), :]
    af, cf, al, cl = f[32:33] * west, f[33:34] * east, l[32:33] * west, l[33:34] * east
    f0, l0 = f[:32], l[:32]

    def sweep(f, l):
        west, east = roll(l, 1), roll(f, -1)
        return f0 + af * west + cf * east, l0 + al * west + cl * east

    f2, l2 = sweep(*sweep(f0, l0))

    def finish(q):
        low = HALO + q * SUB
        ends = jnp.where(lane < SUB, roll(l2, 1 - low), roll(f2, SUB - 1 - low))
        ends = ends[:, : 2 * SUB].astype(jnp.bfloat16)
        fix = jnp.dot(ends, c_st[q], preferred_element_type=jnp.float32)
        spot = step * (TG // SUB) + q - (0 if carried else 1)
        outs = []
        for i in range(SUB):
            cols = slice(i * BLK, (i + 1) * BLK)
            outs.append((u_st[q * SUB + i] + fix[:, cols]).astype(jnp.bfloat16))
        value = jnp.concatenate(outs, axis=1)
        out_ref[:, pl.ds(pl.multiple_of(spot * SW, SW), SW)] = value
        tips = jnp.dot(yw_ref[...], value, preferred_element_type=jnp.float32)
        tips = tips[0:8] + tips[8:16]
        for k in range(2):
            lines = [tips[k : k + 1, i * BLK : (i + 1) * BLK] for i in range(SUB)]
            place = pl.ds(pl.multiple_of(spot * SUB, SUB), SUB)
            part_ref[k, place, :] = jnp.concatenate(lines, axis=0)

    if carried:
        finish(0)
    else:
        pl.when(step > 0)(lambda: finish(0))
    for q in range(1, TG // SUB):
        finish(q)
    pl.when(s == groups - 1)(lambda: finish(TG // SUB))

    @pl.when(step == pl.num_programs(0) - 1)
    def _():
        u_out[...] = u_st[TG:]
        f_out[...] = f_st[...]
        l_out[...] = l_st[...]
        c_out[...] = c_st[TG // SUB]


def run_rows(first, stop, groups, state, kinds, couple, own, got, w, tables, mask, bg, inv, lanes, yw):
    carried = state is not None
    steps = stop - first
    width = steps * GW - (0 if carried else SW) + (SW if stop == groups else 0)
    near, far, away = got
    full = lambda *shape: pl.BlockSpec(shape, lambda l, *_: (0,) * len(shape))
    wide = lambda off: pl.BlockSpec((32, GW), lambda l, *_: (0, l + off))
    edge = lambda off: pl.BlockSpec((32, BLK), lambda l, *_: (0, (l + off + 1) * TG))
    cube = lambda *shape: pl.BlockSpec((TG, *shape), lambda l, *_: (l + first, 0, 0))
    in_specs = [wide(first), wide(first), wide(0), wide(0)]
    in_specs += [edge(first), edge(first), edge(0), edge(0)]
    in_specs += [
        full(64, BLK),
        cube(2 * BLK, BLK),
        wide(first),
        wide(first),
        cube(BLK, BLK),
        full(*lanes.shape),
        full(16, 32),
    ]
    keep = [
        jax.ShapeDtypeStruct((SUB, 32, BLK), jnp.float32),
        jax.ShapeDtypeStruct((40, BLK), jnp.float32),
        jax.ShapeDtypeStruct((40, BLK), jnp.float32),
        jax.ShapeDtypeStruct((2 * SUB, SW), jnp.bfloat16),
    ]
    operands = [kinds, couple, own, near, far, away, own, near, far, away, w, tables, mask, bg]
    operands += [inv, lanes, yw]
    if carried:
        in_specs += [full(*k.shape) for k in keep]
        operands += list(state)
    grid_spec = pltpu.PrefetchScalarGridSpec(
        num_scalar_prefetch=2,
        grid=(steps,),
        in_specs=in_specs,
        out_specs=[full(32, width), full(2, width // BLK, BLK), *[full(*k.shape) for k in keep]],
        scratch_shapes=[
            pltpu.VMEM((2, 32, GW + BLK), jnp.bfloat16),
            pltpu.VMEM((SUB + TG, 32, BLK), jnp.float32),
            pltpu.VMEM((40, BLK), jnp.float32),
            pltpu.VMEM((40, BLK), jnp.float32),
            pltpu.VMEM((TG // SUB + 1, 2 * SUB, SW), jnp.bfloat16),
        ],
    )
    outs = pl.pallas_call(
        functools.partial(rows_kernel, first, groups, carried),
        grid_spec=grid_spec,
        out_shape=[
            jax.ShapeDtypeStruct((32, width), jnp.bfloat16),
            jax.ShapeDtypeStruct((2, width // BLK, BLK), jnp.float32),
            *keep,
        ],
        compiler_params=pltpu.CompilerParams(vmem_limit_bytes=VMEM_LIMIT),
    )(*operands)
    return outs[0], outs[1], tuple(outs[2:])


def ends_kernel(blocks, block_ref, corner_ref, own, other, below, above, distant, out):
    block = block_ref[0]
    pair = block // 2
    value = lambda ref: ref[...].astype(jnp.float32)
    before = jnp.where(pair > 0, value(below), 0.0)
    after = jnp.where(pair < blocks // 2 - 1, value(above), 0.0)
    inside = jnp.where(lax.rem(block, 2) == 1, pair < blocks // 2 - 2, pair > 1)
    beyond = jnp.where(inside, value(distant), 0.0)
    second = lax.rem(block, 2) == 1
    pick = lambda even, odd: jnp.where(second, odd, even)

    def coef(r, k):
        at = block + k
        return jnp.where((at >= 0) & (at < blocks), corner_ref[jnp.clip(at, 0, blocks - 1), r], 0.0)

    f = {0: own[0], -1: pick(before[1], other[0]), 1: pick(other[0], after[0])}
    l = {0: own[1], -1: pick(before[2], other[1]), 1: pick(other[1], after[1])}
    l[-2], l[-3] = pick(before[0], before[2]), pick(beyond, before[0])
    f[2], f[3] = pick(after[0], after[2]), pick(after[2], beyond)
    last = lambda k, west, east: l[k] + coef(2, k) * west + coef(3, k) * east
    head = lambda k, west, east: f[k] + coef(0, k) * west + coef(1, k) * east
    out[0] = last(-1, last(-2, l[-3], f[-1]), head(0, l[-1], f[1]))
    out[1] = head(1, last(0, l[-1], f[1]), head(2, l[1], f[3]))


def run_ends(blocks, block, corner, own, *others):
    smem = pl.BlockSpec(memory_space=pltpu.SMEM)
    vmem = pl.BlockSpec(memory_space=pltpu.VMEM)
    return pl.pallas_call(
        functools.partial(ends_kernel, blocks),
        in_specs=[smem, smem] + [vmem] * 5,
        out_specs=vmem,
        out_shape=jax.ShapeDtypeStruct(own.shape, own.dtype),
        compiler_params=pltpu.CompilerParams(vmem_limit_bytes=VMEM_LIMIT),
    )(block.reshape(1), corner, own, *others)


def columns_kernel(start, w_ref, ends_ref, n0, n1, *rest):
    out_ref, held, sems = rest[-3:]
    south, north = ends_ref[:, 0:1], ends_ref[:, 1:2]
    copies = []
    at = 0
    for chunk in range(0, (len(rest) - 3) // 4 * 4, 4):
        pieces = rest[chunk : chunk + 4]
        for within in range(0, pieces[0].shape[1], SW):
            rows = jnp.concatenate([e[:, within : within + SW] for e in pieces], axis=0)
            both = jnp.dot(w_ref[...], rows, preferred_element_type=jnp.float32)
            value = both[:32] + both[32:]
            for i in range(SUB):
                line = (start + at) // BLK + i
                row = [n0[k, line : line + 1, :] + n1[k, line : line + 1, :] for k in range(2)]
                here = slice(i * BLK, (i + 1) * BLK)
                held[:, at + i * BLK : at + (i + 1) * BLK] = (
                    value[:, here] + south * row[0] + north * row[1]
                )
            copy = pltpu.make_async_copy(
                held.at[:, at : at + SW],
                out_ref.at[:, start + at : start + at + SW],
                sems.at[at // SW],
            )
            copy.start()
            copies.append(copy)
            at += SW
    for copy in copies:
        copy.wait()


def run_columns(start, total, w, ends, chunks, near, far, so_far):
    width = sum(pieces[0].shape[1] for pieces in chunks)
    vmem = pl.BlockSpec(memory_space=pltpu.VMEM)
    operands = [w, ends, near, far] + [piece for pieces in chunks for piece in pieces]
    in_specs = [vmem] * len(operands)
    aliases = {}
    if so_far is not None:
        aliases = {len(operands): 0}
        operands.append(so_far)
        in_specs.append(pl.BlockSpec(memory_space=pl.ANY))
    return pl.pallas_call(
        functools.partial(columns_kernel, start),
        in_specs=in_specs,
        out_specs=pl.BlockSpec(memory_space=pl.ANY),
        out_shape=jax.ShapeDtypeStruct((32, total), jnp.float32),
        scratch_shapes=[
            pltpu.VMEM((32, width), jnp.float32),
            pltpu.SemaphoreType.DMA((width // SW,)),
        ],
        input_output_aliases=aliases,
        compiler_params=pltpu.CompilerParams(vmem_limit_bytes=VMEM_LIMIT),
    )(*operands)


def body(
    panels,
    void_mask,
    background,
    row_offset,
    row_frac,
    tile_kind,
    tile_shift,
    tile_frac,
    inverse_x,
    couple_x,
    inverse_y,
    couple_y,
):
    rows = row_offset.shape[0]
    width = background.shape[1]
    groups = width // GW
    n_wide = lax.axis_size("wide")
    mine = lax.axis_index("band")
    block = lax.axis_index("wide")
    across = [(d, d ^ 2) for d in range(4)]
    sibling = [(d, d ^ 1) for d in range(4)]
    swap = lambda value, pairs: lax.ppermute(value, "band", pairs)

    bounds = [(SPLITS[i], SPLITS[i + 1]) for i in range(len(SPLITS) - 1)]
    gathered = []
    pieces = [run_cut(panels, first * GW, stop * GW + BLK) for first, stop in bounds]
    pieces[0], source = lax.optimization_barrier((pieces[0], panels))
    gathered = [swap(piece, across) for piece in pieces]
    near = swap(source, sibling)

    order = ((jnp.arange(4, dtype=jnp.int32) ^ mine)[:, None] * rows + jnp.arange(rows)[None, :]).reshape(-1)
    w = jnp.concatenate(
        [
            row_matrix(row_offset, row_frac, order, linear_terms),
            row_matrix(row_offset, row_frac, order, cubic_terms),
        ],
        axis=0,
    )
    kinds = (tile_kind == 1).astype(jnp.int32)
    tables, w_y, ends_y, yw, corner = run_tables(
        jnp.stack([block, mine]), tile_shift, tap_weights(tile_kind, tile_frac), inverse_y, couple_y.T
    )
    lanes = jnp.pad(couple_x, ((0, 0), (SUB + HALO, TG - SUB - HALO))).reshape(2, groups + 1, TG)
    lanes = jnp.concatenate([lanes[:, :-1], lanes[:, 1:]], axis=2)
    lanes = jnp.pad(lanes, ((0, 0), (0, 0), (0, BLK - 2 * TG)))

    state = None
    sent = []
    parts = []
    early = len(bounds) - LATE
    for (first, stop), far in zip(bounds, gathered):
        if state is not None:
            far, state = lax.optimization_barrier((far, state))
        got = (near, far, swap(far, sibling))
        east_west, part, state = run_rows(
            first, stop, groups, state, kinds, couple_x, panels, got, w, tables,
            void_mask, background, inverse_x, lanes, yw,
        )
        far = swap(east_west, across) if len(sent) < early else None
        sent.append([east_west, swap(east_west, sibling), far])
        parts.append(part)
    together = lax.optimization_barrier
    part = jnp.concatenate(parts, axis=1) if len(parts) > 1 else parts[0]

    for pieces in sent[:early]:
        part, pieces[1] = together((part, pieces[1]))

    every = [(d, k) for d in range(4) for k in range(n_wide)]
    at = lambda d, k: d * n_wide + k
    half = part.astype(jnp.bfloat16)
    fetch = lambda db, dw: lax.ppermute(
        half, ("band", "wide"), [(at(d ^ db, k ^ dw), at(d, k)) for d, k in every]
    ).astype(jnp.float32)
    second = block % 2
    own = part + fetch(2, 0)
    other = fetch(0, 1) + fetch(2, 1)
    for pieces in sent[:early]:
        own, pieces[2] = together((own, pieces[2]))
        pieces.append(swap(pieces[2], sibling))
    for pieces in sent[early:]:
        last, own, other = together((pieces[0], own, other))
        pieces[2] = swap(last, across)
    even = jnp.where(second == 0, own, other).astype(jnp.bfloat16)
    odd = jnp.where(second == 0, other, own).astype(jnp.bfloat16)
    shifted = lambda value, k: lax.ppermute(
        value, "wide", [(i, (i + 2 * k) % n_wide) for i in range(n_wide)]
    )
    before = shifted(jnp.stack([even[1], odd[0], odd[1]]), 1)
    after = shifted(jnp.stack([even[0], even[1], odd[0]]), -1)
    beyond = lax.ppermute(
        jnp.where(second == 0, odd[1], even[0]),
        "wide",
        [(i, j) for i in range(n_wide) for j in [i + 4 * (1 - 2 * (i % 2))] if 0 <= j < n_wide],
    )
    for pieces in sent[early:]:
        before, pieces[1] = together((before, pieces[1]))
    forced = run_ends(n_wide, block, corner, own, other, before, after, beyond)
    for pieces in sent[early:]:
        pieces[2], forced = together((pieces[2], forced))
    rest = swap(forced, sibling)
    for pieces in sent[early:]:
        pieces.append(swap(pieces[2], sibling))

    return run_columns(0, width, w_y, ends_y, sent, forced, rest, None)


def solution(mesh):
    placed = (
        P(("wide", "band"), None),
        P(("wide", "band"), None),
        P(("wide", "band"), None),
        P(("wide", "band")),
        P(("wide", "band")),
        P(),
        P(),
        P(),
        P(),
        P(),
        P(),
        P(),
    )
    return jax.shard_map(
        body, mesh=mesh, in_specs=placed, out_specs=P(("wide", "band"), None), check_vma=False
    )
```

```python
import functools

import jax
import jax.numpy as jnp
from jax import lax
from jax.experimental import pallas as pl
from jax.experimental.pallas import tpu as pltpu
from jax.sharding import PartitionSpec as P

BLK = 128
TG = 32
GW = TG * BLK
SUB = 8
SW = SUB * BLK
HALO = 3
SPLITS = (0, 2, 4)
LATE = 1
VMEM_LIMIT = 32 * 1024 * 1024


def cubic_terms(frac):
    f2 = frac * frac
    f3 = f2 * frac
    return [
        -0.5 * f3 + f2 - 0.5 * frac,
        1.5 * f3 - 2.5 * f2 + 1.0,
        -1.5 * f3 + 2.0 * f2 + 0.5 * frac,
        0.5 * f3 - 0.5 * f2,
    ]


def linear_terms(frac):
    zeros = jnp.zeros_like(frac)
    return [zeros, 1.0 - frac, frac, zeros]


def row_matrix(offsets, fracs, columns, terms):
    total = jnp.zeros((offsets.shape[0], columns.shape[0]), jnp.float32)
    for index, weight in enumerate(terms(fracs)):
        hit = (columns[None, :] == offsets[:, None] + index).astype(jnp.float32)
        total = total + weight[:, None] * hit
    return total.astype(jnp.bfloat16)


def tap_weights(kind, frac):
    taps = [
        jnp.where(kind == 1, wc, wl)
        for wc, wl in zip(cubic_terms(frac), linear_terms(frac))
    ]
    return lax.reduce_precision(jnp.stack(taps), 8, 7)


NT = (((1,), (1,)), ((), ()))


def tables_kernel(here_ref, shift_ref, tap_ref, inv_ref, first_ref, last_ref, couple_ref, *outs):
    t_ref, w_ref, ends_ref, yw_ref, corner_ref = outs
    step = pl.program_id(0)
    block, mine = here_ref[0], here_ref[1]
    shape = (2 * BLK, BLK)
    delta = lax.broadcasted_iota(jnp.int32, shape, 0) - lax.broadcasted_iota(jnp.int32, shape, 1)
    for i in range(TG):
        tile = step * TG + i
        tap = delta - shift_ref[tile]
        total = jnp.zeros(shape, jnp.float32)
        for k in range(4):
            total = jnp.where(tap == k, tap_ref[k, tile], total)
        t_ref[i] = total.astype(jnp.bfloat16)

    @pl.when(step == 0)
    def _():
        lane = lax.broadcasted_iota(jnp.int32, (32, BLK), 1)
        odd, high = lax.rem(mine, 2) == 1, mine > 1
        own = inv_ref[0, pl.ds(pl.multiple_of(mine * 32, 32), 32), :]
        swapped = jnp.where(lax.rem(lane // 32, 2) == 0, pltpu.roll(own, 96, 1), pltpu.roll(own, 32, 1))
        turned = jnp.where(odd, swapped, own)
        turned = jnp.where(high, pltpu.roll(turned, 64, 1), turned)
        w_ref[...] = jnp.concatenate(split_hi_lo(turned), axis=0)
        pair = jnp.where(lane == 0, own[:, :1], own[:, BLK - 1 :])
        couple = couple_ref[pl.ds(block, 1), :]
        ends_ref[...] = pair * jnp.where(lane == 0, couple[:, :1], couple[:, 1:2])
        row = lax.broadcasted_iota(jnp.int32, (8, BLK), 0)
        tips = jnp.where(row == 0, inv_ref[0, 0:1, :], inv_ref[0, BLK - 1 :, :])
        tips = jnp.where(row < 2, tips, 0.0)
        tips = jnp.where(odd, pltpu.roll(tips, 96, 1), tips)
        tips = jnp.where(high, pltpu.roll(tips, 64, 1), tips)
        yw_ref[...] = jnp.concatenate(split_hi_lo(tips), axis=0)[:, :32]
        top, bottom = first_ref[:, 0, :], last_ref[:, 7, :]
        west, east = couple_ref[:, 0:1], couple_ref[:, 1:2]
        values = (top[:, :1] * west, top[:, BLK - 1 :] * east, bottom[:, :1] * west, bottom[:, BLK - 1 :] * east)
        total = jnp.zeros((32, BLK), jnp.float32)
        for k, value in enumerate(values):
            total = jnp.where(lane == k, value, total)
        corner_ref[...] = total


CUTS = 5


def cut_kernel(start, source, out, held, sems):
    size = out.shape[1] // CUTS
    arrive, leave = [], []
    for k in range(CUTS):
        here = held.at[:, k * size : (k + 1) * size]
        at = start + k * size
        arrive.append(pltpu.make_async_copy(source.at[:, at : at + size], here, sems.at[0, k]))
        leave.append(pltpu.make_async_copy(here, out.at[:, k * size : (k + 1) * size], sems.at[1, k]))
    for copy in arrive:
        copy.start()
    for k in range(CUTS):
        arrive[k].wait()
        leave[k].start()
    for copy in leave:
        copy.wait()


def run_cut(source, start, stop):
    return pl.pallas_call(
        functools.partial(cut_kernel, start),
        in_specs=[pl.BlockSpec(memory_space=pltpu.HBM)],
        out_specs=pl.BlockSpec(memory_space=pl.ANY),
        out_shape=jax.ShapeDtypeStruct((32, stop - start), source.dtype),
        scratch_shapes=[
            pltpu.VMEM((32, stop - start), source.dtype),
            pltpu.SemaphoreType.DMA((2, CUTS)),
        ],
        compiler_params=pltpu.CompilerParams(vmem_limit_bytes=VMEM_LIMIT),
    )(source)


def run_tables(here, shift, taps, inverse_y, couple_y):
    tiles = shift.shape[0]
    full = lambda *shape: pl.BlockSpec(shape, lambda l, *_: (0,) * len(shape))
    return pl.pallas_call(
        tables_kernel,
        grid_spec=pltpu.PrefetchScalarGridSpec(
            num_scalar_prefetch=3,
            grid=(tiles // TG,),
            in_specs=[
                pl.BlockSpec((1, BLK, BLK), lambda l, here, *_: (here[0], 0, 0)),
                pl.BlockSpec((inverse_y.shape[0], 8, BLK), lambda l, *_: (0, 0, 0)),
                pl.BlockSpec((inverse_y.shape[0], 8, BLK), lambda l, *_: (0, BLK // 8 - 1, 0)),
                full(*couple_y.shape),
            ],
            out_specs=[
                pl.BlockSpec((TG, 2 * BLK, BLK), lambda l, *_: (l, 0, 0)),
                full(64, BLK),
                full(32, BLK),
                full(16, 32),
                full(32, BLK),
            ],
        ),
        out_shape=[
            jax.ShapeDtypeStruct((tiles, 2 * BLK, BLK), jnp.bfloat16),
            jax.ShapeDtypeStruct((64, BLK), jnp.bfloat16),
            jax.ShapeDtypeStruct((32, BLK), jnp.float32),
            jax.ShapeDtypeStruct((16, 32), jnp.bfloat16),
            jax.ShapeDtypeStruct((32, BLK), jnp.float32),
        ],
        compiler_params=pltpu.CompilerParams(vmem_limit_bytes=VMEM_LIMIT),
    )(here, shift, taps, inverse_y, inverse_y, inverse_y, couple_y)


def split_hi_lo(value):
    hi = value.astype(jnp.bfloat16)
    lo = (value - hi.astype(jnp.float32)).astype(jnp.bfloat16)
    return hi, lo


def rows_kernel(first, groups, carried, *refs):
    kind_ref, couple_ref, p0, p1, p2, p3, q0, q1, q2, q3, w_ref, t_ref = refs[:12]
    mask_ref, bg_ref, inv_ref, lanes_ref, yw_ref = refs[12:17]
    refs = refs[17:]
    if carried:
        u_in, f_in, l_in, c_in = refs[:4]
        refs = refs[4:]
    out_ref, part_ref, u_out, f_out, l_out, c_out, sec, u_st, f_st, l_st, c_st = refs
    step = pl.program_id(0)
    s = step + first
    tall = (40, BLK)
    tall_lane = lax.broadcasted_iota(jnp.int32, tall, 1)
    lane = lax.broadcasted_iota(jnp.int32, (32, BLK), 1)
    row = lax.broadcasted_iota(jnp.int32, (2 * SUB, BLK), 0)
    units = row * (BLK - 1) == lax.broadcasted_iota(jnp.int32, (2 * SUB, BLK), 1)
    units = units.astype(jnp.float32).astype(jnp.bfloat16)
    roll = lambda value, by: pltpu.roll(value, by % BLK, 1)

    @pl.when(step == 0)
    def _():
        if carried:
            u_st[TG:] = u_in[...]
            f_st[...] = f_in[...]
            l_st[...] = l_in[...]
            c_st[TG // SUB] = c_in[...]
        else:
            c_st[...] = jnp.zeros_like(c_st)
            u_st[...] = jnp.zeros_like(u_st)
            f_st[...] = jnp.zeros_like(f_st)
            l_st[...] = jnp.zeros_like(l_st)

    u_st[:SUB] = u_st[TG:]
    c_st[0] = c_st[TG // SUB]
    rows = jnp.concatenate([p0[...], p1[...], p2[...], p3[...]], axis=0)
    edge = jnp.concatenate([q0[...], q1[...], q2[...], q3[...]], axis=0)
    w = w_ref[...]
    both = jnp.dot(w, rows, preferred_element_type=jnp.float32).astype(jnp.bfloat16)
    tail = jnp.dot(w, edge, preferred_element_type=jnp.float32).astype(jnp.bfloat16)
    for k in range(2):
        sec[k, :, :GW] = both[k * 32 : (k + 1) * 32]
        sec[k, :, GW:] = tail[k * 32 : (k + 1) * 32]
    f = jnp.where(tall_lane < HALO + SUB, roll(f_st[...], -TG), 0.0)
    l = jnp.where(tall_lane < HALO + SUB, roll(l_st[...], -TG), 0.0)
    for at in range(0, TG, SUB):
        tiles = range(at, at + SUB)
        ests = []
        for i in tiles:
            kind = kind_ref[s * TG + i]
            taken = sec[kind, :, i * BLK : (i + 2) * BLK]
            ests.append(jnp.dot(taken, t_ref[i], preferred_element_type=jnp.float32))
        sides = []
        for i in tiles:
            cols = slice(i * BLK, (i + 1) * BLK)
            misfit = mask_ref[:, cols].astype(jnp.float32) * (ests[i - at] - bg_ref[:, cols])
            sides.append(jnp.concatenate([*split_hi_lo(misfit), units], axis=0))
        solved = []
        for i in tiles:
            pair = jnp.concatenate(split_hi_lo(inv_ref[i]), axis=0)
            solved.append(
                lax.dot_general(sides[i - at], pair, NT, preferred_element_type=jnp.float32)
            )
        for i in tiles:
            u = solved[i - at]
            tips = u[64:72, :BLK] + u[64:72, BLK:]
            u = u[:32, :BLK] + (u[32:64, :BLK] + u[:32, BLK:])
            u_st[SUB + i] = u
            tile = s * TG + i
            west, east = couple_ref[0, tile] * tips[0:1], couple_ref[1, tile] * tips[1:2]
            both = jnp.where(row == i - at, west, jnp.where(row == SUB + i - at, east, 0.0))
            spot = (i - at) * BLK
            c_st[at // SUB + 1, :, spot : spot + BLK] = both.astype(jnp.bfloat16)
            u = jnp.concatenate([u, tips], axis=0)
            here = tall_lane == HALO + SUB + i
            f = jnp.where(here, u[:, :1], f)
            l = jnp.where(here, u[:, BLK - 1 :], l)
    f_st[...] = f
    l_st[...] = l

    west, east = lanes_ref[0, pl.ds(s, 1), :], lanes_ref[1, pl.ds(s, 1), :]
    af, cf, al, cl = f[32:33] * west, f[33:34] * east, l[32:33] * west, l[33:34] * east
    f0, l0 = f[:32], l[:32]

    def sweep(f, l):
        west, east = roll(l, 1), roll(f, -1)
        return f0 + af * west + cf * east, l0 + al * west + cl * east

    f2, l2 = sweep(*sweep(f0, l0))

    def finish(q):
        low = HALO + q * SUB
        ends = jnp.where(lane < SUB, roll(l2, 1 - low), roll(f2, SUB - 1 - low))
        ends = ends[:, : 2 * SUB].astype(jnp.bfloat16)
        fix = jnp.dot(ends, c_st[q], preferred_element_type=jnp.float32)
        spot = step * (TG // SUB) + q - (0 if carried else 1)
        outs = []
        for i in range(SUB):
            cols = slice(i * BLK, (i + 1) * BLK)
            outs.append((u_st[q * SUB + i] + fix[:, cols]).astype(jnp.bfloat16))
        value = jnp.concatenate(outs, axis=1)
        out_ref[:, pl.ds(pl.multiple_of(spot * SW, SW), SW)] = value
        tips = jnp.dot(yw_ref[...], value, preferred_element_type=jnp.float32)
        tips = tips[0:8] + tips[8:16]
        for k in range(2):
            lines = [tips[k : k + 1, i * BLK : (i + 1) * BLK] for i in range(SUB)]
            place = pl.ds(pl.multiple_of(spot * SUB, SUB), SUB)
            part_ref[k, place, :] = jnp.concatenate(lines, axis=0)

    if carried:
        finish(0)
    else:
        pl.when(step > 0)(lambda: finish(0))
    for q in range(1, TG // SUB):
        finish(q)
    pl.when(s == groups - 1)(lambda: finish(TG // SUB))

    @pl.when(step == pl.num_programs(0) - 1)
    def _():
        u_out[...] = u_st[TG:]
        f_out[...] = f_st[...]
        l_out[...] = l_st[...]
        c_out[...] = c_st[TG // SUB]


def run_rows(first, stop, groups, state, kinds, couple, own, got, w, tables, mask, bg, inv, lanes, yw):
    carried = state is not None
    steps = stop - first
    width = steps * GW - (0 if carried else SW) + (SW if stop == groups else 0)
    near, far, away = got
    full = lambda *shape: pl.BlockSpec(shape, lambda l, *_: (0,) * len(shape))
    wide = lambda off: pl.BlockSpec((32, GW), lambda l, *_: (0, l + off))
    edge = lambda off: pl.BlockSpec((32, BLK), lambda l, *_: (0, (l + off + 1) * TG))
    cube = lambda *shape: pl.BlockSpec((TG, *shape), lambda l, *_: (l + first, 0, 0))
    in_specs = [wide(first), wide(first), wide(0), wide(0)]
    in_specs += [edge(first), edge(first), edge(0), edge(0)]
    in_specs += [
        full(64, BLK),
        cube(2 * BLK, BLK),
        wide(first),
        wide(first),
        cube(BLK, BLK),
        full(*lanes.shape),
        full(16, 32),
    ]
    keep = [
        jax.ShapeDtypeStruct((SUB, 32, BLK), jnp.float32),
        jax.ShapeDtypeStruct((40, BLK), jnp.float32),
        jax.ShapeDtypeStruct((40, BLK), jnp.float32),
        jax.ShapeDtypeStruct((2 * SUB, SW), jnp.bfloat16),
    ]
    operands = [kinds, couple, own, near, far, away, own, near, far, away, w, tables, mask, bg]
    operands += [inv, lanes, yw]
    if carried:
        in_specs += [full(*k.shape) for k in keep]
        operands += list(state)
    grid_spec = pltpu.PrefetchScalarGridSpec(
        num_scalar_prefetch=2,
        grid=(steps,),
        in_specs=in_specs,
        out_specs=[full(32, width), full(2, width // BLK, BLK), *[full(*k.shape) for k in keep]],
        scratch_shapes=[
            pltpu.VMEM((2, 32, GW + BLK), jnp.bfloat16),
            pltpu.VMEM((SUB + TG, 32, BLK), jnp.float32),
            pltpu.VMEM((40, BLK), jnp.float32),
            pltpu.VMEM((40, BLK), jnp.float32),
            pltpu.VMEM((TG // SUB + 1, 2 * SUB, SW), jnp.bfloat16),
        ],
    )
    outs = pl.pallas_call(
        functools.partial(rows_kernel, first, groups, carried),
        grid_spec=grid_spec,
        out_shape=[
            jax.ShapeDtypeStruct((32, width), jnp.bfloat16),
            jax.ShapeDtypeStruct((2, width // BLK, BLK), jnp.float32),
            *keep,
        ],
        compiler_params=pltpu.CompilerParams(vmem_limit_bytes=VMEM_LIMIT),
    )(*operands)
    return outs[0], outs[1], tuple(outs[2:])


def ends_kernel(blocks, block_ref, corner_ref, own, other, below, above, distant, out):
    block = block_ref[0]
    pair = block // 2
    value = lambda ref: ref[...].astype(jnp.float32)
    before = jnp.where(pair > 0, value(below), 0.0)
    after = jnp.where(pair < blocks // 2 - 1, value(above), 0.0)
    inside = jnp.where(lax.rem(block, 2) == 1, pair < blocks // 2 - 2, pair > 1)
    beyond = jnp.where(inside, value(distant), 0.0)
    second = lax.rem(block, 2) == 1
    pick = lambda even, odd: jnp.where(second, odd, even)

    def coef(r, k):
        at = block + k
        return jnp.where((at >= 0) & (at < blocks), corner_ref[jnp.clip(at, 0, blocks - 1), r], 0.0)

    f = {0: own[0], -1: pick(before[1], other[0]), 1: pick(other[0], after[0])}
    l = {0: own[1], -1: pick(before[2], other[1]), 1: pick(other[1], after[1])}
    l[-2], l[-3] = pick(before[0], before[2]), pick(beyond, before[0])
    f[2], f[3] = pick(after[0], after[2]), pick(after[2], beyond)
    last = lambda k, west, east: l[k] + coef(2, k) * west + coef(3, k) * east
    head = lambda k, west, east: f[k] + coef(0, k) * west + coef(1, k) * east
    out[0] = last(-1, last(-2, l[-3], f[-1]), head(0, l[-1], f[1]))
    out[1] = head(1, last(0, l[-1], f[1]), head(2, l[1], f[3]))


def run_ends(blocks, block, corner, own, *others):
    smem = pl.BlockSpec(memory_space=pltpu.SMEM)
    vmem = pl.BlockSpec(memory_space=pltpu.VMEM)
    return pl.pallas_call(
        functools.partial(ends_kernel, blocks),
        in_specs=[smem, smem] + [vmem] * 5,
        out_specs=vmem,
        out_shape=jax.ShapeDtypeStruct(own.shape, own.dtype),
        compiler_params=pltpu.CompilerParams(vmem_limit_bytes=VMEM_LIMIT),
    )(block.reshape(1), corner, own, *others)


def columns_kernel(start, w_ref, ends_ref, n0, n1, *rest):
    out_ref, held, sems = rest[-3:]
    south, north = ends_ref[:, 0:1], ends_ref[:, 1:2]
    copies = []
    at = 0
    for chunk in range(0, (len(rest) - 3) // 4 * 4, 4):
        pieces = rest[chunk : chunk + 4]
        for within in range(0, pieces[0].shape[1], SW):
            rows = jnp.concatenate([e[:, within : within + SW] for e in pieces], axis=0)
            both = jnp.dot(w_ref[...], rows, preferred_element_type=jnp.float32)
            value = both[:32] + both[32:]
            for i in range(SUB):
                line = (start + at) // BLK + i
                row = [n0[k, line : line + 1, :] + n1[k, line : line + 1, :] for k in range(2)]
                here = slice(i * BLK, (i + 1) * BLK)
                held[:, at + i * BLK : at + (i + 1) * BLK] = (
                    value[:, here] + south * row[0] + north * row[1]
                )
            copy = pltpu.make_async_copy(
                held.at[:, at : at + SW],
                out_ref.at[:, start + at : start + at + SW],
                sems.at[at // SW],
            )
            copy.start()
            copies.append(copy)
            at += SW
    for copy in copies:
        copy.wait()


def run_columns(start, total, w, ends, chunks, near, far, so_far):
    width = sum(pieces[0].shape[1] for pieces in chunks)
    vmem = pl.BlockSpec(memory_space=pltpu.VMEM)
    operands = [w, ends, near, far] + [piece for pieces in chunks for piece in pieces]
    in_specs = [vmem] * len(operands)
    aliases = {}
    if so_far is not None:
        aliases = {len(operands): 0}
        operands.append(so_far)
        in_specs.append(pl.BlockSpec(memory_space=pl.ANY))
    return pl.pallas_call(
        functools.partial(columns_kernel, start),
        in_specs=in_specs,
        out_specs=pl.BlockSpec(memory_space=pl.ANY),
        out_shape=jax.ShapeDtypeStruct((32, total), jnp.float32),
        scratch_shapes=[
            pltpu.VMEM((32, width), jnp.float32),
            pltpu.SemaphoreType.DMA((width // SW,)),
        ],
        input_output_aliases=aliases,
        compiler_params=pltpu.CompilerParams(vmem_limit_bytes=VMEM_LIMIT),
    )(*operands)


def body(
    panels,
    void_mask,
    background,
    row_offset,
    row_frac,
    tile_kind,
    tile_shift,
    tile_frac,
    inverse_x,
    couple_x,
    inverse_y,
    couple_y,
):
    rows = row_offset.shape[0]
    width = background.shape[1]
    groups = width // GW
    n_wide = lax.axis_size("wide")
    mine = lax.axis_index("band")
    block = lax.axis_index("wide")
    across = [(d, d ^ 2) for d in range(4)]
    sibling = [(d, d ^ 1) for d in range(4)]
    swap = lambda value, pairs: lax.ppermute(value, "band", pairs)

    bounds = [(SPLITS[i], SPLITS[i + 1]) for i in range(len(SPLITS) - 1)]
    gathered = []
    pieces = [run_cut(panels, first * GW, stop * GW + BLK) for first, stop in bounds]
    pieces[0], source = lax.optimization_barrier((pieces[0], panels))
    gathered = [swap(piece, across) for piece in pieces]
    near = swap(source, sibling)

    order = ((jnp.arange(4, dtype=jnp.int32) ^ mine)[:, None] * rows + jnp.arange(rows)[None, :]).reshape(-1)
    w = jnp.concatenate(
        [
            row_matrix(row_offset, row_frac, order, linear_terms),
            row_matrix(row_offset, row_frac, order, cubic_terms),
        ],
        axis=0,
    )
    kinds = (tile_kind == 1).astype(jnp.int32)
    tables, w_y, ends_y, yw, corner = run_tables(
        jnp.stack([block, mine]), tile_shift, tap_weights(tile_kind, tile_frac), inverse_y, couple_y.T
    )
    lanes = jnp.pad(couple_x, ((0, 0), (SUB + HALO, TG - SUB - HALO))).reshape(2, groups + 1, TG)
    lanes = jnp.concatenate([lanes[:, :-1], lanes[:, 1:]], axis=2)
    lanes = jnp.pad(lanes, ((0, 0), (0, 0), (0, BLK - 2 * TG)))

    state = None
    sent = []
    parts = []
    early = len(bounds) - LATE
    for (first, stop), far in zip(bounds, gathered):
        if state is not None:
            far, state = lax.optimization_barrier((far, state))
        got = (near, far, swap(far, sibling))
        east_west, part, state = run_rows(
            first, stop, groups, state, kinds, couple_x, panels, got, w, tables,
            void_mask, background, inverse_x, lanes, yw,
        )
        far = swap(east_west, across) if len(sent) < early else None
        sent.append([east_west, swap(east_west, sibling), far])
        parts.append(part)
    together = lax.optimization_barrier
    part = jnp.concatenate(parts, axis=1) if len(parts) > 1 else parts[0]

    for pieces in sent[:early]:
        part, pieces[1] = together((part, pieces[1]))

    every = [(d, k) for d in range(4) for k in range(n_wide)]
    at = lambda d, k: d * n_wide + k
    half = part.astype(jnp.bfloat16)
    fetch = lambda db, dw: lax.ppermute(
        half, ("band", "wide"), [(at(d ^ db, k ^ dw), at(d, k)) for d, k in every]
    ).astype(jnp.float32)
    second = block % 2
    own = part + fetch(2, 0)
    other = fetch(0, 1) + fetch(2, 1)
    for pieces in sent[:early]:
        own, pieces[2] = together((own, pieces[2]))
        pieces.append(swap(pieces[2], sibling))
    for pieces in sent[early:]:
        last, own, other = together((pieces[0], own, other))
        pieces[2] = swap(last, across)
    even = jnp.where(second == 0, own, other).astype(jnp.bfloat16)
    odd = jnp.where(second == 0, other, own).astype(jnp.bfloat16)
    shifted = lambda value, k: lax.ppermute(
        value, "wide", [(i, (i + 2 * k) % n_wide) for i in range(n_wide)]
    )
    before = shifted(jnp.stack([even[1], odd[0], odd[1]]), 1)
    after = shifted(jnp.stack([even[0], even[1], odd[0]]), -1)
    beyond = lax.ppermute(
        jnp.where(second == 0, odd[1], even[0]),
        "wide",
        [(i, j) for i in range(n_wide) for j in [i + 4 * (1 - 2 * (i % 2))] if 0 <= j < n_wide],
    )
    for pieces in sent[early:]:
        before, pieces[1] = together((before, pieces[1]))
    forced = run_ends(n_wide, block, corner, own, other, before, after, beyond)
    for pieces in sent[early:]:
        pieces[2], forced = together((pieces[2], forced))
    rest = swap(forced, sibling)
    for pieces in sent[early:]:
        pieces.append(swap(pieces[2], sibling))

    return run_columns(0, width, w_y, ends_y, sent, forced, rest, None)


def solution(mesh):
    placed = (
        P(("wide", "band"), None),
        P(("wide", "band"), None),
        P(("wide", "band"), None),
        P(("wide", "band")),
        P(("wide", "band")),
        P(),
        P(),
        P(),
        P(),
        P(),
        P(),
        P(),
    )
    return jax.shard_map(
        body, mesh=mesh, in_specs=placed, out_specs=P(("wide", "band"), None), check_vma=False
    )
```
